32 devices in a mesh: dp: 8 (over y, x, core), mp: 4 (over z).
Axes of the slice: x: 2, y: 2, z: 4, core: 2. Of those that a mesh axis runs over, the one named last changes fastest.
Arguments:
- tokens: bfloat16 [32, 1024, 768], P(('dp', 'mp')), may hold values from -6 to 6
- prompt: float32 [76800], P(('dp', 'mp')), may hold values from -6 to 6
- moment_one: float32 [76800], P(('dp', 'mp')), may hold values from -6 to 6
- moment_two: float32 [76800], P(('dp', 'mp')), may hold values from 0.5 to 20
- segments: int32 [32, 1024], P(('dp', 'mp')), may hold values from 0 to 10, as said below
- live: int32 [32, 1024], P(('dp', 'mp')), may hold values from 0 to 1, as said below
- out_grad: bfloat16 [32, 1024, 768], P(('dp', 'mp')), may hold values from -6 to 6
- w_query: bfloat16 [768, 768], P('dp', 'mp'), may hold values from -0.02734375 to 0.02734375
- w_key: bfloat16 [768, 768], P('dp', 'mp'), may hold values from -0.21875 to 0.21875
- w_value: bfloat16 [768, 768], P('dp', 'mp'), may hold values from -0.21875 to 0.21875
- w_output: bfloat16 [768, 768], P('mp', 'dp'), may hold values from -1.25 to 1.25
- w_inner: bfloat16 [768, 3072], P('dp', 'mp'), may hold values from -0.21875 to 0.21875
- w_outer: bfloat16 [3072, 768], P('mp', 'dp'), may hold values from -0.109375 to 0.109375
- gain_attn: bfloat16 [768], P('dp'), may hold values from 0.5 to 1.5
- gain_ffn: bfloat16 [768], P('dp'), may hold values from 0.5 to 1.5
- rel_table: bfloat16 [32, 12], P(None, 'mp'), may hold values from -4 to 4
Outputs:
- layer_output: bfloat16 [32, 1024, 768], P(('dp', 'mp'))
- input_grad: float32 [32, 1024, 768], P(('dp', 'mp'))
- prompt_new: float32 [76800], P(('dp', 'mp'))
- first_new: float32 [76800], P(('dp', 'mp'))
- second_new: float32 [76800], P(('dp', 'mp'))
The draws below stay inside these ranges and needn't reach their ends.
Inputs may be any that keep to these rules, and one draw needn't show every extreme that they name: `segments`: in each row the numbers start at 0 and never fall. Each sequence holds 100 prompt slots followed by 1 to 512 input slots, and some sequence of every draw has exactly 512. The slots after a row's last sequence carry the next number. Some row of every draw reaches the largest number. `live`: 1 exactly on the slots of a row's sequences, which fill a prefix of the row.
All inputs are finite; a program needn't handle non-finite values.
Results may differ from the reference program's by a relative error of at most 0.01.
Values may be sent and summed in bfloat16 or wider, within the bound.
A program may use at most 384 MiB of HBM per device.

```python
import math
import jax
import jax.numpy as jnp
from jax import lax

D = 768
HEADS = 12
HEAD_DIM = 64
FF = 3072
BUCKETS = 32
PROMPT = 100
SLOTS = 1024
MAXLEN = 512
ADAM_STEP = 10
ROWS = 32


def packing(key):
    key = jax.random.fold_in(key, 11)
    candidates = SLOTS // (PROMPT + 1)
    key_class, key_short, key_long = jax.random.split(key, 3)
    length_class = jax.random.randint(key_class, (ROWS, candidates), 0, 16)
    short_inputs = jax.random.randint(key_short, (ROWS, candidates), 1, MAXLEN // 4 + 1)
    long_inputs = jax.random.randint(key_long, (ROWS, candidates), MAXLEN // 4, MAXLEN + 1)
    inputs = jnp.where(length_class < 13, short_inputs, jnp.where(length_class < 15, long_inputs, MAXLEN))
    inputs = inputs.at[0, 0].set(MAXLEN)
    inputs = inputs.at[ROWS - 1].set(1)
    ends = jnp.cumsum(inputs + PROMPT, axis=1)
    kept = ends <= SLOTS
    used = jnp.max(jnp.where(kept, ends, 0), axis=1)
    places = jnp.arange(SLOTS)
    numbers = jnp.sum((ends[:, None, :] <= places[None, :, None]) & kept[:, None, :], axis=2)
    alive = places[None, :] < used[:, None]
    return (numbers.astype(jnp.int32), alive.astype(jnp.int32))


def draw_segments(key, part):
    numbers, alive = packing(key)
    return numbers


def draw_live(key, part):
    numbers, alive = packing(key)
    return alive


def level_of(own_key, shape, shards, smallest, top_value):
    def one(axis_at, parts):
        draws = jax.random.uniform(jax.random.fold_in(jax.random.fold_in(own_key, 6), axis_at), (parts,), jnp.float32, smallest / len(shards), top_value / len(shards))
        return jnp.repeat(jnp.exp(draws), shape[axis_at] // parts).reshape((-1,) + (1,) * (len(shape) - axis_at - 1))

    level = one(*shards[0])
    for cut in shards[1:]:
        level = level * one(*cut)
    return level


def gaussian(key, shape, width, most, shards=(), kind=jnp.bfloat16):
    values = width * jax.random.normal(key, shape, jnp.float32)
    if shards:
        values = values * level_of(key, shape, shards, -0.22, 0.18)
    return jnp.clip(values, -most, most).astype(kind)


def setup_inputs(seed: int = 0) -> dict:
    keys = jax.random.split(jax.random.key(seed), 17)
    return {
        "tokens": gaussian(keys[0], (ROWS, SLOTS, D), 1.0, 6.0, ((0, 32),)),
        "prompt": gaussian(keys[1], (PROMPT * D,), 1.0, 6.0, ((0, 32),), jnp.float32),
        "moment_one": gaussian(keys[2], (PROMPT * D,), 1.0, 6.0, ((0, 32),), jnp.float32),
        "moment_two": jnp.clip(jnp.exp(math.log(20.0) - 3.6888795 * jax.random.uniform(keys[3], (PROMPT * D,), jnp.float32) ** level_of(keys[3], (PROMPT * D,), ((0, 32),), -0.2, 0.2)), 0.5, 20.0),
        "segments": draw_segments(jax.random.fold_in(keys[16], 71), 0),
        "live": draw_live(jax.random.fold_in(keys[16], 71), 0),
        "out_grad": gaussian(keys[6], (ROWS, SLOTS, D), 1.0, 6.0, ((0, 32),)),
        "w_query": gaussian(keys[7], (D, HEADS * HEAD_DIM), (D * HEAD_DIM) ** -0.5, 0.02734375, ((0, 8), (1, 4))),
        "w_key": gaussian(keys[8], (D, HEADS * HEAD_DIM), D ** -0.5, 0.21875, ((0, 8), (1, 4))),
        "w_value": gaussian(keys[9], (D, HEADS * HEAD_DIM), D ** -0.5, 0.21875, ((0, 8), (1, 4))),
        "w_output": gaussian(keys[10], (HEADS * HEAD_DIM, D), (HEADS * HEAD_DIM // 32) ** -0.5, 1.25, ((0, 4), (1, 8))),
        "w_inner": gaussian(keys[11], (D, FF), D ** -0.5, 0.21875, ((0, 8), (1, 4))),
        "w_outer": gaussian(keys[12], (FF, D), FF ** -0.5, 0.109375, ((0, 4), (1, 8))),
        "gain_attn": jnp.clip(1.0 + 0.1 * jax.random.normal(keys[13], (D,), jnp.float32), 0.5, 1.5).astype(jnp.bfloat16),
        "gain_ffn": jnp.clip(1.0 + 0.1 * jax.random.normal(keys[14], (D,), jnp.float32), 0.5, 1.5).astype(jnp.bfloat16),
        "rel_table": gaussian(keys[15], (BUCKETS, HEADS), 1.0, 4.0, ((1, 4),)),
    }


BOUNDS = (1, 2, 3, 4, 5, 6, 7, 8, 12, 16, 23, 32, 46, 64, 91)
EPSILON = 1e-06
MASKED = -1e+30
HIGHEST = lax.Precision.HIGHEST

@jax.custom_vjp
def low(v):
    return lax.optimization_barrier(v.astype(jnp.bfloat16)).astype(jnp.float32)

@jax.custom_vjp
def low_back(v):
    return v

def low_keep(v):
    return (low(v), None)

def low_pass(kept, grad):
    return (grad,)

def back_keep(v):
    return (v, None)

def back_low(kept, grad):
    return (low(grad),)
low.defvjp(low_keep, low_pass)
low_back.defvjp(back_keep, back_low)

def bucket_of(offset, half):
    distance = jnp.abs(offset)
    counted = sum(((distance >= limit).astype(jnp.int32) for limit in BOUNDS))
    return counted + jnp.where(offset > 0, half, 0).astype(jnp.int32)

def slot_info(segments, live):
    last_axis = segments.ndim - 1
    places = jnp.broadcast_to(jnp.arange(segments.shape[-1], dtype=jnp.int32), segments.shape)
    leading = jnp.ones(segments.shape[:-1] + (1,), dtype=jnp.bool_)
    change = jnp.concatenate([leading, segments[..., 1:] != segments[..., :-1]], axis=last_axis)
    first_slot = lax.cummax(jnp.where(change, places, 0).astype(jnp.int32), axis=last_axis)
    position = (places - first_slot).astype(jnp.int32)
    is_prompt = (live == 1) & (position < PROMPT)
    return (position, is_prompt)

def rms_scale(values, gain):
    return values * lax.rsqrt(lax.optimization_barrier(jnp.mean(values * values, axis=-1, keepdims=True)) + EPSILON) * gain

def reference(tokens, prompt, moment_one, moment_two, segments, live, out_grad, w_query, w_key, w_value, w_output, w_inner, w_outer, gain_attn, gain_ffn, rel_table):
    frozen = tuple((item.astype(jnp.float32) for item in (w_query, w_key, w_value, w_output, w_inner, w_outer, gain_attn, gain_ffn, rel_table)))
    query_w, key_w, value_w, output_w, inner_w, outer_w, attn_gain, ffn_gain, table = frozen
    places = jnp.arange(SLOTS, dtype=jnp.int32)
    bucket = bucket_of(places[None, :] - places[:, None], BUCKETS // 2)
    bias = jnp.transpose(table[bucket], (2, 0, 1))
    prompt_rows = prompt.reshape(PROMPT, D)
    prompt_ids = jnp.arange(PROMPT, dtype=jnp.int32)

    def one_row(total, row_data):
        token_row, segment_row, live_row, cotangent = row_data
        position, is_prompt = slot_info(segment_row, live_row)
        one_hot = ((position[:, None] == prompt_ids[None, :]) & is_prompt[:, None]).astype(jnp.float32)
        mask = (segment_row[:, None] == segment_row[None, :]) & (live_row[None, :] == 1)
        alive = live_row.astype(jnp.float32)[:, None]

        def forward(prompt_in, token_in):
            placed = jnp.dot(one_hot, low(prompt_in), precision=HIGHEST)
            layer_input = jnp.where(is_prompt[:, None], placed, token_in)
            normed = low(rms_scale(layer_input, attn_gain))
            query = low_back(low(jnp.dot(normed, query_w, precision=HIGHEST))).reshape(SLOTS, HEADS, HEAD_DIM)
            keyed = low_back(low(jnp.dot(normed, key_w, precision=HIGHEST))).reshape(SLOTS, HEADS, HEAD_DIM)
            valued = low_back(low(jnp.dot(normed, value_w, precision=HIGHEST))).reshape(SLOTS, HEADS, HEAD_DIM)
            raw = low_back(jnp.einsum('qhd,khd->hqk', query, keyed, precision=HIGHEST))
            scores = jnp.where(mask[None], raw + bias, MASKED)
            top = lax.optimization_barrier(jnp.max(scores, axis=-1, keepdims=True))
            expo = jnp.exp(scores - top)
            probs = low(expo / lax.optimization_barrier(jnp.sum(expo, axis=-1, keepdims=True)))
            context = jnp.einsum('hqk,khd->qhd', probs, valued, precision=HIGHEST).reshape(SLOTS, HEADS * HEAD_DIM)
            context = low_back(low(context))
            hidden = layer_input + low_back(jnp.dot(context, output_w, precision=HIGHEST))
            normed_ffn = low(rms_scale(hidden, ffn_gain))
            inner = low_back(jnp.dot(normed_ffn, inner_w, precision=HIGHEST))
            activated = low(jax.nn.gelu(inner, approximate=True))
            branch = low_back(jnp.dot(activated, outer_w, precision=HIGHEST))
            return alive * (hidden + branch)
        result, pullback = jax.vjp(forward, prompt_rows, token_row.astype(jnp.float32))
        grad_prompt, grad_tokens = pullback(cotangent.astype(jnp.float32))
        return (total + grad_prompt, (result.astype(jnp.bfloat16), grad_tokens))
    summed, outputs = lax.scan(one_row, jnp.zeros((PROMPT, D), jnp.float32), (tokens, segments, live, out_grad))
    layer_output, input_grad = outputs
    grad_flat = summed.reshape(-1)
    first_new = 0.9 * moment_one + 0.1 * grad_flat
    second_new = 0.999 * moment_two + 0.001 * grad_flat * grad_flat
    correct_one = 1.0 - 0.9 ** ADAM_STEP
    correct_two = 1.0 - 0.999 ** ADAM_STEP
    prompt_new = prompt - 0.3 * (first_new / correct_one) / (jnp.sqrt(second_new / correct_two) + 1e-08)
    return (layer_output, input_grad, prompt_new, first_new, second_new)
```

```python
import functools

import jax
import jax.numpy as jnp
from jax import lax
from jax.experimental import pallas as pl
from jax.experimental.pallas import tpu as pltpu
from jax.sharding import PartitionSpec as P

HEADS = 12
HEAD_DIM = 64
BUCKETS = 32
PROMPT = 100
ADAM_STEP = 10
BOUNDS = (1, 2, 3, 4, 5, 6, 7, 8, 12, 16, 23, 32, 46, 64, 91)
EPSILON = 1e-06
MASKED = -1e30
LOG2E = 1.4426950408889634
LN2 = 0.6931471805599453
GELU_C = 0.7978845608028654

BLK = 256
TILE = 128
GROUP = 4
BF = jnp.bfloat16
F32 = jnp.float32
NN = (((1,), (0,)), ((), ()))
NT = (((1,), (1,)), ((), ()))
TN = (((0,), (0,)), ((), ()))
MESH = pl.DeviceIdType.MESH
VMEM_LIMIT = 62 * 1024 * 1024
SMEM_SPEC = pl.BlockSpec(memory_space=pltpu.SMEM)
VMEM_SPEC = pl.BlockSpec(memory_space=pltpu.VMEM)
ANY_SPEC = pl.BlockSpec(memory_space=pl.ANY)


def mm(left, right, dims):
    return lax.dot_general(left, right, dims, preferred_element_type=F32)


def bucket_of(offset, half):
    distance = jnp.abs(offset)
    counted = sum(((distance >= limit).astype(jnp.int32) for limit in BOUNDS))
    return counted + jnp.where(offset > 0, half, 0).astype(jnp.int32)


def span(block, size=BLK):
    return pl.ds(pl.multiple_of(block * size, size), size)


def low_lanes(width=TILE):
    return lax.rem(lax.broadcasted_iota(jnp.int32, (1, width), 1), TILE) < HEAD_DIM


def fill_bias(line_ref, tiles_ref):
    def one(head, carry):
        row = line_ref[pl.ds(head, 1), :]
        wide = pltpu.roll(
            jnp.broadcast_to(row, (BLK, 4 * BLK)), 0, 1, stride=1, stride_axis=0
        )
        for near in range(1, 4):
            tiles_ref[head, near] = wide[:, near * BLK : (near + 1) * BLK]
        tiles_ref[head, 0] = jnp.broadcast_to(row[:, 0:1], (BLK, BLK))
        tiles_ref[head, 4] = jnp.broadcast_to(row[:, 4 * BLK - 1 :], (BLK, BLK))
        return carry

    lax.fori_loop(0, HEADS, one, 0)


def rms_factor(values):
    return lax.rsqrt(jnp.mean(values * values, axis=-1, keepdims=True) + EPSILON)


def forward_kernel(
    lo_ref, hi_ref, tok_ref, hot_ref, isp_ref, live_ref, prompt_ref, gain_ref, line_ref, qa_ref,
    ka_ref, w_hbm,
    x_ref, kv_ref, q_ref, ctx_ref, lse_ref,
    w_ref, tiles_ref, norm_ref, lsem_ref, mean_ref, sems,
):
    slots = tok_ref.shape[0]
    groups = w_hbm.shape[0]
    half = w_hbm.shape[2] // 2
    copies = [pltpu.make_async_copy(w_hbm.at[m], w_ref.at[m], sems.at[m]) for m in range(groups)]
    for copy in copies:
        copy.start()
    fill_bias(line_ref, tiles_ref)
    gain = gain_ref[...]
    for first in range(0, slots, BLK):
        rows = slice(first, first + BLK)
        placed = mm(hot_ref[rows, :], prompt_ref[...], NN)
        value = jnp.where(isp_ref[rows, :] > 0, placed, tok_ref[rows, :].astype(F32))
        x_ref[rows, :] = value
        norm_ref[rows, :] = (value * rms_factor(value) * gain).astype(BF)
    low = low_lanes(half)
    for m in range(groups):
        copies[m].wait()
        cols = slice(m * half, (m + 1) * half)
        parts = [mm(norm_ref[f : f + BLK, :], w_ref[m], NN) for f in range(0, slots, BLK)]
        for i, part in enumerate(parts):
            rows = slice(i * BLK, (i + 1) * BLK)
            kv_ref[rows, cols] = part[:, :half].astype(BF)
            q_ref[rows, cols] = jnp.where(low, part[:, half:] * LOG2E, 0.0).astype(BF)
    mean_ref[...] = mm(jnp.full((8, slots), 1.0 / slots, BF), kv_ref[...], NN)
    high = jnp.logical_not(low_lanes())
    lane = lax.broadcasted_iota(jnp.int32, (1, TILE), 1)
    ones = jnp.ones((BLK, TILE), BF)

    def query_block(qb, carry):
        qs = span(qb)
        lo = lo_ref[qb]
        count = hi_ref[qb] - lo
        alive = live_ref[qs, :] > 0
        lsem_ref[...] = jnp.zeros_like(lsem_ref)

        def attend(width):
            def group_body(g, inner):
                heads = [g * GROUP + i for i in range(GROUP)]
                cols = [span(h, TILE) for h in heads]
                key_spans = [span(lo + j) for j in range(width)]
                kinds = [jnp.clip(lo + j - qb, -2, 2) + 2 for j in range(width)]
                query_mask = qa_ref[qs, :]
                key_masks = [ka_ref[ks, :] for ks in key_spans]
                scores = []
                for h, c in zip(heads, cols):
                    query = jnp.concatenate([q_ref[qs, c], query_mask], axis=1)
                    scores.append(
                        [
                            mm(query, jnp.concatenate([kv_ref[ks, c], km], axis=1), NT)
                            + tiles_ref[h, kind]
                            for ks, km, kind in zip(key_spans, key_masks, kinds)
                        ]
                    )
                tops = []
                weights = []
                for row in scores:
                    top = functools.reduce(jnp.maximum, row)
                    top = jnp.max(top, axis=1, keepdims=True)
                    tops.append(top)
                    weights.append(
                        jnp.concatenate([jnp.exp2(s - top).astype(BF) for s in row], axis=1)
                    )
                for h, c, top, weight in zip(heads, cols, tops, weights):
                    values = jnp.concatenate(
                        [
                            jnp.concatenate([kv_ref[ks, c] for ks in key_spans], axis=0),
                            jnp.concatenate([ones] * width, axis=0),
                        ],
                        axis=1,
                    )
                    both = mm(weight, values, NN)
                    total = both[:, TILE:]
                    context = jnp.where(alive, both[:, :TILE] / total, mean_ref[0:1, c])
                    ctx_ref[qs, c] = jnp.where(high, context, 0.0).astype(BF)
                    lsem_ref[...] = jnp.where(
                        (lane == h) & alive, top + jnp.log2(total), lsem_ref[...]
                    )
                return inner

            lax.fori_loop(0, HEADS // GROUP, group_body, 0)

        for width in range(1, slots // BLK + 1):
            pl.when(count == width)(functools.partial(attend, width))

        @pl.when(count == 0)
        def _():
            every = jnp.logical_not(low_lanes(HEADS * TILE))
            ctx_ref[qs, :] = jnp.broadcast_to(
                jnp.where(every, mean_ref[0:1, :], 0.0), (BLK, HEADS * TILE)
            ).astype(BF)

        lse_ref[:, qs] = lsem_ref[...].T[0:16]
        return carry

    lax.fori_loop(0, slots // BLK, query_block, 0)


def forward_call(lo, hi, tok, hot, isp, live, prompt, gain, line, qa, ka, w):
    slots, width = tok.shape
    wide = HEADS * TILE
    return pl.pallas_call(
        forward_kernel,
        in_specs=[SMEM_SPEC] * 2 + [VMEM_SPEC] * 9 + [ANY_SPEC],
        out_specs=[VMEM_SPEC] * 5,
        out_shape=[
            jax.ShapeDtypeStruct((slots, width), F32),
            jax.ShapeDtypeStruct((slots, wide), BF),
            jax.ShapeDtypeStruct((slots, wide), BF),
            jax.ShapeDtypeStruct((slots, wide), BF),
            jax.ShapeDtypeStruct((16, slots), F32),
        ],
        scratch_shapes=[
            pltpu.VMEM(w.shape, BF),
            pltpu.VMEM((HEADS, 5, BLK, BLK), F32),
            pltpu.VMEM((slots, width), BF),
            pltpu.VMEM((BLK, TILE), F32),
            pltpu.VMEM((8, wide), F32),
            pltpu.SemaphoreType.DMA((w.shape[0],)),
        ],
        compiler_params=pltpu.CompilerParams(vmem_limit_bytes=VMEM_LIMIT),
        name="embed_attend",
    )(lo, hi, tok, hot, isp, live, prompt, gain, line, qa, ka, w)


def gelu_both(inner, upstream):
    square = inner * inner
    bent = jnp.tanh(inner * (GELU_C + (GELU_C * 0.044715) * square))
    half = 0.5 + 0.5 * bent
    activated = inner * half
    slope = half + activated * ((1.0 - half) * (2 * GELU_C + (6 * GELU_C * 0.044715) * square))
    return activated.astype(BF), (upstream * slope).astype(BF)


def feed_kernel(
    x_ref, og_ref, live_ref, gain_ref, ctx_hbm, w_hbm, wi_hbm, wo_hbm,
    out_ref, gh_ref,
    ctx_ref, w_ref, wi_ref, wo_ref, norm_ref, gb_ref, hid_ref, br_ref, dn_ref, sems,
):
    slots = x_ref.shape[0]
    groups = w_hbm.shape[0]
    half = w_hbm.shape[2] // 2
    first = [pltpu.make_async_copy(ctx_hbm, ctx_ref, sems.at[0])]
    for m in range(groups):
        first.append(
            pltpu.make_async_copy(w_hbm.at[m, :, half:], w_ref.at[m], sems.at[1 + m])
        )
    later = []
    for m in range(groups):
        later.append(
            (
                pltpu.make_async_copy(wi_hbm.at[m], wi_ref.at[m], sems.at[1 + groups + 2 * m]),
                pltpu.make_async_copy(wo_hbm.at[m], wo_ref.at[m], sems.at[2 + groups + 2 * m]),
            )
        )
    for copy in first:
        copy.start()
    for pair in later:
        pair[0].start()
        pair[1].start()
    for copy in first:
        copy.wait()
    gain = gain_ref[...]
    blocks = [slice(f, f + BLK) for f in range(0, slots, BLK)]
    for rows in blocks:
        hid_ref[rows, :] = x_ref[rows, :]
    for m in range(groups):
        cols = slice(m * half, (m + 1) * half)
        for rows in blocks:
            hid_ref[rows, :] += mm(ctx_ref[rows, cols], w_ref[m], NT)
    for rows in blocks:
        hidden = hid_ref[rows, :]
        norm_ref[rows, :] = (hidden * rms_factor(hidden) * gain).astype(BF)
        gb_ref[rows, :] = (og_ref[rows, :].astype(F32) * live_ref[rows, :]).astype(BF)
    br_ref[...] = jnp.zeros_like(br_ref)
    dn_ref[...] = jnp.zeros_like(dn_ref)
    for m in range(groups):
        later[m][0].wait()
        later[m][1].wait()
    def unit_block(m, carry):
        inner = [mm(norm_ref[rows, :], wi_ref[m], NN) for rows in blocks]
        upstream = [mm(gb_ref[rows, :], wo_ref[m], NN) for rows in blocks]
        pairs = [gelu_both(a, b) for a, b in zip(inner, upstream)]
        for rows, (activated, grad_inner) in zip(blocks, pairs):
            br_ref[rows, :] += mm(activated, wo_ref[m], NT)
            dn_ref[rows, :] += mm(grad_inner, wi_ref[m], NT)
        return carry

    lax.fori_loop(0, groups, unit_block, 0)
    for rows in blocks:
        hidden = hid_ref[rows, :]
        alive = live_ref[rows, :]
        out_ref[rows, :] = (alive * (hidden + br_ref[rows, :])).astype(BF)
        factor = rms_factor(hidden)
        weighted = dn_ref[rows, :] * gain
        gh_ref[rows, :] = og_ref[rows, :].astype(F32) * alive + (
            factor * weighted
            - hidden
            * (factor * factor * factor)
            * jnp.mean(weighted * hidden, axis=-1, keepdims=True)
        )


def feed_call(x, og, live, gain, ctx, w, wi, wo):
    slots, width = x.shape
    groups = w.shape[0]
    return pl.pallas_call(
        feed_kernel,
        in_specs=[VMEM_SPEC] * 4 + [ANY_SPEC] * 4,
        out_specs=[VMEM_SPEC] * 2,
        out_shape=[
            jax.ShapeDtypeStruct((slots, width), BF),
            jax.ShapeDtypeStruct((slots, width), F32),
        ],
        scratch_shapes=[
            pltpu.VMEM(ctx.shape, BF),
            pltpu.VMEM((groups, w.shape[1], w.shape[2] // 2), BF),
            pltpu.VMEM(wi.shape, BF),
            pltpu.VMEM(wo.shape, BF),
            pltpu.VMEM((slots, width), BF),
            pltpu.VMEM((slots, width), BF),
            pltpu.VMEM((slots, width), F32),
            pltpu.VMEM((slots, width), F32),
            pltpu.VMEM((slots, width), F32),
            pltpu.SemaphoreType.DMA((1 + 3 * groups,)),
        ],
        compiler_params=pltpu.CompilerParams(vmem_limit_bytes=VMEM_LIMIT),
        name="feed_forward",
    )(x, og, live, gain, ctx, w, wi, wo)


def backward_kernel(
    lo_ref, hi_ref, gh_ref, kv_ref, lse_ref, line_ref, qa_ref, ka_ref, w_hbm, q_hbm, ctx_hbm,
    x_hbm, hot_hbm, isp_ref, gain_ref,
    ig_ref, pg_ref,
    w_ref, q_ref, ctx_ref, x_ref, hot_ref, tiles_ref, all_ref, kt_ref, dsum_ref, dqt_ref, acc_ref, sems,
):
    slots = gh_ref.shape[0]
    groups = w_hbm.shape[0]
    half = w_hbm.shape[2] // 2
    per = HEADS // groups
    weights = [pltpu.make_async_copy(w_hbm.at[m], w_ref.at[m], sems.at[m]) for m in range(groups)]
    ctx_copy = pltpu.make_async_copy(ctx_hbm, ctx_ref, sems.at[groups])
    x_copy = pltpu.make_async_copy(x_hbm, x_ref, sems.at[groups + 1])
    hot_copy = pltpu.make_async_copy(hot_hbm, hot_ref, sems.at[groups + 2])
    q_copy = pltpu.make_async_copy(q_hbm, q_ref, sems.at[groups + 3])
    for copy in weights + [q_copy, ctx_copy, x_copy, hot_copy]:
        copy.start()
    fill_bias(line_ref, tiles_ref)
    blocks = [slice(f, f + BLK) for f in range(0, slots, BLK)]
    low_half = low_lanes(half)
    q_copy.wait()
    for m in range(groups):
        weights[m].wait()
        cols = slice(m * half, (m + 1) * half)
        parts = [mm(gh_ref[rows, :].astype(BF), w_ref[m, :, half:], NN) for rows in blocks]
        for rows, part in zip(blocks, parts):
            q_ref[rows, cols] = jnp.where(low_half, q_ref[rows, cols], part.astype(BF))
    ctx_copy.wait()
    wide = HEADS * TILE
    pick = (
        lax.broadcasted_iota(jnp.int32, (16, wide), 1) // TILE
        == lax.broadcasted_iota(jnp.int32, (16, wide), 0)
    ).astype(F32).astype(BF)
    for rows in blocks:
        product = q_ref[rows, :].astype(F32) * ctx_ref[rows, :].astype(F32)
        upper = product.astype(BF)
        lower = (product - upper.astype(F32)).astype(BF)
        dsum_ref[:, rows] = mm(pick, upper, NT) + mm(pick, lower, NT)
    for h in range(HEADS):
        kt_ref[h] = kv_ref[:, h * TILE : (h + 1) * TILE].T[0:HEAD_DIM]
    low = low_lanes()
    zero = jnp.zeros((BLK, TILE), BF)

    def group_body(g, carry):
        heads = [g * GROUP + i for i in range(GROUP)]
        cols = [span(h, TILE) for h in heads]
        dqt_ref[...] = jnp.zeros_like(dqt_ref)

        def key_block(kb, inner):
            ks = span(kb)
            acc_ref[...] = jnp.zeros_like(acc_ref)

            def query_block(qb, deep):
                qs = span(qb)
                kind = jnp.clip(qb - kb, -2, 2) + 2
                query_mask = qa_ref[qs, :]
                key_mask = ka_ref[ks, :]
                both = [q_ref[qs, c] for c in cols]
                keys = [kv_ref[ks, c] for c in cols]
                scores = [
                    mm(
                        jnp.concatenate([key, key_mask], axis=1),
                        jnp.concatenate([jnp.where(low, pair, zero), query_mask], axis=1),
                        NT,
                    )
                    + tiles_ref[h, kind]
                    for h, key, pair in zip(heads, keys, both)
                ]
                grads = [
                    mm(key, jnp.where(low, zero, pair), NT) for key, pair in zip(keys, both)
                ]
                probs = [
                    jnp.exp2(s - lse_ref[pl.ds(h, 1), qs]) for h, s in zip(heads, scores)
                ]
                outs = [
                    (p * (d - dsum_ref[pl.ds(h, 1), qs])).astype(BF)
                    for h, p, d in zip(heads, probs, grads)
                ]
                lows = [p.astype(BF) for p in probs]
                for i, h in enumerate(heads):
                    acc_ref[i] += jnp.where(
                        low, mm(outs[i], both[i], NN), mm(lows[i], both[i], NN)
                    )
                    dqt_ref[i, 0:HEAD_DIM, qs] += mm(kt_ref[h, :, ks], outs[i], NN)
                return deep

            lax.fori_loop(lo_ref[kb], hi_ref[kb], query_block, 0)
            for i, h in enumerate(heads):
                place = lax.div(h, per) * (2 * half) + lax.rem(h, per) * TILE
                all_ref[ks, pl.ds(pl.multiple_of(place, TILE), TILE)] = (
                    acc_ref[i] * jnp.where(low, LN2, 1.0)
                ).astype(BF)
            return inner

        lax.fori_loop(0, slots // BLK, key_block, 0)
        for i, h in enumerate(heads):
            place = lax.div(h, per) * (2 * half) + half + lax.rem(h, per) * TILE
            all_ref[:, pl.ds(pl.multiple_of(place, TILE), TILE)] = dqt_ref[i].astype(BF).T
        return carry

    lax.fori_loop(0, HEADS // GROUP, group_body, 0)
    x_copy.wait()
    hot_copy.wait()
    gain = gain_ref[...]
    pg_ref[...] = jnp.zeros_like(pg_ref)
    for rows in blocks:
        back = functools.reduce(
            jnp.add,
            [
                mm(all_ref[rows, m * 2 * half : (m + 1) * 2 * half], w_ref[m], NT)
                for m in range(groups)
            ],
        )
        value = x_ref[rows, :]
        factor = rms_factor(value)
        weighted = back * gain
        grad = gh_ref[rows, :] + (
            factor * weighted
            - value
            * (factor * factor * factor)
            * jnp.mean(weighted * value, axis=-1, keepdims=True)
        )
        ig_ref[rows, :] = jnp.where(isp_ref[rows, :] > 0, 0.0, grad)
        upper = grad.astype(BF)
        lower = (grad - upper.astype(F32)).astype(BF)
        hot = hot_ref[rows, :]
        pg_ref[...] += mm(hot, upper, TN) + mm(hot, lower, TN)


def backward_call(lo, hi, gh, q, kv, lse, line, qa, ka, w, ctx, x, hot, isp, gain):
    slots, width = gh.shape
    groups = w.shape[0]
    return pl.pallas_call(
        backward_kernel,
        in_specs=[SMEM_SPEC] * 2 + [VMEM_SPEC] * 6 + [ANY_SPEC] * 5 + [VMEM_SPEC] * 2,
        out_specs=[VMEM_SPEC] * 2,
        out_shape=[
            jax.ShapeDtypeStruct((slots, width), F32),
            jax.ShapeDtypeStruct((TILE, width), F32),
        ],
        scratch_shapes=[
            pltpu.VMEM(w.shape, BF),
            pltpu.VMEM(q.shape, BF),
            pltpu.VMEM(ctx.shape, BF),
            pltpu.VMEM(x.shape, F32),
            pltpu.VMEM(hot.shape, BF),
            pltpu.VMEM((HEADS, 5, BLK, BLK), F32),
            pltpu.VMEM((slots, 2 * HEADS * TILE), BF),
            pltpu.VMEM((HEADS, HEAD_DIM, slots), BF),
            pltpu.VMEM((16, slots), F32),
            pltpu.VMEM((GROUP, TILE, slots), F32),
            pltpu.VMEM((GROUP, BLK, TILE), F32),
            pltpu.SemaphoreType.DMA((groups + 4,)),
        ],
        compiler_params=pltpu.CompilerParams(vmem_limit_bytes=VMEM_LIMIT),
        name="attend_back",
    )(lo, hi, gh, kv, lse, line, qa, ka, w, q, ctx, x, hot, isp, gain)


def slot_arrays(segments, live):
    slots = segments.shape[0]
    place = jnp.arange(slots, dtype=jnp.int32)
    first = jnp.sum((segments[None, :] < segments[:, None]).astype(jnp.int32), axis=1)
    position = place - first
    is_prompt = (live == 1) & (position < PROMPT)
    lane = jnp.arange(TILE, dtype=jnp.int32)[None, :]
    hot = ((position[:, None] == lane) & is_prompt[:, None]).astype(BF)
    same = segments[:, None] == lane
    query_side = same.astype(BF)
    reach = same & (live[:, None] == 1)
    key_side = jnp.where((lane < 16) & jnp.logical_not(reach), MASKED, 0.0).astype(BF)
    by_block = segments.reshape(-1, BLK)
    top = jnp.max(jnp.where(live.reshape(-1, BLK) == 1, by_block, -1), axis=1)
    hi = jnp.sum((segments[None, :] <= top[:, None]) & (live[None, :] == 1), axis=1)
    hi = (hi.astype(jnp.int32) + BLK - 1) // BLK
    lo = jnp.sum((segments[None, :] < by_block[:, :1]).astype(jnp.int32), axis=1) // BLK
    return hot, is_prompt, query_side, key_side, jnp.minimum(lo, hi), hi


def bias_lines(table):
    offset = jnp.arange(4 * BLK, dtype=jnp.int32) - 2 * BLK
    code = jnp.arange(BUCKETS, dtype=jnp.int32)[:, None]
    lines = []
    for sign in (1, -1):
        hot = (bucket_of(sign * offset, BUCKETS // 2)[None, :] == code).astype(F32)
        line = jnp.einsum("bh,bx->hx", table.astype(F32), hot, precision=lax.Precision.HIGHEST)
        lines.append(jnp.pad(line * LOG2E, ((0, 16 - HEADS), (0, 0))))
    return lines


def tiles_of(first, second):
    rows = first.shape[0]
    shaped = [part.reshape(rows, -1, 1, HEAD_DIM) for part in (first, second)]
    return jnp.concatenate(shaped, axis=2).reshape(rows, -1)


def neighbours():
    dp = lax.axis_index("dp")
    core = lax.rem(dp, 2)
    across = lax.rem(lax.div(dp, 2), 2)
    down = lax.div(dp, 4)
    return (
        dp + 1 - 2 * core,
        dp + 2 - 4 * across,
        dp + 4 - 8 * down,
        dp + 6 - 4 * across - 8 * down,
    )


def gather_kernel(
    small_ref, w_ref, small_out, w_out, own_sem, z_send, z_recv, send, recv
):
    mp = lax.axis_index("mp")
    dp = lax.axis_index("dp")
    depth = w_out.shape[1]
    sib, east, south, corner = neighbours()
    barrier = pltpu.get_barrier_semaphore()
    peers = [{"dp": sib}, {"dp": east}, {"dp": south}]
    for step in range(1, depth):
        peers.append({"mp": lax.rem(mp + step, depth)})
    for peer in peers:
        pl.semaphore_signal(barrier, inc=1, device_id=peer, device_id_type=MESH)
    pl.semaphore_wait(barrier, len(peers))

    units = [(small_ref, small_out)]
    for t in range(w_ref.shape[0]):
        units.append((w_ref.at[t], w_out.at[t]))

    def remote(src, dst, send_sem, recv_sem, peer):
        return pltpu.make_async_remote_copy(
            src_ref=src, dst_ref=dst, send_sem=send_sem, recv_sem=recv_sem,
            device_id=peer, device_id_type=MESH,
        )

    started = []
    own = []
    arrivals = {}
    for u, (src, dst) in enumerate(units):
        copy = pltpu.make_async_copy(src, dst.at[mp, dp], own_sem.at[u])
        copy.start()
        own.append(copy)
        for step in range(1, depth):
            copy = remote(
                src, dst.at[mp, dp], z_send.at[u, step - 1], z_recv.at[u, depth - step - 1],
                {"mp": lax.rem(mp + step, depth)},
            )
            copy.start()
            started.append(copy)

    def push(u, o, kind, src, dst, peer):
        copy = remote(src, dst, send.at[u, o, kind], recv.at[u, o, kind], peer)
        copy.start()
        started.append(copy)

    def landed(u, o, kind, dst, half=None):
        remote(dst, dst, send.at[u, o, kind], recv.at[u, o, kind], {"dp": sib}).wait_recv()

    def step(u, o):
        src, dst = units[u]
        z = lax.rem(mp + o, depth)
        block = dst.at[z, dp]
        if o:
            remote(
                block, block, z_send.at[u, o - 1], z_recv.at[u, o - 1], {"dp": sib}
            ).wait_recv()
            src = block
        push(u, o, 0, src, block, {"dp": east})
        push(u, o, 1, src, block, {"dp": south})
        push(u, o, 2, src, block, {"dp": sib})

    def forward(u, o):
        dst = units[u][1]
        z = lax.rem(mp + o, depth)
        rows = dst.shape[2] // 2
        landed(u, o, 0, dst.at[z, east])
        push(u, o, 3, dst.at[z, east, 0:rows], dst.at[z, east, 0:rows], {"dp": south})
        push(u, o, 4, dst.at[z, east], dst.at[z, east], {"dp": sib})
        landed(u, o, 1, dst.at[z, south])
        push(u, o, 5, dst.at[z, south, rows:], dst.at[z, south, rows:], {"dp": east})
        push(u, o, 6, dst.at[z, south], dst.at[z, south], {"dp": sib})

    def finish(u, o):
        dst = units[u][1]
        z = lax.rem(mp + o, depth)
        rows = dst.shape[2] // 2
        landed(u, o, 3, dst.at[z, corner, 0:rows])
        landed(u, o, 5, dst.at[z, corner, rows:])
        push(u, o, 7, dst.at[z, corner], dst.at[z, corner], {"dp": sib})

    order = [(u, o) for u in range(len(units)) for o in range(depth)]
    for i in range(len(order) + 2):
        if i < len(order):
            step(*order[i])
        if 0 <= i - 1 < len(order):
            forward(*order[i - 1])
        if 0 <= i - 2:
            finish(*order[i - 2])
    flip = 1 - 2 * lax.rem(dp, 2)
    for u, o in order:
        dst = units[u][1]
        z = lax.rem(mp + o, depth)
        landed(u, o, 2, dst.at[z, sib])
        landed(u, o, 4, dst.at[z, east + flip])
        landed(u, o, 6, dst.at[z, south + flip])
        landed(u, o, 7, dst.at[z, corner + flip])
    for copy in own:
        copy.wait()
    for copy in started:
        copy.wait_send()


def gather_call(small, packs, dp, mp):
    count = packs.shape[0] + 1
    return pl.pallas_call(
        gather_kernel,
        in_specs=[ANY_SPEC] * 2,
        out_specs=[ANY_SPEC] * 2,
        out_shape=[
            jax.ShapeDtypeStruct((mp, dp) + small.shape, BF),
            jax.ShapeDtypeStruct((packs.shape[0], mp, dp) + packs.shape[1:], BF),
        ],
        scratch_shapes=[
            pltpu.SemaphoreType.DMA((count,)),
            pltpu.SemaphoreType.DMA((count, mp - 1)),
            pltpu.SemaphoreType.DMA((count, mp - 1)),
            pltpu.SemaphoreType.DMA((count, mp, 8)),
            pltpu.SemaphoreType.DMA((count, mp, 8)),
        ],
        compiler_params=pltpu.CompilerParams(collective_id=0, has_side_effects=True),
        name="gather_weights",
    )(small, packs)


def adam_kernel(
    part_ref, state_ref, out_ref, land_one, land_two, mid_ref, send_one, recv_one, send_two,
    recv_two,
):
    dp = lax.axis_index("dp")
    mp = lax.axis_index("mp")
    wide = part_ref.shape[0]
    deep = part_ref.shape[1]
    barrier = pltpu.get_barrier_semaphore()
    peers = [{"dp": lax.rem(dp + s, wide)} for s in range(1, wide)]
    peers += [{"mp": lax.rem(mp + s, deep)} for s in range(1, deep)]
    for peer in peers:
        pl.semaphore_signal(barrier, inc=1, device_id=peer, device_id_type=MESH)
    pl.semaphore_wait(barrier, len(peers))
    first = []
    for s in range(1, wide):
        to = lax.rem(dp + s, wide)
        copy = pltpu.make_async_remote_copy(
            src_ref=part_ref.at[to], dst_ref=land_one.at[s - 1],
            send_sem=send_one.at[s - 1], recv_sem=recv_one.at[s - 1],
            device_id={"dp": to}, device_id_type=MESH,
        )
        copy.start()
        first.append(copy)
    total = part_ref[dp]
    for s, copy in enumerate(first):
        copy.wait_recv()
        total = total + land_one[s]
    mid_ref[...] = total
    second = []
    for s in range(1, deep):
        to = lax.rem(mp + s, deep)
        copy = pltpu.make_async_remote_copy(
            src_ref=mid_ref.at[to], dst_ref=land_two.at[s - 1],
            send_sem=send_two.at[s - 1], recv_sem=recv_two.at[s - 1],
            device_id={"mp": to}, device_id_type=MESH,
        )
        copy.start()
        second.append(copy)
    grad = mid_ref[mp]
    for s, copy in enumerate(second):
        copy.wait_recv()
        grad = grad + land_two[s]
    out_ref[...] = jnp.stack(adam_step(grad, state_ref[0], state_ref[1], state_ref[2]))
    for copy in first + second:
        copy.wait_send()


def adam_step(grad, prompt, moment_one, moment_two):
    first_new = 0.9 * moment_one + 0.1 * grad
    second_new = 0.999 * moment_two + 0.001 * grad * grad
    correct_one = 1.0 - 0.9**ADAM_STEP
    correct_two = 1.0 - 0.999**ADAM_STEP
    prompt_new = prompt - 0.3 * (first_new / correct_one) / (
        jnp.sqrt(second_new / correct_two) + 1e-08
    )
    return prompt_new, first_new, second_new


def adam_call(part, state):
    wide, deep, rows, cols = part.shape
    return pl.pallas_call(
        adam_kernel,
        in_specs=[VMEM_SPEC] * 2,
        out_specs=VMEM_SPEC,
        out_shape=jax.ShapeDtypeStruct(state.shape, F32),
        scratch_shapes=[
            pltpu.VMEM((wide - 1, deep, rows, cols), F32),
            pltpu.VMEM((deep - 1, rows, cols), F32),
            pltpu.VMEM((deep, rows, cols), F32),
            pltpu.SemaphoreType.DMA((wide - 1,)),
            pltpu.SemaphoreType.DMA((wide - 1,)),
            pltpu.SemaphoreType.DMA((deep - 1,)),
            pltpu.SemaphoreType.DMA((deep - 1,)),
        ],
        compiler_params=pltpu.CompilerParams(collective_id=1, has_side_effects=True),
        name="sum_and_step",
    )(part, state)


def body(
    dp, mp, tokens, prompt, moment_one, moment_two, segments, live, out_grad, w_query, w_key,
    w_value, w_output, w_inner, w_outer, gain_attn, gain_ffn, rel_table,
):
    _, slots, width = tokens.shape
    tuned = (dp, mp) == (8, 4)
    share = prompt.shape[0]
    packs = jnp.stack(
        [
            jnp.concatenate([tiles_of(w_key, w_value), tiles_of(w_query, w_output.T)], axis=1),
            w_inner,
            w_outer.T,
        ]
    )
    flat = jnp.concatenate(
        [prompt.astype(BF), gain_attn, gain_ffn, rel_table.reshape(-1)]
    )
    if tuned:
        small = jnp.pad(flat, (0, -flat.shape[0] % (32 * TILE))).reshape(-1, TILE)
        small_all, weights = gather_call(small, packs, dp, mp)
        small_all = small_all.reshape(mp, dp, -1)
        weights = weights.reshape(3, mp, width, -1)
    else:
        small_all = lax.all_gather(lax.all_gather(flat, "dp"), "mp")
        weights = lax.all_gather(
            lax.all_gather(packs, "dp", axis=1, tiled=True), "mp", axis=1
        )
    part = gain_attn.shape[0]
    prompt_all = small_all[:, :, :share].transpose(1, 0, 2).reshape(PROMPT, width)
    prompt_all = jnp.pad(prompt_all, ((0, TILE - PROMPT), (0, 0)))
    attn_gain = small_all[0, :, share : share + part].reshape(1, width).astype(F32)
    ffn_gain = small_all[0, :, share + part : share + 2 * part].reshape(1, width).astype(F32)
    table = small_all[:, 0, share + 2 * part : share + 2 * part + rel_table.size]
    table = table.reshape(mp, BUCKETS, -1).transpose(1, 0, 2).reshape(BUCKETS, HEADS)
    ahead, behind = bias_lines(table)
    hot, is_prompt, query_side, key_side, lo, hi = slot_arrays(segments[0], live[0])
    isp = is_prompt[:, None].astype(F32)
    alive = live[0][:, None].astype(F32)
    x, kv, q, ctx, lse = forward_call(
        lo, hi, tokens[0], hot, isp, alive, prompt_all, attn_gain, ahead, query_side, key_side,
        weights[0],
    )
    layer_output, grad_hidden = feed_call(
        x, out_grad[0], alive, ffn_gain, ctx, weights[0], weights[1], weights[2]
    )
    input_grad, prompt_part = backward_call(
        lo, hi, grad_hidden, q, kv, lse, behind, query_side, key_side, weights[0], ctx, x, hot,
        isp, attn_gain,
    )
    flat_part = prompt_part[:PROMPT].reshape(dp, mp, share)
    if tuned:
        fill = -share % (8 * TILE)
        flat_part = jnp.pad(flat_part, ((0, 0), (0, 0), (0, fill)))
        state = jnp.pad(jnp.stack([prompt, moment_one, moment_two]), ((0, 0), (0, fill)))
        stepped = adam_call(
            flat_part.reshape(dp, mp, -1, TILE), state.reshape(3, -1, TILE)
        )
        stepped = stepped.reshape(3, -1)[:, :share]
        prompt_new, first_new, second_new = stepped[0], stepped[1], stepped[2]
    else:
        grad = lax.psum_scatter(
            flat_part.reshape(-1), ("dp", "mp"), scatter_dimension=0, tiled=True
        )
        prompt_new, first_new, second_new = adam_step(grad, prompt, moment_one, moment_two)
    return (layer_output[None], input_grad[None], prompt_new, first_new, second_new)


def solution(mesh):
    both = ("dp", "mp")
    return jax.shard_map(
        functools.partial(body, mesh.shape["dp"], mesh.shape["mp"]),
        mesh=mesh,
        in_specs=(
            P(both, None, None),
            P(both),
            P(both),
            P(both),
            P(both, None),
            P(both, None),
            P(both, None, None),
            P("dp", "mp"),
            P("dp", "mp"),
            P("dp", "mp"),
            P("mp", "dp"),
            P("dp", "mp"),
            P("mp", "dp"),
            P("dp"),
            P("dp"),
            P(None, "mp"),
        ),
        out_specs=(
            P(both, None, None),
            P(both, None, None),
            P(both),
            P(both),
            P(both),
        ),
        check_vma=False,
    )
```

```python
import functools

import jax
import jax.numpy as jnp
from jax import lax
from jax.experimental import pallas as pl
from jax.experimental.pallas import tpu as pltpu
from jax.sharding import PartitionSpec as P

HEADS = 12
HEAD_DIM = 64
BUCKETS = 32
PROMPT = 100
ADAM_STEP = 10
BOUNDS = (1, 2, 3, 4, 5, 6, 7, 8, 12, 16, 23, 32, 46, 64, 91)
EPSILON = 1e-06
MASKED = -1e30
LOG2E = 1.4426950408889634
LN2 = 0.6931471805599453
GELU_C = 0.7978845608028654

BLK = 256
TILE = 128
GROUP = 4
ALIVE = 126
IS_PROMPT = 127
BF = jnp.bfloat16
F32 = jnp.float32
NN = (((1,), (0,)), ((), ()))
NT = (((1,), (1,)), ((), ()))
TN = (((0,), (0,)), ((), ()))
MESH = pl.DeviceIdType.MESH
VMEM_LIMIT = 62 * 1024 * 1024
SMEM_SPEC = pl.BlockSpec(memory_space=pltpu.SMEM)
VMEM_SPEC = pl.BlockSpec(memory_space=pltpu.VMEM)
ANY_SPEC = pl.BlockSpec(memory_space=pl.ANY)


def mm(left, right, dims):
    return lax.dot_general(left, right, dims, preferred_element_type=F32)


def bucket_of(offset, half):
    distance = jnp.abs(offset)
    counted = sum(((distance >= limit).astype(jnp.int32) for limit in BOUNDS))
    return counted + jnp.where(offset > 0, half, 0).astype(jnp.int32)


def span(block, size=BLK):
    return pl.ds(pl.multiple_of(block * size, size), size)


def low_lanes(width=TILE):
    return lax.rem(lax.broadcasted_iota(jnp.int32, (1, width), 1), TILE) < HEAD_DIM


def fill_bias(line_ref, tiles_ref):
    def one(head, carry):
        row = line_ref[pl.ds(head, 1), :]
        wide = pltpu.roll(
            jnp.broadcast_to(row, (BLK, 4 * BLK)), 0, 1, stride=1, stride_axis=0
        )
        for near in range(1, 4):
            tiles_ref[head, near] = wide[:, near * BLK : (near + 1) * BLK]
        tiles_ref[head, 0] = jnp.broadcast_to(row[:, 0:1], (BLK, BLK))
        tiles_ref[head, 4] = jnp.broadcast_to(row[:, 4 * BLK - 1 :], (BLK, BLK))
        return carry

    lax.fori_loop(0, HEADS, one, 0)


def rms_factor(values):
    return lax.rsqrt(jnp.mean(values * values, axis=-1, keepdims=True) + EPSILON)


def neighbours():
    dp = lax.axis_index("dp")
    core = lax.rem(dp, 2)
    across = lax.rem(lax.div(dp, 2), 2)
    down = lax.div(dp, 4)
    return (
        dp + 1 - 2 * core,
        dp + 2 - 4 * across,
        dp + 4 - 8 * down,
        dp + 6 - 4 * across - 8 * down,
    )


def place_rows(small, shift_flat, shift_gain):
    width = small.shape[1]
    lane = lax.broadcasted_iota(jnp.int32, (8, width), 1)
    row = lax.broadcasted_iota(jnp.int32, (8, width), 0)
    turned = pltpu.roll(small[0:8], shift_flat, 1)
    top = jnp.where(lane >= shift_flat, turned, pltpu.roll(turned, 1, 0))
    bottom = jnp.where(row < 2, pltpu.roll(small[8:16], shift_gain, 1), small[8:16])
    return jnp.concatenate([top, bottom], axis=0).astype(BF)


def interleave(first, second):
    parts = []
    for at in range(0, first.shape[1], HEAD_DIM):
        parts += [first[:, at : at + HEAD_DIM], second[:, at : at + HEAD_DIM]]
    return jnp.concatenate(parts, axis=1)


def open_kernel(
    small_ref, wq_ref, wk_ref, wv_ref, wo_ref, wi_ref, wu_ref, seg_ref, live_ref, tok_ref,
    w_out, own_out, line_out, near_out, x_out, kv_out, q_out,
    marks_ref, qa_ref, ka_ref, gains_ref, ahead_ref, behind_ref,
    small_src, small_v, pack_src, w_v, ff_src, x_v, norm_v, kv_v, q_v,
    own_sem, z_send, z_recv, send, recv, fz_send, fz_recv, fn_send, fn_recv, out_sem,
):
    mp = lax.axis_index("mp")
    dp = lax.axis_index("dp")
    depth, wide = w_v.shape[0], w_v.shape[1]
    sib, east, south, corner = neighbours()
    barrier = pltpu.get_barrier_semaphore()
    peers = [{"dp": sib}, {"dp": east}, {"dp": south}]
    for step in range(1, depth):
        peers.append({"mp": lax.rem(mp + step, depth)})
    for peer in peers:
        pl.semaphore_signal(barrier, inc=1, device_id=peer, device_id_type=MESH)

    share = lax.rem(dp * depth + mp, 8)
    small_src[...] = place_rows(small_ref[...], 96 * share, 96 * dp)
    pack_src[...] = jnp.concatenate(
        [interleave(wk_ref[...], wv_ref[...]), interleave(wq_ref[...], wo_ref[...].T)], axis=1
    )
    pl.semaphore_wait(barrier, len(peers))

    def remote(src, dst, send_sem, recv_sem, peer):
        return pltpu.make_async_remote_copy(
            src_ref=src, dst_ref=dst, send_sem=send_sem, recv_sem=recv_sem,
            device_id=peer, device_id_type=MESH,
        )

    started = []
    local = []
    units = [(small_src, small_v), (pack_src, w_v)]

    def push(u, o, kind, src, dst, peer):
        copy = remote(src, dst, send.at[u, o, kind], recv.at[u, o, kind], peer)
        copy.start()
        started.append(copy)

    def landed(u, o, kind, dst):
        remote(dst, dst, send.at[u, o, kind], recv.at[u, o, kind], {"dp": sib}).wait_recv()

    def spread(u):
        src, dst = units[u]
        for step in range(1, depth):
            copy = remote(
                src, dst.at[mp, dp], z_send.at[u, step - 1], z_recv.at[u, depth - step - 1],
                {"mp": lax.rem(mp + step, depth)},
            )
            copy.start()
            started.append(copy)

    def step(u, o):
        src, dst = units[u]
        z = lax.rem(mp + o, depth)
        block = dst.at[z, dp]
        if o:
            remote(
                block, block, z_send.at[u, o - 1], z_recv.at[u, o - 1], {"dp": sib}
            ).wait_recv()
            src = block
        push(u, o, 0, src, block, {"dp": east})
        push(u, o, 1, src, block, {"dp": south})
        push(u, o, 2, src, block, {"dp": sib})

    def forward(u, o):
        dst = units[u][1]
        z = lax.rem(mp + o, depth)
        rows = dst.shape[2] // 2 if u else dst.shape[2]
        landed(u, o, 0, dst.at[z, east])
        push(u, o, 3, dst.at[z, east, 0:rows], dst.at[z, east, 0:rows], {"dp": south})
        push(u, o, 4, dst.at[z, east], dst.at[z, east], {"dp": sib})
        landed(u, o, 1, dst.at[z, south])
        if u:
            push(u, o, 5, dst.at[z, south, rows:], dst.at[z, south, rows:], {"dp": east})
        push(u, o, 6, dst.at[z, south], dst.at[z, south], {"dp": sib})

    def finish(u, o):
        dst = units[u][1]
        z = lax.rem(mp + o, depth)
        rows = dst.shape[2] // 2 if u else dst.shape[2]
        landed(u, o, 3, dst.at[z, corner, 0:rows])
        if u:
            landed(u, o, 5, dst.at[z, corner, rows:])
        push(u, o, 7, dst.at[z, corner], dst.at[z, corner], {"dp": sib})

    flip = 1 - 2 * lax.rem(dp, 2)

    def complete(u, o):
        dst = units[u][1]
        z = lax.rem(mp + o, depth)
        landed(u, o, 2, dst.at[z, sib])
        landed(u, o, 4, dst.at[z, east + flip])
        landed(u, o, 6, dst.at[z, south + flip])
        landed(u, o, 7, dst.at[z, corner + flip])

    for u in range(2):
        spread(u)
        step(u, 0)
        src, dst = units[u]
        copy = pltpu.make_async_copy(src, dst.at[mp, dp], own_sem.at[u])
        copy.start()
        local.append(copy)
    ff_src[0] = wi_ref[...]
    ff_src[1] = wu_ref[...].T
    for step_z in range(1, depth):
        copy = remote(
            ff_src, line_out.at[depth - step_z - 1], fz_send.at[step_z - 1],
            fz_recv.at[depth - step_z - 1], {"mp": lax.rem(mp + step_z, depth)},
        )
        copy.start()
        started.append(copy)
    copy = pltpu.make_async_copy(ff_src, own_out, own_sem.at[2])
    copy.start()
    local.append(copy)

    slots = tok_ref.shape[0]
    segment_row = seg_ref[...].astype(F32)
    lane = lax.broadcasted_iota(jnp.int32, (slots, TILE), 1)
    lane_f = lane.astype(F32)
    segment = jnp.broadcast_to(segment_row, (TILE, slots)).T
    alive = jnp.broadcast_to(live_ref[...].astype(F32), (TILE, slots)).T
    same = segment == lane_f
    start = jnp.sum((segment < lane_f).astype(F32), axis=0, keepdims=True)
    first = jnp.sum(jnp.where(same, start, 0.0), axis=1, keepdims=True)
    position = lax.broadcasted_iota(jnp.int32, (slots, TILE), 0).astype(F32) - first
    prompt_slot = (alive > 0) & (position < PROMPT)
    marks = jnp.where((position == lane_f) & prompt_slot, 1.0, 0.0)
    marks = jnp.where(lane == ALIVE, alive, marks)
    marks = jnp.where(lane == IS_PROMPT, prompt_slot.astype(F32), marks)
    marks_ref[...] = marks.astype(BF)
    qa_ref[...] = same.astype(F32).astype(BF)
    ka_ref[...] = jnp.where(
        (lane < 16) & jnp.logical_not(same & (alive > 0)), MASKED, 0.0
    ).astype(BF)

    for o in range(1, depth):
        step(0, o)
    for o in range(depth):
        forward(0, o)
    step(1, 1)
    forward(1, 0)
    for o in range(depth):
        finish(0, o)
    for o in range(depth):
        complete(0, o)
    local[0].wait()
    step(1, 2)
    forward(1, 1)
    finish(1, 0)

    gains = functools.reduce(jnp.add, [small_v[0, d].astype(F32) for d in range(wide)])
    gains_ref[...] = gains
    table = jnp.concatenate(
        [small_v[m, 0].astype(F32)[10 : 10 + HEADS // depth, 0:TILE] for m in range(depth)]
        + [jnp.zeros((16 - HEADS, TILE), F32)],
        axis=0,
    ).astype(BF)
    span_x = ahead_ref.shape[1]
    offset = lax.broadcasted_iota(jnp.int32, (1, span_x), 1) - span_x // 2
    code = lax.broadcasted_iota(jnp.int32, (TILE, span_x), 0)
    for sign, out in ((1, ahead_ref), (-1, behind_ref)):
        hot = (code == bucket_of(sign * offset, BUCKETS // 2)).astype(F32).astype(BF)
        out[...] = mm(table, hot, NN) * LOG2E

    rows_all = depth * wide * 16
    at = lax.broadcasted_iota(jnp.int32, (1, rows_all), 1)
    inside = lax.rem(at, 16)
    holder = lax.div(at, 16)
    device = lax.rem(holder, wide) * depth + lax.div(holder, wide)
    target = 25 * lax.div(device, 8) + 3 * lax.rem(device, 8) + inside
    target = jnp.where(inside < 4, target, -1).astype(F32)
    windows = small_v[...].reshape(rows_all, small_v.shape[3])
    gain = gains[8:9]
    for f in range(0, slots, BLK):
        rows = slice(f, f + BLK)
        hot = (position[rows, 0:1] == target).astype(F32).astype(BF)
        placed = mm(hot, windows, NN)
        value = jnp.where(prompt_slot[rows, 0:1], placed, tok_ref[rows, :].astype(F32))
        x_v[rows, :] = value
        norm_v[rows, :] = (value * rms_factor(value) * gain).astype(BF)
    copy = pltpu.make_async_copy(x_v, x_out, out_sem.at[0])
    copy.start()
    local.append(copy)

    half = w_v.shape[3] // 2
    low = low_lanes(half)

    def project(o):
        complete(1, o)
        if o == 0:
            local[1].wait()
        z = lax.rem(mp + o, depth)
        copy = pltpu.make_async_copy(w_v.at[z], w_out.at[z], out_sem.at[1 + o])
        copy.start()
        local.append(copy)
        weight = w_v[z].reshape(wide * w_v.shape[2], 2 * half)
        cols = span(z, half)
        parts = [mm(norm_v[f : f + BLK, :], weight, NN) for f in range(0, slots, BLK)]
        for i, part in enumerate(parts):
            rows = slice(i * BLK, (i + 1) * BLK)
            kv_v[rows, cols] = part[:, :half].astype(BF)
            q_v[rows, cols] = jnp.where(low, part[:, half:] * LOG2E, 0.0).astype(BF)
        for at_sem, (src, dst) in enumerate(((kv_v, kv_out), (q_v, q_out))):
            copy = pltpu.make_async_copy(
                src.at[:, cols], dst.at[:, cols], out_sem.at[1 + depth + 2 * o + at_sem]
            )
            copy.start()
            local.append(copy)

    step(1, 3)
    forward(1, 2)
    finish(1, 1)
    project(0)
    forward(1, 3)
    finish(1, 2)
    for kind, peer in enumerate((east, south, sib)):
        copy = remote(
            ff_src, near_out.at[kind], fn_send.at[kind], fn_recv.at[kind], {"dp": peer}
        )
        copy.start()
        started.append(copy)
    project(1)
    finish(1, 3)
    project(2)
    project(3)
    for o in range(1, depth):
        block = line_out.at[o - 1]
        remote(block, block, fz_send.at[o - 1], fz_recv.at[o - 1], {"dp": sib}).wait_recv()
    for kind in range(3):
        block = near_out.at[kind]
        remote(block, block, fn_send.at[kind], fn_recv.at[kind], {"dp": sib}).wait_recv()
    for copy in local[2:]:
        copy.wait()
    for copy in started:
        copy.wait_send()


def open_call(small, wq, wk, wv, wo, wi, wu, seg, live, tok, dp, mp):
    slots, width = tok.shape
    rows = wi.shape[0]
    wide = HEADS * TILE
    pack = (rows, width)
    shape = jax.ShapeDtypeStruct
    dma = pltpu.SemaphoreType.DMA
    return pl.pallas_call(
        open_kernel,
        in_specs=[VMEM_SPEC] * 10,
        out_specs=[ANY_SPEC] * 7 + [VMEM_SPEC] * 6,
        out_shape=[
            shape((mp, dp) + pack, BF),
            shape((2,) + pack, BF),
            shape((mp - 1, 2) + pack, BF),
            shape((3, 2) + pack, BF),
            shape((slots, width), F32),
            shape((slots, wide), BF),
            shape((slots, wide), BF),
            shape((slots, TILE), BF),
            shape((slots, TILE), BF),
            shape((slots, TILE), BF),
            shape((16, width), F32),
            shape((16, 4 * BLK), F32),
            shape((16, 4 * BLK), F32),
        ],
        scratch_shapes=[
            pltpu.VMEM((16, width), BF),
            pltpu.VMEM((mp, dp, 16, width), BF),
            pltpu.VMEM(pack, BF),
            pltpu.VMEM((mp, dp) + pack, BF),
            pltpu.VMEM((2,) + pack, BF),
            pltpu.VMEM((slots, width), F32),
            pltpu.VMEM((slots, width), BF),
            pltpu.VMEM((slots, wide), BF),
            pltpu.VMEM((slots, wide), BF),
            dma((3,)),
            dma((2, mp - 1)),
            dma((2, mp - 1)),
            dma((2, mp, 8)),
            dma((2, mp, 8)),
            dma((mp - 1,)),
            dma((mp - 1,)),
            dma((3,)),
            dma((3,)),
            dma((1 + 3 * mp,)),
        ],
        compiler_params=pltpu.CompilerParams(
            collective_id=0, has_side_effects=True, vmem_limit_bytes=VMEM_LIMIT
        ),
        cost_estimate=pl.CostEstimate(
            flops=16 * 10**9, bytes_accessed=40 * 10**6, transcendentals=0
        ),
        name="open_layer",
    )(small, wq, wk, wv, wo, wi, wu, seg, live, tok)


def block_spans(seg_ref, live_ref, lo_ref, hi_ref):
    segments = seg_ref[...].astype(F32)
    lives = live_ref[...].astype(F32)
    for b in range(lo_ref.shape[0]):
        here = segments[:, b * BLK : (b + 1) * BLK]
        top = jnp.max(jnp.where(lives[:, b * BLK : (b + 1) * BLK] > 0, here, -1.0))
        before = jnp.sum((segments < jnp.min(here)).astype(F32))
        through = jnp.sum(((segments <= top) & (lives > 0)).astype(F32))
        hi = lax.div(through.astype(jnp.int32) + BLK - 1, BLK)
        hi_ref[b] = hi
        lo_ref[b] = jnp.minimum(lax.div(before.astype(jnp.int32), BLK), hi)


def attend_kernel(
    seg_ref, live_ref, line_ref, qa_ref, ka_ref, marks_ref, kv_hbm, q_hbm,
    ctx_out, lse_ref,
    kv_ref, q_ref, ctx_ref, tiles_ref, lsem_ref, mean_ref, lo_ref, hi_ref, sems,
):
    slots = qa_ref.shape[0]
    kv_copy = pltpu.make_async_copy(kv_hbm, kv_ref, sems.at[0])
    q_copy = pltpu.make_async_copy(q_hbm, q_ref, sems.at[1])
    kv_copy.start()
    q_copy.start()
    block_spans(seg_ref, live_ref, lo_ref, hi_ref)
    fill_bias(line_ref, tiles_ref)
    kv_copy.wait()
    q_copy.wait()
    mean_ref[...] = mm(jnp.full((8, slots), 1.0 / slots, BF), kv_ref[...], NN)
    high = jnp.logical_not(low_lanes())
    lane = lax.broadcasted_iota(jnp.int32, (1, TILE), 1)
    ones = jnp.ones((BLK, TILE), BF)

    def query_block(qb, carry):
        qs = span(qb)
        lo = lo_ref[qb]
        count = hi_ref[qb] - lo
        alive = marks_ref[qs, ALIVE : ALIVE + 1].astype(F32) > 0
        lsem_ref[...] = jnp.zeros_like(lsem_ref)

        def attend(width):
            def group_body(g, inner):
                heads = [g * GROUP + i for i in range(GROUP)]
                cols = [span(h, TILE) for h in heads]
                key_spans = [span(lo + j) for j in range(width)]
                kinds = [jnp.clip(lo + j - qb, -2, 2) + 2 for j in range(width)]
                query_mask = qa_ref[qs, :]
                key_masks = [ka_ref[ks, :] for ks in key_spans]
                scores = []
                for h, c in zip(heads, cols):
                    query = jnp.concatenate([q_ref[qs, c], query_mask], axis=1)
                    scores.append(
                        [
                            mm(query, jnp.concatenate([kv_ref[ks, c], km], axis=1), NT)
                            + tiles_ref[h, kind]
                            for ks, km, kind in zip(key_spans, key_masks, kinds)
                        ]
                    )
                tops = []
                weights = []
                for row in scores:
                    top = functools.reduce(jnp.maximum, row)
                    top = jnp.max(top, axis=1, keepdims=True)
                    tops.append(top)
                    weights.append(
                        jnp.concatenate([jnp.exp2(s - top).astype(BF) for s in row], axis=1)
                    )
                for h, c, top, weight in zip(heads, cols, tops, weights):
                    values = jnp.concatenate(
                        [
                            jnp.concatenate([kv_ref[ks, c] for ks in key_spans], axis=0),
                            jnp.concatenate([ones] * width, axis=0),
                        ],
                        axis=1,
                    )
                    both = mm(weight, values, NN)
                    total = both[:, TILE:]
                    context = jnp.where(alive, both[:, :TILE] / total, mean_ref[0:1, c])
                    ctx_ref[qs, c] = jnp.where(high, context, 0.0).astype(BF)
                    lsem_ref[...] = jnp.where(
                        (lane == h) & alive, top + jnp.log2(total), lsem_ref[...]
                    )
                return inner

            lax.fori_loop(0, HEADS // GROUP, group_body, 0)

        for width in range(1, slots // BLK + 1):
            pl.when(count == width)(functools.partial(attend, width))

        @pl.when(count == 0)
        def _():
            every = jnp.logical_not(low_lanes(HEADS * TILE))
            ctx_ref[qs, :] = jnp.broadcast_to(
                jnp.where(every, mean_ref[0:1, :], 0.0), (BLK, HEADS * TILE)
            ).astype(BF)

        lse_ref[:, qs] = lsem_ref[...].T[0:16]
        pltpu.make_async_copy(ctx_ref.at[qs], ctx_out.at[qs], sems.at[2 + qb]).start()
        return carry

    lax.fori_loop(0, slots // BLK, query_block, 0)
    for b in range(slots // BLK):
        rows = slice(b * BLK, (b + 1) * BLK)
        pltpu.make_async_copy(ctx_ref.at[rows], ctx_out.at[rows], sems.at[2 + b]).wait()


def attend_call(seg, live, line, qa, ka, marks, kv, q):
    slots, wide = kv.shape
    blocks = slots // BLK
    return pl.pallas_call(
        attend_kernel,
        in_specs=[VMEM_SPEC] * 6 + [ANY_SPEC] * 2,
        out_specs=[ANY_SPEC, VMEM_SPEC],
        out_shape=[
            jax.ShapeDtypeStruct((slots, wide), BF),
            jax.ShapeDtypeStruct((16, slots), F32),
        ],
        scratch_shapes=[
            pltpu.VMEM((slots, wide), BF),
            pltpu.VMEM((slots, wide), BF),
            pltpu.VMEM((slots, wide), BF),
            pltpu.VMEM((HEADS, 5, BLK, BLK), F32),
            pltpu.VMEM((BLK, TILE), F32),
            pltpu.VMEM((8, wide), F32),
            pltpu.SMEM((blocks,), jnp.int32),
            pltpu.SMEM((blocks,), jnp.int32),
            pltpu.SemaphoreType.DMA((2 + blocks,)),
        ],
        compiler_params=pltpu.CompilerParams(vmem_limit_bytes=VMEM_LIMIT),
        cost_estimate=pl.CostEstimate(
            flops=25 * 10**9, bytes_accessed=10**7, transcendentals=10**7
        ),
        name="attend",
    )(seg, live, line, qa, ka, marks, kv, q)


def gelu_both(inner, upstream):
    square = inner * inner
    bent = jnp.tanh(inner * (GELU_C + (GELU_C * 0.044715) * square))
    half = 0.5 + 0.5 * bent
    activated = inner * half
    slope = half + activated * ((1.0 - half) * (2 * GELU_C + (6 * GELU_C * 0.044715) * square))
    return activated.astype(BF), (upstream * slope).astype(BF)


def feed_kernel(
    og_ref, marks_ref, gains_ref, x_hbm, ctx_hbm, w_hbm, own_hbm, line_hbm, near_hbm, east_hbm,
    south_hbm, sib_hbm,
    out_ref, gh_ref,
    ff_v, ctx_ref, w_ref, norm_ref, gb_ref, hid_ref, br_ref, dn_ref,
    sems, fill, send, recv,
):
    dp = lax.axis_index("dp")
    depth, wide = ff_v.shape[0], ff_v.shape[1]
    half = w_hbm.shape[3] // 2
    rows_half = ff_v.shape[3] // 2
    sib, east, south, corner = neighbours()
    flip = 1 - 2 * lax.rem(dp, 2)
    barrier = pltpu.get_barrier_semaphore()
    for peer in (sib, east, south):
        pl.semaphore_signal(barrier, inc=1, device_id={"dp": peer}, device_id_type=MESH)
    first = [
        pltpu.make_async_copy(ctx_hbm, ctx_ref, sems.at[0]),
        pltpu.make_async_copy(x_hbm, hid_ref, sems.at[1]),
    ]
    for m in range(depth):
        first.append(
            pltpu.make_async_copy(w_hbm.at[m, :, :, half:], w_ref.at[m], sems.at[2 + m])
        )
    for copy in first:
        copy.start()
    pl.semaphore_wait(barrier, 3)

    def remote(src, dst, o, kind, peer):
        return pltpu.make_async_remote_copy(
            src_ref=src, dst_ref=dst, send_sem=send.at[o, kind], recv_sem=recv.at[o, kind],
            device_id={"dp": peer}, device_id_type=MESH,
        )

    fills = []
    for o in range(depth):
        from_east = near_hbm.at[0] if o == 0 else east_hbm.at[o - 1]
        from_south = near_hbm.at[1] if o == 0 else south_hbm.at[o - 1]
        from_sib = near_hbm.at[2] if o == 0 else sib_hbm.at[o - 1]
        mine = own_hbm if o == 0 else line_hbm.at[o - 1]
        upper, lower = pl.ds(0, rows_half), pl.ds(rows_half, rows_half)
        remote(from_east.at[:, upper], ff_v.at[o, east, :, upper], o, 0, south).start()
        remote(from_south.at[:, lower], ff_v.at[o, south, :, lower], o, 1, east).start()
        remote(from_east, ff_v.at[o, east], o, 2, sib).start()
        remote(from_south, ff_v.at[o, south], o, 3, sib).start()
        for kind, (src, place) in enumerate(
            ((mine, dp), (from_east, east), (from_south, south), (from_sib, sib))
        ):
            copy = pltpu.make_async_copy(src, ff_v.at[o, place], fill.at[o, kind])
            copy.start()
            fills.append(copy)

    def corners(o):
        block = ff_v.at[o, corner]
        upper = ff_v.at[o, corner, :, pl.ds(0, rows_half)]
        lower = ff_v.at[o, corner, :, pl.ds(rows_half, rows_half)]
        remote(upper, upper, o, 0, south).wait_recv()
        remote(lower, lower, o, 1, east).wait_recv()
        remote(block, block, o, 4, sib).start()

    def landed(o):
        for kind, place in ((2, east + flip), (3, south + flip), (4, corner + flip)):
            block = ff_v.at[o, place]
            remote(block, block, o, kind, sib).wait_recv()
        for kind, place in enumerate((dp, east, south, sib)):
            block = ff_v.at[o, place]
            pltpu.make_async_copy(block, block, fill.at[o, kind]).wait()

    slots = og_ref.shape[0]
    gain = gains_ref[9:10]
    blocks = [slice(f, f + BLK) for f in range(0, slots, BLK)]
    for rows in blocks:
        gb_ref[rows, :] = (
            og_ref[rows, :].astype(F32) * marks_ref[rows, ALIVE : ALIVE + 1].astype(F32)
        ).astype(BF)
    br_ref[...] = jnp.zeros_like(br_ref)
    dn_ref[...] = jnp.zeros_like(dn_ref)
    for copy in first:
        copy.wait()
    for m in range(depth):
        cols = slice(m * half, (m + 1) * half)
        weight = w_ref[m].reshape(-1, half)
        for rows in blocks:
            hid_ref[rows, :] += mm(ctx_ref[rows, cols], weight, NT)
        if m == 1:
            corners(0)
    for rows in blocks:
        hidden = hid_ref[rows, :]
        norm_ref[rows, :] = (hidden * rms_factor(hidden) * gain).astype(BF)

    def unit_block(o, carry):
        @pl.when(o < depth - 1)
        def _():
            corners(o + 1)

        landed(o)
        wi = ff_v[o, :, 0].reshape(-1, ff_v.shape[4])
        wo = ff_v[o, :, 1].reshape(-1, ff_v.shape[4])
        inner = [mm(norm_ref[rows, :], wi, NN) for rows in blocks]
        upstream = [mm(gb_ref[rows, :], wo, NN) for rows in blocks]
        pairs = [gelu_both(a, b) for a, b in zip(inner, upstream)]
        for rows, (activated, grad_inner) in zip(blocks, pairs):
            br_ref[rows, :] += mm(activated, wo, NT)
            dn_ref[rows, :] += mm(grad_inner, wi, NT)
        return carry

    lax.fori_loop(0, depth, unit_block, 0)
    for rows in blocks:
        hidden = hid_ref[rows, :]
        alive = marks_ref[rows, ALIVE : ALIVE + 1].astype(F32)
        out_ref[rows, :] = (alive * (hidden + br_ref[rows, :])).astype(BF)
        factor = rms_factor(hidden)
        weighted = dn_ref[rows, :] * gain
        gh_ref[rows, :] = og_ref[rows, :].astype(F32) * alive + (
            factor * weighted
            - hidden
            * (factor * factor * factor)
            * jnp.mean(weighted * hidden, axis=-1, keepdims=True)
        )
    for o in range(depth):
        upper, lower = pl.ds(0, rows_half), pl.ds(rows_half, rows_half)
        block = ff_v.at[o, east]
        remote(ff_v.at[o, east, :, upper], ff_v.at[o, east, :, upper], o, 0, south).wait_send()
        remote(ff_v.at[o, east, :, lower], ff_v.at[o, east, :, lower], o, 1, east).wait_send()
        for kind in (2, 3, 4):
            remote(block, block, o, kind, sib).wait_send()


def feed_call(og, marks, gains, x, ctx, w, own, line, near, from_east, from_south, from_sib):
    slots, width = x.shape
    depth, wide, rows, units = w.shape
    dma = pltpu.SemaphoreType.DMA
    return pl.pallas_call(
        feed_kernel,
        in_specs=[VMEM_SPEC] * 3 + [ANY_SPEC] * 9,
        out_specs=[VMEM_SPEC] * 2,
        out_shape=[
            jax.ShapeDtypeStruct((slots, width), BF),
            jax.ShapeDtypeStruct((slots, width), F32),
        ],
        scratch_shapes=[
            pltpu.VMEM((depth, wide) + own.shape, BF),
            pltpu.VMEM(ctx.shape, BF),
            pltpu.VMEM((depth, wide, rows, units // 2), BF),
            pltpu.VMEM((slots, width), BF),
            pltpu.VMEM((slots, width), BF),
            pltpu.VMEM((slots, width), F32),
            pltpu.VMEM((slots, width), F32),
            pltpu.VMEM((slots, width), F32),
            dma((2 + depth,)),
            dma((depth, 4)),
            dma((depth, 5)),
            dma((depth, 5)),
        ],
        compiler_params=pltpu.CompilerParams(
            collective_id=2, has_side_effects=True, vmem_limit_bytes=VMEM_LIMIT
        ),
        name="feed_forward",
    )(og, marks, gains, x, ctx, w, own, line, near, from_east, from_south, from_sib)


def feed_local_kernel(
    x_ref, og_ref, marks_ref, gain_ref, ctx_hbm, w_hbm, wi_hbm, wo_hbm,
    out_ref, gh_ref,
    ctx_ref, w_ref, wi_ref, wo_ref, norm_ref, gb_ref, hid_ref, br_ref, dn_ref, sems,
):
    slots = x_ref.shape[0]
    groups = w_hbm.shape[0]
    half = w_hbm.shape[2] // 2
    first = [pltpu.make_async_copy(ctx_hbm, ctx_ref, sems.at[0])]
    for m in range(groups):
        first.append(
            pltpu.make_async_copy(w_hbm.at[m, :, half:], w_ref.at[m], sems.at[1 + m])
        )
    later = []
    for m in range(groups):
        later.append(
            (
                pltpu.make_async_copy(wi_hbm.at[m], wi_ref.at[m], sems.at[1 + groups + 2 * m]),
                pltpu.make_async_copy(wo_hbm.at[m], wo_ref.at[m], sems.at[2 + groups + 2 * m]),
            )
        )
    for copy in first:
        copy.start()
    for pair in later:
        pair[0].start()
        pair[1].start()
    for copy in first:
        copy.wait()
    gain = gain_ref[9:10]
    blocks = [slice(f, f + BLK) for f in range(0, slots, BLK)]
    for rows in blocks:
        hid_ref[rows, :] = x_ref[rows, :]
    for m in range(groups):
        cols = slice(m * half, (m + 1) * half)
        for rows in blocks:
            hid_ref[rows, :] += mm(ctx_ref[rows, cols], w_ref[m], NT)
    for rows in blocks:
        hidden = hid_ref[rows, :]
        norm_ref[rows, :] = (hidden * rms_factor(hidden) * gain).astype(BF)
        gb_ref[rows, :] = (
            og_ref[rows, :].astype(F32) * marks_ref[rows, ALIVE : ALIVE + 1].astype(F32)
        ).astype(BF)
    br_ref[...] = jnp.zeros_like(br_ref)
    dn_ref[...] = jnp.zeros_like(dn_ref)
    for m in range(groups):
        later[m][0].wait()
        later[m][1].wait()
    def unit_block(m, carry):
        inner = [mm(norm_ref[rows, :], wi_ref[m], NN) for rows in blocks]
        upstream = [mm(gb_ref[rows, :], wo_ref[m], NN) for rows in blocks]
        pairs = [gelu_both(a, b) for a, b in zip(inner, upstream)]
        for rows, (activated, grad_inner) in zip(blocks, pairs):
            br_ref[rows, :] += mm(activated, wo_ref[m], NT)
            dn_ref[rows, :] += mm(grad_inner, wi_ref[m], NT)
        return carry

    lax.fori_loop(0, groups, unit_block, 0)
    for rows in blocks:
        hidden = hid_ref[rows, :]
        alive = marks_ref[rows, ALIVE : ALIVE + 1].astype(F32)
        out_ref[rows, :] = (alive * (hidden + br_ref[rows, :])).astype(BF)
        factor = rms_factor(hidden)
        weighted = dn_ref[rows, :] * gain
        gh_ref[rows, :] = og_ref[rows, :].astype(F32) * alive + (
            factor * weighted
            - hidden
            * (factor * factor * factor)
            * jnp.mean(weighted * hidden, axis=-1, keepdims=True)
        )


def feed_local(x, og, marks, gain, ctx, w, wi, wo):
    slots, width = x.shape
    groups = w.shape[0]
    return pl.pallas_call(
        feed_local_kernel,
        in_specs=[VMEM_SPEC] * 4 + [ANY_SPEC] * 4,
        out_specs=[VMEM_SPEC] * 2,
        out_shape=[
            jax.ShapeDtypeStruct((slots, width), BF),
            jax.ShapeDtypeStruct((slots, width), F32),
        ],
        scratch_shapes=[
            pltpu.VMEM(ctx.shape, BF),
            pltpu.VMEM((groups, w.shape[1], w.shape[2] // 2), BF),
            pltpu.VMEM(wi.shape, BF),
            pltpu.VMEM(wo.shape, BF),
            pltpu.VMEM((slots, width), BF),
            pltpu.VMEM((slots, width), BF),
            pltpu.VMEM((slots, width), F32),
            pltpu.VMEM((slots, width), F32),
            pltpu.VMEM((slots, width), F32),
            pltpu.SemaphoreType.DMA((1 + 3 * groups,)),
        ],
        compiler_params=pltpu.CompilerParams(vmem_limit_bytes=VMEM_LIMIT),
        name="feed_forward_local",
    )(x, og, marks, gain, ctx, w, wi, wo)


def backward_kernel(
    seg_ref, live_ref, gh_ref, lse_ref, line_ref, qa_ref, ka_ref, marks_ref, gains_ref, kv_hbm,
    w_hbm, q_hbm, ctx_hbm, x_hbm,
    ig_ref, pg_ref,
    kv_ref, w_ref, q_ref, ctx_ref, x_ref, lo_ref, hi_ref, tiles_ref, all_ref, kt_ref, dsum_ref, dqt_ref, acc_ref, sems,
):
    slots = gh_ref.shape[0]
    groups = w_hbm.shape[0]
    half = w_hbm.shape[2] // 2
    per = HEADS // groups
    weights = [pltpu.make_async_copy(w_hbm.at[m], w_ref.at[m], sems.at[m]) for m in range(groups)]
    ctx_copy = pltpu.make_async_copy(ctx_hbm, ctx_ref, sems.at[groups])
    x_copy = pltpu.make_async_copy(x_hbm, x_ref, sems.at[groups + 1])
    kv_copy = pltpu.make_async_copy(kv_hbm, kv_ref, sems.at[groups + 2])
    q_copy = pltpu.make_async_copy(q_hbm, q_ref, sems.at[groups + 3])
    for copy in weights + [q_copy, ctx_copy, kv_copy, x_copy]:
        copy.start()
    block_spans(seg_ref, live_ref, lo_ref, hi_ref)
    fill_bias(line_ref, tiles_ref)
    blocks = [slice(f, f + BLK) for f in range(0, slots, BLK)]
    low_half = low_lanes(half)
    q_copy.wait()
    for m in range(groups):
        weights[m].wait()
        cols = slice(m * half, (m + 1) * half)
        parts = [mm(gh_ref[rows, :].astype(BF), w_ref[m, :, half:], NN) for rows in blocks]
        for rows, part in zip(blocks, parts):
            q_ref[rows, cols] = jnp.where(low_half, q_ref[rows, cols], part.astype(BF))
    ctx_copy.wait()
    wide = HEADS * TILE
    pick = (
        lax.broadcasted_iota(jnp.int32, (16, wide), 1) // TILE
        == lax.broadcasted_iota(jnp.int32, (16, wide), 0)
    ).astype(F32).astype(BF)
    for rows in blocks:
        product = q_ref[rows, :].astype(F32) * ctx_ref[rows, :].astype(F32)
        upper = product.astype(BF)
        lower = (product - upper.astype(F32)).astype(BF)
        dsum_ref[:, rows] = mm(pick, upper, NT) + mm(pick, lower, NT)
    kv_copy.wait()
    for h in range(HEADS):
        kt_ref[h] = kv_ref[:, h * TILE : (h + 1) * TILE].T[0:HEAD_DIM]
    low = low_lanes()
    zero = jnp.zeros((BLK, TILE), BF)

    def group_body(g, carry):
        heads = [g * GROUP + i for i in range(GROUP)]
        cols = [span(h, TILE) for h in heads]
        dqt_ref[...] = jnp.zeros_like(dqt_ref)

        def key_block(kb, inner):
            ks = span(kb)
            acc_ref[...] = jnp.zeros_like(acc_ref)

            def query_block(qb, deep):
                qs = span(qb)
                kind = jnp.clip(qb - kb, -2, 2) + 2
                query_mask = qa_ref[qs, :]
                key_mask = ka_ref[ks, :]
                both = [q_ref[qs, c] for c in cols]
                keys = [kv_ref[ks, c] for c in cols]
                scores = [
                    mm(
                        jnp.concatenate([key, key_mask], axis=1),
                        jnp.concatenate([jnp.where(low, pair, zero), query_mask], axis=1),
                        NT,
                    )
                    + tiles_ref[h, kind]
                    for h, key, pair in zip(heads, keys, both)
                ]
                grads = [
                    mm(key, jnp.where(low, zero, pair), NT) for key, pair in zip(keys, both)
                ]
                probs = [
                    jnp.exp2(s - lse_ref[pl.ds(h, 1), qs]) for h, s in zip(heads, scores)
                ]
                outs = [
                    (p * (d - dsum_ref[pl.ds(h, 1), qs])).astype(BF)
                    for h, p, d in zip(heads, probs, grads)
                ]
                lows = [p.astype(BF) for p in probs]
                for i, h in enumerate(heads):
                    acc_ref[i] += jnp.where(
                        low, mm(outs[i], both[i], NN), mm(lows[i], both[i], NN)
                    )
                    dqt_ref[i, 0:HEAD_DIM, qs] += mm(kt_ref[h, :, ks], outs[i], NN)
                return deep

            lax.fori_loop(lo_ref[kb], hi_ref[kb], query_block, 0)
            for i, h in enumerate(heads):
                place = lax.div(h, per) * (2 * half) + lax.rem(h, per) * TILE
                all_ref[ks, pl.ds(pl.multiple_of(place, TILE), TILE)] = (
                    acc_ref[i] * jnp.where(low, LN2, 1.0)
                ).astype(BF)
            return inner

        lax.fori_loop(0, slots // BLK, key_block, 0)
        for i, h in enumerate(heads):
            place = lax.div(h, per) * (2 * half) + half + lax.rem(h, per) * TILE
            all_ref[:, pl.ds(pl.multiple_of(place, TILE), TILE)] = dqt_ref[i].astype(BF).T
        return carry

    lax.fori_loop(0, HEADS // GROUP, group_body, 0)
    x_copy.wait()
    gain = gains_ref[8:9]
    pg_ref[...] = jnp.zeros_like(pg_ref)
    for rows in blocks:
        back = functools.reduce(
            jnp.add,
            [
                mm(all_ref[rows, m * 2 * half : (m + 1) * 2 * half], w_ref[m], NT)
                for m in range(groups)
            ],
        )
        value = x_ref[rows, :]
        factor = rms_factor(value)
        weighted = back * gain
        grad = gh_ref[rows, :] + (
            factor * weighted
            - value
            * (factor * factor * factor)
            * jnp.mean(weighted * value, axis=-1, keepdims=True)
        )
        ig_ref[rows, :] = jnp.where(
            marks_ref[rows, IS_PROMPT : IS_PROMPT + 1].astype(F32) > 0, 0.0, grad
        )
        upper = grad.astype(BF)
        lower = (grad - upper.astype(F32)).astype(BF)
        hot = marks_ref[rows, :]
        pg_ref[...] += mm(hot, upper, TN) + mm(hot, lower, TN)


def backward_call(seg, live, gh, lse, line, qa, ka, marks, gains, kv, w, q, ctx, x):
    slots, width = gh.shape
    groups = w.shape[0]
    return pl.pallas_call(
        backward_kernel,
        in_specs=[VMEM_SPEC] * 9 + [ANY_SPEC] * 5,
        out_specs=[VMEM_SPEC] * 2,
        out_shape=[
            jax.ShapeDtypeStruct((slots, width), F32),
            jax.ShapeDtypeStruct((TILE, width), F32),
        ],
        scratch_shapes=[
            pltpu.VMEM(kv.shape, BF),
            pltpu.VMEM(w.shape, BF),
            pltpu.VMEM(q.shape, BF),
            pltpu.VMEM(ctx.shape, BF),
            pltpu.VMEM(x.shape, F32),
            pltpu.SMEM((slots // BLK,), jnp.int32),
            pltpu.SMEM((slots // BLK,), jnp.int32),
            pltpu.VMEM((HEADS, 5, BLK, BLK), F32),
            pltpu.VMEM((slots, 2 * HEADS * TILE), BF),
            pltpu.VMEM((HEADS, HEAD_DIM, slots), BF),
            pltpu.VMEM((16, slots), F32),
            pltpu.VMEM((GROUP, TILE, slots), F32),
            pltpu.VMEM((GROUP, BLK, TILE), F32),
            pltpu.SemaphoreType.DMA((groups + 4,)),
        ],
        compiler_params=pltpu.CompilerParams(vmem_limit_bytes=VMEM_LIMIT),
        name="attend_back",
    )(seg, live, gh, lse, line, qa, ka, marks, gains, kv, w, q, ctx, x)


def slot_arrays(segments, live):
    slots = segments.shape[0]
    place = jnp.arange(slots, dtype=jnp.int32)
    first = jnp.sum((segments[None, :] < segments[:, None]).astype(jnp.int32), axis=1)
    position = place - first
    is_prompt = (live == 1) & (position < PROMPT)
    lane = jnp.arange(TILE, dtype=jnp.int32)[None, :]
    hot = ((position[:, None] == lane) & is_prompt[:, None]).astype(BF)
    same = segments[:, None] == lane
    query_side = same.astype(BF)
    reach = same & (live[:, None] == 1)
    key_side = jnp.where((lane < 16) & jnp.logical_not(reach), MASKED, 0.0).astype(BF)
    marks = jnp.where(lane == ALIVE, (live[:, None] == 1).astype(BF), hot)
    marks = jnp.where(lane == IS_PROMPT, is_prompt[:, None].astype(BF), marks)
    return marks, query_side, key_side


def bias_lines(table):
    offset = jnp.arange(4 * BLK, dtype=jnp.int32) - 2 * BLK
    code = jnp.arange(BUCKETS, dtype=jnp.int32)[:, None]
    lines = []
    for sign in (1, -1):
        hot = (bucket_of(sign * offset, BUCKETS // 2)[None, :] == code).astype(F32)
        line = jnp.einsum("bh,bx->hx", table.astype(F32), hot, precision=lax.Precision.HIGHEST)
        lines.append(jnp.pad(line * LOG2E, ((0, 16 - HEADS), (0, 0))))
    return lines


def tiles_of(first, second):
    rows = first.shape[0]
    shaped = [part.reshape(rows, -1, 1, HEAD_DIM) for part in (first, second)]
    return jnp.concatenate(shaped, axis=2).reshape(rows, -1)


def open_plain(
    tok, prompt, seg, live, w_query, w_key, w_value, w_output, w_inner, w_outer, gain_attn,
    gain_ffn, rel_table,
):
    slots, width = tok.shape
    packs = jnp.stack(
        [
            jnp.concatenate([tiles_of(w_key, w_value), tiles_of(w_query, w_output.T)], axis=1),
            w_inner,
            w_outer.T,
        ]
    )
    weights = lax.all_gather(lax.all_gather(packs, "dp", axis=1, tiled=True), "mp", axis=1)
    prompt_all = lax.all_gather(prompt.astype(BF), ("dp", "mp"), tiled=True)
    prompt_all = jnp.pad(prompt_all.reshape(PROMPT, width), ((0, TILE - PROMPT), (0, 0)))
    gains = lax.all_gather(jnp.stack([gain_attn, gain_ffn]), "dp", axis=1, tiled=True)
    gains = jnp.pad(gains.astype(F32), ((8, 6), (0, 0)))
    ahead, behind = bias_lines(lax.all_gather(rel_table, "mp", axis=1, tiled=True))
    marks, query_side, key_side = slot_arrays(seg, live)
    is_prompt = marks[:, IS_PROMPT:] > 0
    placed = jnp.dot(marks, prompt_all, preferred_element_type=F32)
    x = jnp.where(is_prompt, placed, tok.astype(F32))
    normed = (x * rms_factor(x) * gains[8:9]).astype(BF)
    out = jnp.einsum("sd,mdc->smc", normed, weights[0], preferred_element_type=F32)
    half = out.shape[2] // 2
    kv = out[:, :, :half].astype(BF).reshape(slots, -1)
    q = jnp.where(low_lanes(half), out[:, :, half:] * LOG2E, 0.0).astype(BF).reshape(slots, -1)
    return weights, x, kv, q, marks, query_side, key_side, gains, ahead, behind


def adam_kernel(
    part_ref, state_ref, out_ref, land_one, land_two, mid_ref, send_one, recv_one, send_two,
    recv_two,
):
    dp = lax.axis_index("dp")
    mp = lax.axis_index("mp")
    wide = part_ref.shape[0]
    deep = part_ref.shape[1]
    barrier = pltpu.get_barrier_semaphore()
    peers = [{"dp": lax.rem(dp + s, wide)} for s in range(1, wide)]
    peers += [{"mp": lax.rem(mp + s, deep)} for s in range(1, deep)]
    for peer in peers:
        pl.semaphore_signal(barrier, inc=1, device_id=peer, device_id_type=MESH)
    pl.semaphore_wait(barrier, len(peers))
    first = []
    for s in range(1, wide):
        to = lax.rem(dp + s, wide)
        copy = pltpu.make_async_remote_copy(
            src_ref=part_ref.at[to], dst_ref=land_one.at[s - 1],
            send_sem=send_one.at[s - 1], recv_sem=recv_one.at[s - 1],
            device_id={"dp": to}, device_id_type=MESH,
        )
        copy.start()
        first.append(copy)
    total = part_ref[dp]
    for s, copy in enumerate(first):
        copy.wait_recv()
        total = total + land_one[s]
    mid_ref[...] = total
    second = []
    for s in range(1, deep):
        to = lax.rem(mp + s, deep)
        copy = pltpu.make_async_remote_copy(
            src_ref=mid_ref.at[to], dst_ref=land_two.at[s - 1],
            send_sem=send_two.at[s - 1], recv_sem=recv_two.at[s - 1],
            device_id={"mp": to}, device_id_type=MESH,
        )
        copy.start()
        second.append(copy)
    grad = mid_ref[mp]
    for s, copy in enumerate(second):
        copy.wait_recv()
        grad = grad + land_two[s]
    out_ref[...] = jnp.stack(adam_step(grad, state_ref[0], state_ref[1], state_ref[2]))
    for copy in first + second:
        copy.wait_send()


def adam_step(grad, prompt, moment_one, moment_two):
    first_new = 0.9 * moment_one + 0.1 * grad
    second_new = 0.999 * moment_two + 0.001 * grad * grad
    correct_one = 1.0 - 0.9**ADAM_STEP
    correct_two = 1.0 - 0.999**ADAM_STEP
    prompt_new = prompt - 0.3 * (first_new / correct_one) / (
        jnp.sqrt(second_new / correct_two) + 1e-08
    )
    return prompt_new, first_new, second_new


def adam_call(part, state):
    wide, deep, rows, cols = part.shape
    return pl.pallas_call(
        adam_kernel,
        in_specs=[VMEM_SPEC] * 2,
        out_specs=VMEM_SPEC,
        out_shape=jax.ShapeDtypeStruct(state.shape, F32),
        scratch_shapes=[
            pltpu.VMEM((wide - 1, deep, rows, cols), F32),
            pltpu.VMEM((deep - 1, rows, cols), F32),
            pltpu.VMEM((deep, rows, cols), F32),
            pltpu.SemaphoreType.DMA((wide - 1,)),
            pltpu.SemaphoreType.DMA((wide - 1,)),
            pltpu.SemaphoreType.DMA((deep - 1,)),
            pltpu.SemaphoreType.DMA((deep - 1,)),
        ],
        compiler_params=pltpu.CompilerParams(collective_id=1, has_side_effects=True),
        name="sum_and_step",
    )(part, state)


def body(
    dp, mp, tokens, prompt, moment_one, moment_two, segments, live, out_grad, w_query, w_key,
    w_value, w_output, w_inner, w_outer, gain_attn, gain_ffn, rel_table,
):
    _, slots, width = tokens.shape
    tuned = (dp, mp) == (8, 4)
    share = prompt.shape[0]
    if tuned:
        pad = lambda part: jnp.pad(part, ((0, 0), (0, width - part.shape[1])))
        small = jnp.concatenate(
            [
                jnp.pad(prompt, (0, 8 * width - share)).reshape(8, width),
                pad(jnp.stack([gain_attn, gain_ffn]).astype(F32)),
                pad(rel_table.T.astype(F32)),
                jnp.zeros((6 - rel_table.shape[1], width), F32),
            ]
        )
        (
            w, own, line, near, x, kv, q, marks, query_side, key_side, gains, ahead, behind,
        ) = open_call(
            small, w_query, w_key, w_value, w_output, w_inner, w_outer, segments, live,
            tokens[0], dp, mp,
        )
        swap = lambda bit: lax.ppermute(line, "dp", [(i, i ^ bit) for i in range(dp)])
        from_east, from_south, from_sib = swap(2), swap(4), swap(1)
    else:
        weights, x, kv, q, marks, query_side, key_side, gains, ahead, behind = open_plain(
            tokens[0], prompt, segments[0], live[0], w_query, w_key, w_value, w_output, w_inner,
            w_outer, gain_attn, gain_ffn, rel_table,
        )
    ctx, lse = attend_call(segments, live, ahead, query_side, key_side, marks, kv, q)
    if tuned:
        layer_output, grad_hidden = feed_call(
            out_grad[0], marks, gains, x, ctx, w, own, line, near, from_east, from_south,
            from_sib,
        )
        w = w.reshape(mp, width, -1)
    else:
        w = weights[0]
        layer_output, grad_hidden = feed_local(
            x, out_grad[0], marks, gains, ctx, w, weights[1], weights[2]
        )
    input_grad, prompt_part = backward_call(
        segments, live, grad_hidden, lse, behind, query_side, key_side, marks, gains, kv, w, q,
        ctx, x,
    )
    flat_part = prompt_part[:PROMPT].reshape(dp, mp, share)
    if tuned:
        fill = -share % (8 * TILE)
        flat_part = jnp.pad(flat_part, ((0, 0), (0, 0), (0, fill)))
        state = jnp.pad(jnp.stack([prompt, moment_one, moment_two]), ((0, 0), (0, fill)))
        stepped = adam_call(
            flat_part.reshape(dp, mp, -1, TILE), state.reshape(3, -1, TILE)
        )
        stepped = stepped.reshape(3, -1)[:, :share]
        prompt_new, first_new, second_new = stepped[0], stepped[1], stepped[2]
    else:
        grad = lax.psum_scatter(
            flat_part.reshape(-1), ("dp", "mp"), scatter_dimension=0, tiled=True
        )
        prompt_new, first_new, second_new = adam_step(grad, prompt, moment_one, moment_two)
    return (layer_output[None], input_grad[None], prompt_new, first_new, second_new)


def solution(mesh):
    both = ("dp", "mp")
    return jax.shard_map(
        functools.partial(body, mesh.shape["dp"], mesh.shape["mp"]),
        mesh=mesh,
        in_specs=(
            P(both, None, None),
            P(both),
            P(both),
            P(both),
            P(both, None),
            P(both, None),
            P(both, None, None),
            P("dp", "mp"),
            P("dp", "mp"),
            P("dp", "mp"),
            P("mp", "dp"),
            P("dp", "mp"),
            P("mp", "dp"),
            P("dp"),
            P("dp"),
            P(None, "mp"),
        ),
        out_specs=(
            P(both, None, None),
            P(both, None, None),
            P(both),
            P(both),
            P(both),
        ),
        check_vma=False,
    )
```

```python
import functools

import jax
import jax.numpy as jnp
from jax import lax
from jax.experimental import pallas as pl
from jax.experimental.pallas import tpu as pltpu
from jax.sharding import PartitionSpec as P

HEADS = 12
HEAD_DIM = 64
BUCKETS = 32
PROMPT = 100
ADAM_STEP = 10
BOUNDS = (1, 2, 3, 4, 5, 6, 7, 8, 12, 16, 23, 32, 46, 64, 91)
EPSILON = 1e-06
MASKED = -1e30
LOG2E = 1.4426950408889634
LN2 = 0.6931471805599453
GELU_C = 0.7978845608028654

BLK = 256
TILE = 128
GROUP = 12
ALIVE = 126
IS_PROMPT = 127
BF = jnp.bfloat16
F32 = jnp.float32
NN = (((1,), (0,)), ((), ()))
NT = (((1,), (1,)), ((), ()))
TN = (((0,), (0,)), ((), ()))
MESH = pl.DeviceIdType.MESH
VMEM_LIMIT = 62 * 1024 * 1024
SMEM_SPEC = pl.BlockSpec(memory_space=pltpu.SMEM)
VMEM_SPEC = pl.BlockSpec(memory_space=pltpu.VMEM)
ANY_SPEC = pl.BlockSpec(memory_space=pl.ANY)


def mm(left, right, dims):
    return lax.dot_general(left, right, dims, preferred_element_type=F32)


def bucket_of(offset, half):
    distance = jnp.abs(offset)
    counted = sum(((distance >= limit).astype(jnp.int32) for limit in BOUNDS))
    return counted + jnp.where(offset > 0, half, 0).astype(jnp.int32)


def span(block, size=BLK):
    return pl.ds(pl.multiple_of(block * size, size), size)


def low_lanes(width=TILE):
    return lax.rem(lax.broadcasted_iota(jnp.int32, (1, width), 1), TILE) < HEAD_DIM


def fill_bias(line_ref, tiles_ref):
    def one(head, carry):
        row = line_ref[pl.ds(head, 1), :]
        wide = pltpu.roll(
            jnp.broadcast_to(row, (TILE, 4 * TILE)), 0, 1, stride=1, stride_axis=0
        )
        for near in range(1, 4):
            tiles_ref[head, near] = wide[:, near * TILE : (near + 1) * TILE]
        tiles_ref[head, 0] = jnp.broadcast_to(row[:, 0:1], (TILE, TILE))
        tiles_ref[head, 4] = jnp.broadcast_to(row[:, 4 * TILE - 1 :], (TILE, TILE))
        return carry

    lax.fori_loop(0, HEADS, one, 0)


def rms_factor(values):
    return lax.rsqrt(jnp.mean(values * values, axis=-1, keepdims=True) + EPSILON)


def neighbours():
    dp = lax.axis_index("dp")
    core = lax.rem(dp, 2)
    across = lax.rem(lax.div(dp, 2), 2)
    down = lax.div(dp, 4)
    return (
        dp + 1 - 2 * core,
        dp + 2 - 4 * across,
        dp + 4 - 8 * down,
        dp + 6 - 4 * across - 8 * down,
    )


def line_order(z, j):
    upper = lax.div(z, 2)
    return (z, z + 1 - 2 * lax.rem(z, 2), 2 - upper, 3 - 3 * upper)[j]


def line_rank(z, source):
    same = lax.div(z, 2) == lax.div(source, 2)
    return jnp.where(same, jnp.abs(z - source), jnp.where(z < 2, source, 3 - source))


def flat_shift(rows, shift, width):
    lane = lax.broadcasted_iota(jnp.int32, (8, width), 1)
    turned = pltpu.roll(rows, shift, 1)
    return jnp.where(lane >= shift, turned, pltpu.roll(turned, 1, 0))


def interleave(first, second):
    parts = []
    for at in range(0, first.shape[1], HEAD_DIM):
        parts += [first[:, at : at + HEAD_DIM], second[:, at : at + HEAD_DIM]]
    return jnp.concatenate(parts, axis=1)


def open_kernel(
    state_ref, ga_ref, gf_ref, table_ref, wq_ref, wk_ref, wv_ref, wo_ref, wi_ref, wu_ref,
    seg_ref, live_ref, tok_ref,
    w_out, own_out, line_out, near_out, x_out, kv_out, q_out, ahead_out, behind_out,
    marks_ref, qa_ref, ka_ref, gains_ref, lo_ref, hi_ref,
    small_src, small_v, pack_src, w_v, ff_src, x_v, norm_v, kv_v, q_v, lines_v, ahead_v,
    behind_v,
    own_sem, z_send, z_recv, send, recv, fz_send, fz_recv, fn_send, fn_recv, out_sem,
):
    mp = lax.axis_index("mp")
    dp = lax.axis_index("dp")
    depth, wide = w_v.shape[0], w_v.shape[1]
    width = tok_ref.shape[1]
    sib, east, south, corner = neighbours()
    up, down = mp + 1 < depth, mp > 0
    barrier = pltpu.get_barrier_semaphore()

    def greet(peer):
        pl.semaphore_signal(barrier, inc=1, device_id=peer, device_id_type=MESH)

    for peer in (sib, east, south):
        greet({"dp": peer})
    pl.when(up)(lambda: greet({"mp": mp + 1}))
    pl.when(down)(lambda: greet({"mp": mp - 1}))

    share = lax.rem(dp * depth + mp, 8)
    part = ga_ref.shape[1]
    empty = jnp.zeros((1, width - part), F32)
    gain_rows = [
        pltpu.roll(jnp.concatenate([ref[...].astype(F32), empty], axis=1), part * dp, 1)
        for ref in (ga_ref, gf_ref)
    ]
    table_rows = jnp.concatenate(
        [table_ref[...].astype(F32), jnp.zeros((HEADS // depth, width - BUCKETS), F32)], axis=1
    )
    small_src[...] = jnp.concatenate(
        [flat_shift(state_ref[0], part * share, width)]
        + gain_rows
        + [table_rows, jnp.zeros((6 - HEADS // depth, width), F32)],
        axis=0,
    ).astype(BF)
    pack_src[...] = jnp.concatenate(
        [interleave(wk_ref[...], wv_ref[...]), interleave(wq_ref[...], wo_ref[...].T)], axis=1
    )
    ff_src[0] = wi_ref[...]
    ff_src[1] = wu_ref[...]
    pl.semaphore_wait(barrier, 3 + up.astype(jnp.int32) + down.astype(jnp.int32))

    def remote(src, dst, send_sem, recv_sem, peer):
        return pltpu.make_async_remote_copy(
            src_ref=src, dst_ref=dst, send_sem=send_sem, recv_sem=recv_sem,
            device_id=peer, device_id_type=MESH,
        )

    started = []
    local = []
    units = [(small_src, small_v), (pack_src, w_v)]

    def along(u, j, src):
        dst = units[u][1]
        z = line_order(mp, j)
        copies = []
        for at, (ahead, there, move) in enumerate(((up, z <= mp, 1), (down, z >= mp, -1))):
            copy = remote(
                src, dst.at[z, dp], z_send.at[u, j, at], z_recv.at[u, z], {"mp": mp + move}
            )
            copies.append((jnp.logical_and(ahead, there), copy))
        return copies

    def along_ff(j, src):
        z = line_order(mp, j)
        copies = []
        for at, (ahead, there, move) in enumerate(((up, z <= mp, 1), (down, z >= mp, -1))):
            slot = jnp.maximum(line_rank(mp + move, z) - 1, 0)
            slot = jnp.minimum(slot, depth - 2)
            copy = remote(
                src, line_out.at[slot], fz_send.at[j, at], fz_recv.at[slot], {"mp": mp + move}
            )
            copies.append((jnp.logical_and(ahead, there), copy))
        return copies

    lined = []

    def launch(copies):
        for condition, copy in copies:
            pl.when(condition)(copy.start)
        lined.extend(copies)

    def push(u, o, kind, src, dst, peer):
        copy = remote(src, dst, send.at[u, o, kind], recv.at[u, o, kind], peer)
        copy.start()
        started.append(copy)

    def landed(u, o, kind, dst):
        remote(dst, dst, send.at[u, o, kind], recv.at[u, o, kind], {"dp": sib}).wait_recv()

    def step(u, o):
        src, dst = units[u]
        z = line_order(mp, o)
        block = dst.at[z, dp]
        if o:
            remote(block, block, z_send.at[u, o, 0], z_recv.at[u, z], {"dp": sib}).wait_recv()
            src = block
        launch(along(u, o, src))
        push(u, o, 0, src, block, {"dp": east})
        push(u, o, 1, src, block, {"dp": south})
        push(u, o, 2, src, block, {"dp": sib})

    def step_ff(o):
        block = line_out.at[o - 1]
        remote(block, block, fz_send.at[o, 0], fz_recv.at[o - 1], {"dp": sib}).wait_recv()
        launch(along_ff(o, block))

    def forward(u, o):
        dst = units[u][1]
        z = line_order(mp, o)
        rows = dst.shape[2] // 2 if u else dst.shape[2]
        landed(u, o, 0, dst.at[z, east])
        push(u, o, 3, dst.at[z, east, 0:rows], dst.at[z, east, 0:rows], {"dp": south})
        push(u, o, 4, dst.at[z, east], dst.at[z, east], {"dp": sib})
        landed(u, o, 1, dst.at[z, south])
        if u:
            push(u, o, 5, dst.at[z, south, rows:], dst.at[z, south, rows:], {"dp": east})
        push(u, o, 6, dst.at[z, south], dst.at[z, south], {"dp": sib})

    def finish(u, o):
        dst = units[u][1]
        z = line_order(mp, o)
        rows = dst.shape[2] // 2 if u else dst.shape[2]
        landed(u, o, 3, dst.at[z, corner, 0:rows])
        if u:
            landed(u, o, 5, dst.at[z, corner, rows:])
        push(u, o, 7, dst.at[z, corner], dst.at[z, corner], {"dp": sib})

    flip = 1 - 2 * lax.rem(dp, 2)

    def complete(u, o):
        dst = units[u][1]
        z = line_order(mp, o)
        landed(u, o, 2, dst.at[z, sib])
        landed(u, o, 4, dst.at[z, east + flip])
        landed(u, o, 6, dst.at[z, south + flip])
        landed(u, o, 7, dst.at[z, corner + flip])

    for u in range(2):
        step(u, 0)
        src, dst = units[u]
        copy = pltpu.make_async_copy(src, dst.at[mp, dp], own_sem.at[u])
        copy.start()
        local.append(copy)
    copy = pltpu.make_async_copy(ff_src, own_out, own_sem.at[2])
    copy.start()
    local.append(copy)

    slots = tok_ref.shape[0]
    segment_row = seg_ref[...].astype(F32)
    live_row = live_ref[...].astype(F32)
    lane = lax.broadcasted_iota(jnp.int32, (slots, TILE), 1)
    lane_f = lane.astype(F32)
    segment = jnp.broadcast_to(segment_row, (TILE, slots)).T
    alive = jnp.broadcast_to(live_row, (TILE, slots)).T
    same = segment == lane_f
    start = jnp.sum((segment < lane_f).astype(F32), axis=0, keepdims=True)
    first = jnp.sum(jnp.where(same, start, 0.0), axis=1, keepdims=True)
    position = lax.broadcasted_iota(jnp.int32, (slots, 1), 0).astype(F32) - first
    prompt_slot = (alive > 0) & (position < PROMPT)
    sides = jnp.where(lane == ALIVE, alive, same.astype(F32))
    qa_ref[...] = jnp.where(lane == IS_PROMPT, prompt_slot.astype(F32), sides).astype(BF)
    ka_ref[...] = jnp.where(
        (lane < 16) & jnp.logical_not(same & (alive > 0)), MASKED, 0.0
    ).astype(BF)
    for u in range(1):
        for o in range(1, depth):
            step(u, o)
    step(1, 1)

    def window_rows(device, inside):
        target = 25 * lax.div(device, 8) + 3 * lax.rem(device, 8) + inside
        return jnp.where(inside < 4, target, -1).astype(F32)

    at = lax.broadcasted_iota(jnp.int32, (1, TILE), 1)
    target = window_rows(lax.div(at, 4), lax.rem(at, 4))
    marks_ref[...] = jnp.where((position == target) & prompt_slot, 1.0, 0.0).astype(BF)
    for o in range(depth):
        forward(0, o)
    forward(1, 0)
    block_lane = lax.broadcasted_iota(jnp.int32, (8, TILE), 1)
    lows = jnp.zeros((8, TILE), F32)
    highs = jnp.zeros((8, TILE), F32)
    for block in range(slots // TILE):
        here = segment_row[:, block * TILE : (block + 1) * TILE]
        lives = live_row[:, block * TILE : (block + 1) * TILE] > 0
        top = jnp.max(jnp.where(lives, here, -1.0), axis=1, keepdims=True)
        bottom = jnp.min(here, axis=1, keepdims=True)
        before = jnp.sum((segment_row < bottom).astype(F32), axis=1, keepdims=True)
        through = (segment_row <= top) & (live_row > 0)
        through = jnp.sum(through.astype(F32), axis=1, keepdims=True)
        lows = jnp.where(block_lane == block, before, lows)
        highs = jnp.where(block_lane == block, through, highs)
    highs = lax.div(highs.astype(jnp.int32) + TILE - 1, TILE)
    hi_ref[...] = highs
    lo_ref[...] = jnp.minimum(lax.div(lows.astype(jnp.int32), TILE), highs)
    for o in range(depth):
        finish(0, o)
    step(1, 2)
    forward(1, 1)
    for o in range(depth):
        complete(0, o)
    local[0].wait()
    finish(1, 0)

    gains = functools.reduce(jnp.add, [small_v[0, d].astype(F32) for d in range(wide)])
    gains_ref[...] = gains
    rows_all = depth * wide * 16
    at = lax.broadcasted_iota(jnp.int32, (1, rows_all), 1)
    holder = lax.div(at, 16)
    target = window_rows(
        lax.rem(holder, wide) * depth + lax.div(holder, wide), lax.rem(at, 16)
    )
    windows = small_v[...].reshape(rows_all, width)
    gain = gains[8:9]

    def embed(f):
        rows = slice(f, f + BLK)
        hot = (position[rows] == target).astype(F32).astype(BF)
        placed = mm(hot, windows, NN)
        value = jnp.where(prompt_slot[rows, 0:1], placed, tok_ref[rows, :].astype(F32))
        x_v[rows, :] = value
        norm_v[rows, :] = (value * rms_factor(value) * gain).astype(BF)

    for f in range(0, slots, BLK):
        embed(f)
        if f == slots // 2 - BLK:
            step(1, 3)
            forward(1, 2)
            finish(1, 1)
    copy = pltpu.make_async_copy(x_v, x_out, out_sem.at[0])
    copy.start()
    local.append(copy)
    launch(along_ff(0, ff_src))

    half = w_v.shape[3] // 2
    low = low_lanes(half)

    def project(o):
        complete(1, o)
        if o == 0:
            local[1].wait()
        z = line_order(mp, o)
        copy = pltpu.make_async_copy(w_v.at[z], w_out.at[z], out_sem.at[1 + o])
        copy.start()
        local.append(copy)
        weight = w_v[z].reshape(wide * w_v.shape[2], 2 * half)
        cols = span(z, half)
        parts = [mm(norm_v[f : f + BLK, :], weight, NN) for f in range(0, slots, BLK)]
        for i, piece in enumerate(parts):
            rows = slice(i * BLK, (i + 1) * BLK)
            kv_v[rows, cols] = piece[:, :half].astype(BF)
            q_v[rows, cols] = jnp.where(low, piece[:, half:] * LOG2E, 0.0).astype(BF)
        for at_sem, (src, dst) in enumerate(((kv_v, kv_out), (q_v, q_out))):
            copy = pltpu.make_async_copy(
                src.at[:, cols], dst.at[:, cols], out_sem.at[1 + depth + 2 * o + at_sem]
            )
            copy.start()
            local.append(copy)

    forward(1, 3)
    finish(1, 2)
    step_ff(1)
    for kind, peer in enumerate((east, south, sib)):
        copy = remote(
            ff_src, near_out.at[kind], fn_send.at[kind], fn_recv.at[kind], {"dp": peer}
        )
        copy.start()
        started.append(copy)
    table = jnp.concatenate(
        [small_v[m, 0].astype(F32)[10 : 10 + HEADS // depth, 0:TILE] for m in range(depth)]
        + [jnp.zeros((16 - HEADS, TILE), F32)],
        axis=0,
    ).astype(BF)
    offset = lax.broadcasted_iota(jnp.int32, (1, 4 * TILE), 1) - 2 * TILE
    code = lax.broadcasted_iota(jnp.int32, (TILE, 4 * TILE), 0)
    for at_sem, (sign, tiles, out) in enumerate(
        ((1, ahead_v, ahead_out), (-1, behind_v, behind_out))
    ):
        hot = (code == bucket_of(sign * offset, BUCKETS // 2)).astype(F32).astype(BF)
        lines_v[...] = mm(table, hot, NN) * LOG2E
        fill_bias(lines_v, tiles)
        copy = pltpu.make_async_copy(tiles, out, out_sem.at[1 + 3 * depth + at_sem])
        copy.start()
        local.append(copy)
        if at_sem == 0:
            project(0)
            finish(1, 3)
            step_ff(2)
    project(1)
    step_ff(3)
    project(2)
    project(3)
    for kind in range(3):
        block = near_out.at[kind]
        remote(block, block, fn_send.at[kind], fn_recv.at[kind], {"dp": sib}).wait_recv()
    for copy in local[2:]:
        copy.wait()
    for copy in started:
        copy.wait_send()
    for condition, copy in lined:
        pl.when(condition)(copy.wait_send)


def open_call(state, ga, gf, table, wq, wk, wv, wo, wi, wu, seg, live, tok, dp, mp):
    slots, width = tok.shape
    rows = wi.shape[0]
    wide = HEADS * TILE
    pack = (rows, width)
    shape = jax.ShapeDtypeStruct
    dma = pltpu.SemaphoreType.DMA
    tiles = (HEADS, 5, TILE, TILE)
    return pl.pallas_call(
        open_kernel,
        in_specs=[VMEM_SPEC] * 13,
        out_specs=[ANY_SPEC] * 9 + [VMEM_SPEC] * 6,
        out_shape=[
            shape((mp, dp) + pack, BF),
            shape((2,) + pack, BF),
            shape((mp - 1, 2) + pack, BF),
            shape((3, 2) + pack, BF),
            shape((slots, width), F32),
            shape((slots, wide), BF),
            shape((slots, wide), BF),
            shape(tiles, F32),
            shape(tiles, F32),
            shape((slots, TILE), BF),
            shape((slots, TILE), BF),
            shape((slots, TILE), BF),
            shape((16, width), F32),
            shape((8, TILE), jnp.int32),
            shape((8, TILE), jnp.int32),
        ],
        scratch_shapes=[
            pltpu.VMEM((16, width), BF),
            pltpu.VMEM((mp, dp, 16, width), BF),
            pltpu.VMEM(pack, BF),
            pltpu.VMEM((mp, dp) + pack, BF),
            pltpu.VMEM((2,) + pack, BF),
            pltpu.VMEM((slots, width), F32),
            pltpu.VMEM((slots, width), BF),
            pltpu.VMEM((slots, wide), BF),
            pltpu.VMEM((slots, wide), BF),
            pltpu.VMEM((16, 4 * TILE), F32),
            pltpu.VMEM(tiles, F32),
            pltpu.VMEM(tiles, F32),
            dma((3,)),
            dma((2, mp, 2)),
            dma((2, mp)),
            dma((2, mp, 8)),
            dma((2, mp, 8)),
            dma((mp, 2)),
            dma((mp - 1,)),
            dma((3,)),
            dma((3,)),
            dma((3 + 3 * mp,)),
        ],
        compiler_params=pltpu.CompilerParams(
            collective_id=0, has_side_effects=True, vmem_limit_bytes=VMEM_LIMIT
        ),
        cost_estimate=pl.CostEstimate(
            flops=16 * 10**9, bytes_accessed=40 * 10**6, transcendentals=0
        ),
        name="open_layer",
    )(state, ga, gf, table, wq, wk, wv, wo, wi, wu, seg, live, tok)


def window_of(lo_ref, hi_ref, block, blocks):
    lo = lo_ref[0, block]
    pairs = lax.div(hi_ref[0, block] - lo + 1, 2)
    return jnp.minimum(lo, blocks - 2 * pairs), pairs


def bias_row(tiles_ref, head, first, block, pairs):
    return jnp.concatenate(
        [
            tiles_ref[head, jnp.clip(first + j - block, -2, 2) + 2]
            for j in range(2 * pairs)
        ],
        axis=1,
    )


def attend_kernel(
    lo_ref, hi_ref, qa_ref, ka_ref, kv_hbm, q_hbm, tiles_hbm,
    ctx_out, lse_ref,
    kv_ref, val_ref, q_ref, ctx_ref, tiles_ref, lsem_ref, mean_ref, sems, ctx_sems,
):
    slots = qa_ref.shape[0]
    blocks = slots // TILE
    copies = [
        pltpu.make_async_copy(src, dst, sems.at[i])
        for i, (src, dst) in enumerate(
            ((kv_hbm, kv_ref), (q_hbm, q_ref), (tiles_hbm, tiles_ref))
        )
    ]
    for copy in copies:
        copy.start()
    copies[0].wait()
    mean_ref[...] = mm(jnp.full((8, slots), 1.0 / slots, BF), kv_ref[...], NN)
    high = jnp.logical_not(low_lanes())
    ones = jnp.ones((slots, TILE), BF)
    for h in range(HEADS):
        cols = slice(h * TILE, (h + 1) * TILE)
        val_ref[:, cols] = jnp.where(high, kv_ref[:, cols], ones)
    lane = lax.broadcasted_iota(jnp.int32, (1, TILE), 1)
    copies[1].wait()
    copies[2].wait()

    def query_block(qb, carry):
        qs = span(qb, TILE)
        first, count = window_of(lo_ref, hi_ref, qb, blocks)
        alive = qa_ref[qs, ALIVE : ALIVE + 1].astype(F32) > 0
        lsem_ref[...] = jnp.zeros_like(lsem_ref)

        def attend(pairs):
            size = 2 * pairs * TILE
            ks = pl.ds(pl.multiple_of(first * TILE, TILE), size)
            mask = mm(qa_ref[qs, :], ka_ref[ks, :], NT)

            def group_body(g, inner):
                heads = [g * GROUP + i for i in range(GROUP)]
                cols = [span(h, TILE) for h in heads]
                scores = [
                    mm(q_ref[qs, c], kv_ref[ks, c], NT)
                    + (bias_row(tiles_ref, h, first, qb, pairs) + mask)
                    for h, c in zip(heads, cols)
                ]
                tops = [jnp.max(row, axis=1, keepdims=True) for row in scores]
                weights = [jnp.exp2(row - top).astype(BF) for row, top in zip(scores, tops)]
                for h, c, top, weight in zip(heads, cols, tops, weights):
                    both = mm(weight, val_ref[ks, c], NN)
                    context = both / pltpu.roll(both, HEAD_DIM, 1)
                    context = jnp.where(alive, context, mean_ref[0:1, c])
                    ctx_ref[qs, c] = jnp.where(high, context, 0.0).astype(BF)
                    lsem_ref[...] = jnp.where(
                        (lane == h) & alive, top + jnp.log2(both), lsem_ref[...]
                    )
                return inner

            lax.fori_loop(0, HEADS // GROUP, group_body, 0)

        for pairs in range(1, blocks // 2 + 1):
            pl.when(count == pairs)(functools.partial(attend, pairs))

        @pl.when(count == 0)
        def _():
            every = jnp.logical_not(low_lanes(HEADS * TILE))
            ctx_ref[qs, :] = jnp.broadcast_to(
                jnp.where(every, mean_ref[0:1, :], 0.0), (TILE, HEADS * TILE)
            ).astype(BF)

        lse_ref[:, qs] = lsem_ref[...].T[0:16]
        pltpu.make_async_copy(ctx_ref.at[qs], ctx_out.at[qs], ctx_sems.at[qb]).start()
        return carry

    lax.fori_loop(0, blocks, query_block, 0)
    for b in range(blocks):
        rows = slice(b * TILE, (b + 1) * TILE)
        pltpu.make_async_copy(ctx_ref.at[rows], ctx_out.at[rows], ctx_sems.at[b]).wait()


def attend_call(lo, hi, qa, ka, kv, q, tiles):
    slots, wide = kv.shape
    return pl.pallas_call(
        attend_kernel,
        in_specs=[SMEM_SPEC] * 2 + [VMEM_SPEC] * 2 + [ANY_SPEC] * 3,
        out_specs=[ANY_SPEC, VMEM_SPEC],
        out_shape=[
            jax.ShapeDtypeStruct((slots, wide), BF),
            jax.ShapeDtypeStruct((16, slots), F32),
        ],
        scratch_shapes=[
            pltpu.VMEM((slots, wide), BF),
            pltpu.VMEM((slots, wide), BF),
            pltpu.VMEM((slots, wide), BF),
            pltpu.VMEM((slots, wide), BF),
            pltpu.VMEM(tiles.shape, F32),
            pltpu.VMEM((TILE, TILE), F32),
            pltpu.VMEM((8, wide), F32),
            pltpu.SemaphoreType.DMA((3,)),
            pltpu.SemaphoreType.DMA((slots // TILE,)),
        ],
        compiler_params=pltpu.CompilerParams(vmem_limit_bytes=VMEM_LIMIT),
        cost_estimate=pl.CostEstimate(
            flops=25 * 10**9, bytes_accessed=10**7, transcendentals=10**7
        ),
        name="attend",
    )(lo, hi, qa, ka, kv, q, tiles)


def gelu_both(inner, upstream):
    square = inner * inner
    bent = jnp.tanh(inner * (GELU_C + (GELU_C * 0.044715) * square))
    half = 0.5 + 0.5 * bent
    activated = inner * half
    slope = half + activated * ((1.0 - half) * (2 * GELU_C + (6 * GELU_C * 0.044715) * square))
    return activated.astype(BF), (upstream * slope).astype(BF)


def feed_kernel(
    og_ref, qa_ref, gains_ref, x_hbm, ctx_hbm, w_hbm, own_hbm, line_hbm, near_hbm, east_hbm,
    south_hbm, sib_hbm,
    out_ref, gh_ref,
    ff_v, ctx_ref, w_ref, norm_ref, gb_ref, hid_ref, br_ref, dn_ref,
    sems, fill, send, recv,
):
    dp = lax.axis_index("dp")
    depth, wide = ff_v.shape[0], ff_v.shape[1]
    half = w_hbm.shape[3] // 2
    rows_half = ff_v.shape[3] // 2
    sib, east, south, corner = neighbours()
    flip = 1 - 2 * lax.rem(dp, 2)
    barrier = pltpu.get_barrier_semaphore()
    for peer in (sib, east, south):
        pl.semaphore_signal(barrier, inc=1, device_id={"dp": peer}, device_id_type=MESH)
    first = [
        pltpu.make_async_copy(ctx_hbm, ctx_ref, sems.at[0]),
        pltpu.make_async_copy(x_hbm, hid_ref, sems.at[1]),
    ]
    for m in range(depth):
        first.append(
            pltpu.make_async_copy(w_hbm.at[m, :, :, half:], w_ref.at[m], sems.at[2 + m])
        )
    for copy in first:
        copy.start()
    pl.semaphore_wait(barrier, 3)

    def remote(src, dst, o, kind, peer):
        return pltpu.make_async_remote_copy(
            src_ref=src, dst_ref=dst, send_sem=send.at[o, kind], recv_sem=recv.at[o, kind],
            device_id={"dp": peer}, device_id_type=MESH,
        )

    fills = []
    for o in range(depth):
        from_east = near_hbm.at[0] if o == 0 else east_hbm.at[o - 1]
        from_south = near_hbm.at[1] if o == 0 else south_hbm.at[o - 1]
        from_sib = near_hbm.at[2] if o == 0 else sib_hbm.at[o - 1]
        mine = own_hbm if o == 0 else line_hbm.at[o - 1]
        upper, lower = pl.ds(0, rows_half), pl.ds(rows_half, rows_half)
        remote(from_east.at[:, upper], ff_v.at[o, east, :, upper], o, 0, south).start()
        remote(from_south.at[:, lower], ff_v.at[o, south, :, lower], o, 1, east).start()
        remote(from_east, ff_v.at[o, east], o, 2, sib).start()
        remote(from_south, ff_v.at[o, south], o, 3, sib).start()
        for kind, (src, place) in enumerate(
            ((mine, dp), (from_east, east), (from_south, south), (from_sib, sib))
        ):
            copy = pltpu.make_async_copy(src, ff_v.at[o, place], fill.at[o, kind])
            copy.start()
            fills.append(copy)

    def corners(o):
        block = ff_v.at[o, corner]
        upper = ff_v.at[o, corner, :, pl.ds(0, rows_half)]
        lower = ff_v.at[o, corner, :, pl.ds(rows_half, rows_half)]
        remote(upper, upper, o, 0, south).wait_recv()
        remote(lower, lower, o, 1, east).wait_recv()
        remote(block, block, o, 4, sib).start()

    def landed(o):
        for kind, place in ((2, east + flip), (3, south + flip), (4, corner + flip)):
            block = ff_v.at[o, place]
            remote(block, block, o, kind, sib).wait_recv()
        for kind, place in enumerate((dp, east, south, sib)):
            block = ff_v.at[o, place]
            pltpu.make_async_copy(block, block, fill.at[o, kind]).wait()

    slots = og_ref.shape[0]
    gain = gains_ref[9:10]
    blocks = [slice(f, f + BLK) for f in range(0, slots, BLK)]
    for rows in blocks:
        gb_ref[rows, :] = (
            og_ref[rows, :].astype(F32) * qa_ref[rows, ALIVE : ALIVE + 1].astype(F32)
        ).astype(BF)
    br_ref[...] = jnp.zeros_like(br_ref)
    dn_ref[...] = jnp.zeros_like(dn_ref)
    for copy in first:
        copy.wait()
    for m in range(depth):
        cols = slice(m * half, (m + 1) * half)
        weight = w_ref[m].reshape(-1, half)
        for rows in blocks:
            hid_ref[rows, :] += mm(ctx_ref[rows, cols], weight, NT)
        if m == 1:
            corners(0)
    for rows in blocks:
        hidden = hid_ref[rows, :]
        norm_ref[rows, :] = (hidden * rms_factor(hidden) * gain).astype(BF)

    def unit_block(o, carry):
        @pl.when(o < depth - 1)
        def _():
            corners(o + 1)

        landed(o)
        wi = ff_v[o, :, 0].reshape(-1, ff_v.shape[4])
        wo = ff_v[o, :, 1].reshape(-1, ff_v.shape[4])
        inner = [mm(norm_ref[rows, :], wi, NN) for rows in blocks]
        upstream = [mm(gb_ref[rows, :], wo, NN) for rows in blocks]
        pairs = [gelu_both(a, b) for a, b in zip(inner, upstream)]
        for rows, (activated, grad_inner) in zip(blocks, pairs):
            br_ref[rows, :] += mm(activated, wo, NT)
            dn_ref[rows, :] += mm(grad_inner, wi, NT)
        return carry

    lax.fori_loop(0, depth, unit_block, 0)
    for rows in blocks:
        hidden = hid_ref[rows, :]
        alive = qa_ref[rows, ALIVE : ALIVE + 1].astype(F32)
        out_ref[rows, :] = (alive * (hidden + br_ref[rows, :])).astype(BF)
        factor = rms_factor(hidden)
        weighted = dn_ref[rows, :] * gain
        gh_ref[rows, :] = og_ref[rows, :].astype(F32) * alive + (
            factor * weighted
            - hidden
            * (factor * factor * factor)
            * jnp.mean(weighted * hidden, axis=-1, keepdims=True)
        )
    for o in range(depth):
        upper, lower = pl.ds(0, rows_half), pl.ds(rows_half, rows_half)
        block = ff_v.at[o, east]
        remote(ff_v.at[o, east, :, upper], ff_v.at[o, east, :, upper], o, 0, south).wait_send()
        remote(ff_v.at[o, east, :, lower], ff_v.at[o, east, :, lower], o, 1, east).wait_send()
        for kind in (2, 3, 4):
            remote(block, block, o, kind, sib).wait_send()


def feed_call(og, qa, gains, x, ctx, w, own, line, near, from_east, from_south, from_sib):
    slots, width = x.shape
    depth, wide, rows, units = w.shape
    dma = pltpu.SemaphoreType.DMA
    return pl.pallas_call(
        feed_kernel,
        in_specs=[VMEM_SPEC] * 3 + [ANY_SPEC] * 9,
        out_specs=[VMEM_SPEC] * 2,
        out_shape=[
            jax.ShapeDtypeStruct((slots, width), BF),
            jax.ShapeDtypeStruct((slots, width), F32),
        ],
        scratch_shapes=[
            pltpu.VMEM((depth, wide) + own.shape, BF),
            pltpu.VMEM(ctx.shape, BF),
            pltpu.VMEM((depth, wide, rows, units // 2), BF),
            pltpu.VMEM((slots, width), BF),
            pltpu.VMEM((slots, width), BF),
            pltpu.VMEM((slots, width), F32),
            pltpu.VMEM((slots, width), F32),
            pltpu.VMEM((slots, width), F32),
            dma((2 + depth,)),
            dma((depth, 4)),
            dma((depth, 5)),
            dma((depth, 5)),
        ],
        compiler_params=pltpu.CompilerParams(
            collective_id=2, has_side_effects=True, vmem_limit_bytes=VMEM_LIMIT
        ),
        name="feed_forward",
    )(og, qa, gains, x, ctx, w, own, line, near, from_east, from_south, from_sib)


def feed_local_kernel(
    x_ref, og_ref, qa_ref, gain_ref, ctx_hbm, w_hbm, wi_hbm, wo_hbm,
    out_ref, gh_ref,
    ctx_ref, w_ref, wi_ref, wo_ref, norm_ref, gb_ref, hid_ref, br_ref, dn_ref, sems,
):
    slots = x_ref.shape[0]
    groups = w_hbm.shape[0]
    half = w_hbm.shape[2] // 2
    first = [pltpu.make_async_copy(ctx_hbm, ctx_ref, sems.at[0])]
    for m in range(groups):
        first.append(
            pltpu.make_async_copy(w_hbm.at[m, :, half:], w_ref.at[m], sems.at[1 + m])
        )
    later = []
    for m in range(groups):
        later.append(
            (
                pltpu.make_async_copy(wi_hbm.at[m], wi_ref.at[m], sems.at[1 + groups + 2 * m]),
                pltpu.make_async_copy(wo_hbm.at[m], wo_ref.at[m], sems.at[2 + groups + 2 * m]),
            )
        )
    for copy in first:
        copy.start()
    for pair in later:
        pair[0].start()
        pair[1].start()
    for copy in first:
        copy.wait()
    gain = gain_ref[9:10]
    blocks = [slice(f, f + BLK) for f in range(0, slots, BLK)]
    for rows in blocks:
        hid_ref[rows, :] = x_ref[rows, :]
    for m in range(groups):
        cols = slice(m * half, (m + 1) * half)
        for rows in blocks:
            hid_ref[rows, :] += mm(ctx_ref[rows, cols], w_ref[m], NT)
    for rows in blocks:
        hidden = hid_ref[rows, :]
        norm_ref[rows, :] = (hidden * rms_factor(hidden) * gain).astype(BF)
        gb_ref[rows, :] = (
            og_ref[rows, :].astype(F32) * qa_ref[rows, ALIVE : ALIVE + 1].astype(F32)
        ).astype(BF)
    br_ref[...] = jnp.zeros_like(br_ref)
    dn_ref[...] = jnp.zeros_like(dn_ref)
    for m in range(groups):
        later[m][0].wait()
        later[m][1].wait()
    def unit_block(m, carry):
        inner = [mm(norm_ref[rows, :], wi_ref[m], NN) for rows in blocks]
        upstream = [mm(gb_ref[rows, :], wo_ref[m], NN) for rows in blocks]
        pairs = [gelu_both(a, b) for a, b in zip(inner, upstream)]
        for rows, (activated, grad_inner) in zip(blocks, pairs):
            br_ref[rows, :] += mm(activated, wo_ref[m], NT)
            dn_ref[rows, :] += mm(grad_inner, wi_ref[m], NT)
        return carry

    lax.fori_loop(0, groups, unit_block, 0)
    for rows in blocks:
        hidden = hid_ref[rows, :]
        alive = qa_ref[rows, ALIVE : ALIVE + 1].astype(F32)
        out_ref[rows, :] = (alive * (hidden + br_ref[rows, :])).astype(BF)
        factor = rms_factor(hidden)
        weighted = dn_ref[rows, :] * gain
        gh_ref[rows, :] = og_ref[rows, :].astype(F32) * alive + (
            factor * weighted
            - hidden
            * (factor * factor * factor)
            * jnp.mean(weighted * hidden, axis=-1, keepdims=True)
        )


def feed_local(x, og, qa, gain, ctx, w, wi, wo):
    slots, width = x.shape
    groups = w.shape[0]
    return pl.pallas_call(
        feed_local_kernel,
        in_specs=[VMEM_SPEC] * 4 + [ANY_SPEC] * 4,
        out_specs=[VMEM_SPEC] * 2,
        out_shape=[
            jax.ShapeDtypeStruct((slots, width), BF),
            jax.ShapeDtypeStruct((slots, width), F32),
        ],
        scratch_shapes=[
            pltpu.VMEM(ctx.shape, BF),
            pltpu.VMEM((groups, w.shape[1], w.shape[2] // 2), BF),
            pltpu.VMEM(wi.shape, BF),
            pltpu.VMEM(wo.shape, BF),
            pltpu.VMEM((slots, width), BF),
            pltpu.VMEM((slots, width), BF),
            pltpu.VMEM((slots, width), F32),
            pltpu.VMEM((slots, width), F32),
            pltpu.VMEM((slots, width), F32),
            pltpu.SemaphoreType.DMA((1 + 3 * groups,)),
        ],
        compiler_params=pltpu.CompilerParams(vmem_limit_bytes=VMEM_LIMIT),
        name="feed_forward_local",
    )(x, og, qa, gain, ctx, w, wi, wo)


def backward_kernel(
    lo_ref, hi_ref, gh_ref, lse_ref, qa_ref, ka_ref, marks_ref, gains_ref, kv_hbm, w_hbm, q_hbm,
    ctx_hbm, x_hbm, tiles_hbm, layer_hbm,
    ig_ref, pg_ref, layer_out,
    kv_ref, w_ref, q_ref, ctx_ref, x_ref, tiles_ref, layer_ref, all_ref, kt_ref, dsum_ref,
    dqt_ref, sems,
):
    slots = gh_ref.shape[0]
    count_blocks = slots // TILE
    groups = w_hbm.shape[0]
    half = w_hbm.shape[2] // 2
    per = HEADS // groups
    weights = [pltpu.make_async_copy(w_hbm.at[m], w_ref.at[m], sems.at[m]) for m in range(groups)]
    q_copy, ctx_copy, kv_copy, tiles_copy, x_copy, layer_copy = [
        pltpu.make_async_copy(src, dst, sems.at[groups + i])
        for i, (src, dst) in enumerate(
            (
                (q_hbm, q_ref),
                (ctx_hbm, ctx_ref),
                (kv_hbm, kv_ref),
                (tiles_hbm, tiles_ref),
                (x_hbm, x_ref),
                (layer_hbm, layer_ref),
            )
        )
    ]
    for copy in [q_copy] + weights + [ctx_copy, kv_copy, tiles_copy, x_copy, layer_copy]:
        copy.start()
    dqt_ref[...] = jnp.zeros_like(dqt_ref)
    blocks = [slice(f, f + BLK) for f in range(0, slots, BLK)]
    low_half = low_lanes(half)
    q_copy.wait()
    grads_low = [gh_ref[rows, :].astype(BF) for rows in blocks]
    for m in range(groups):
        weights[m].wait()
        cols = slice(m * half, (m + 1) * half)
        parts = [mm(grad, w_ref[m, :, half:], NN) for grad in grads_low]
        for rows, part in zip(blocks, parts):
            q_ref[rows, cols] = jnp.where(low_half, q_ref[rows, cols], part.astype(BF))
    ctx_copy.wait()
    wide = HEADS * TILE
    pick = (
        lax.broadcasted_iota(jnp.int32, (wide, TILE), 0) // TILE
        == lax.broadcasted_iota(jnp.int32, (wide, TILE), 1)
    ).astype(F32).astype(BF)
    sums = []
    for rows in blocks:
        product = q_ref[rows, :].astype(F32) * ctx_ref[rows, :].astype(F32)
        upper = product.astype(BF)
        lower = (product - upper.astype(F32)).astype(BF)
        sums.append(mm(upper, pick, NN) + mm(lower, pick, NN))
    for rows, value in zip(blocks, sums):
        dsum_ref[:, rows] = value.T[0:16]
    kv_copy.wait()
    for h in range(HEADS):
        kt_ref[h] = kv_ref[:, h * TILE : (h + 1) * TILE].T[0:HEAD_DIM]
    tiles_copy.wait()
    low = low_lanes()

    def place_of(h, second):
        place = lax.div(h, per) * (2 * half) + second * half + lax.rem(h, per) * TILE
        return pl.ds(pl.multiple_of(place, TILE), TILE)

    def key_block(kb, carry):
        ks = span(kb, TILE)
        first, count = window_of(lo_ref, hi_ref, kb, count_blocks)

        def attend(pairs):
            size = 2 * pairs * TILE
            qs = pl.ds(pl.multiple_of(first * TILE, TILE), size)
            mask = mm(ka_ref[ks, :], qa_ref[qs, :], NT)

            def group_body(g, inner):
                heads = [g * GROUP + i for i in range(GROUP)]
                cols = [span(h, TILE) for h in heads]
                zero = jnp.zeros((TILE, TILE), BF)
                keys = [kv_ref[ks, c] for c in cols]
                raw = [
                    mm(
                        jnp.concatenate(
                            [jnp.where(low, key, zero), jnp.where(low, zero, key)], axis=0
                        ),
                        q_ref[qs, c],
                        NT,
                    )
                    for key, c in zip(keys, cols)
                ]
                probs = [
                    jnp.exp2(
                        both[:TILE]
                        + (bias_row(tiles_ref, h, first, kb, pairs) + mask)
                        - lse_ref[pl.ds(h, 1), qs]
                    )
                    for h, both in zip(heads, raw)
                ]
                outs = [
                    (p * (both[TILE:] - dsum_ref[pl.ds(h, 1), qs])).astype(BF)
                    for h, p, both in zip(heads, probs, raw)
                ]
                sides = [
                    jnp.concatenate([out, p.astype(BF)], axis=0) for out, p in zip(outs, probs)
                ]
                for h, c, out, side in zip(heads, cols, outs, sides):
                    both = mm(side, q_ref[qs, c], NN)
                    all_ref[ks, place_of(h, 0)] = jnp.where(
                        low, both[:TILE] * LN2, both[TILE:]
                    ).astype(BF)
                    dqt_ref[h, :, qs] += mm(kt_ref[h, :, ks], out, NN)
                return inner

            lax.fori_loop(0, HEADS // GROUP, group_body, 0)

        for pairs in range(1, count_blocks // 2 + 1):
            pl.when(count == pairs)(functools.partial(attend, pairs))

        @pl.when(count == 0)
        def _():
            all_ref[ks, :] = jnp.zeros((TILE, all_ref.shape[1]), BF)

        return carry

    lax.fori_loop(0, count_blocks, key_block, 0)
    rest = jnp.zeros((TILE - HEAD_DIM, slots), BF)
    for h in range(HEADS):
        place = (h // per) * (2 * half) + half + (h % per) * TILE
        all_ref[:, place : place + TILE] = jnp.concatenate(
            [dqt_ref[h].astype(BF), rest], axis=0
        ).T
    x_copy.wait()
    layer_copy.wait()
    layer_copy = pltpu.make_async_copy(layer_ref, layer_out, sems.at[groups + 5])
    layer_copy.start()
    gain = gains_ref[8:9]
    backs = [
        functools.reduce(
            jnp.add,
            [
                mm(all_ref[rows, m * 2 * half : (m + 1) * 2 * half], w_ref[m], NT)
                for m in range(groups)
            ],
        )
        for rows in blocks
    ]
    total = None
    for rows, back in zip(blocks, backs):
        value = x_ref[rows, :]
        factor = rms_factor(value)
        weighted = back * gain
        grad = gh_ref[rows, :] + (
            factor * weighted
            - value
            * (factor * factor * factor)
            * jnp.mean(weighted * value, axis=-1, keepdims=True)
        )
        ig_ref[rows, :] = jnp.where(
            qa_ref[rows, IS_PROMPT : IS_PROMPT + 1].astype(F32) > 0, 0.0, grad
        )
        upper = grad.astype(BF)
        lower = (grad - upper.astype(F32)).astype(BF)
        hot = marks_ref[rows, :]
        part = mm(hot, upper, TN) + mm(hot, lower, TN)
        total = part if total is None else total + part
    pg_ref[...] = total
    layer_copy.wait()


def backward_call(
    lo, hi, gh, lse, qa, ka, marks, gains, kv, w, q, ctx, x, tiles, layer_output
):
    slots, width = gh.shape
    groups = w.shape[0]
    return pl.pallas_call(
        backward_kernel,
        in_specs=[SMEM_SPEC] * 2 + [VMEM_SPEC] * 6 + [ANY_SPEC] * 7,
        out_specs=[VMEM_SPEC] * 2 + [ANY_SPEC],
        out_shape=[
            jax.ShapeDtypeStruct((slots, width), F32),
            jax.ShapeDtypeStruct((TILE, width), F32),
            jax.ShapeDtypeStruct((slots, width), BF),
        ],
        scratch_shapes=[
            pltpu.VMEM(kv.shape, BF),
            pltpu.VMEM(w.shape, BF),
            pltpu.VMEM(q.shape, BF),
            pltpu.VMEM(ctx.shape, BF),
            pltpu.VMEM(x.shape, F32),
            pltpu.VMEM(tiles.shape, F32),
            pltpu.VMEM(layer_output.shape, BF),
            pltpu.VMEM((slots, 2 * HEADS * TILE), BF),
            pltpu.VMEM((HEADS, HEAD_DIM, slots), BF),
            pltpu.VMEM((16, slots), F32),
            pltpu.VMEM((HEADS, HEAD_DIM, slots), F32),
            pltpu.SemaphoreType.DMA((groups + 6,)),
        ],
        compiler_params=pltpu.CompilerParams(vmem_limit_bytes=VMEM_LIMIT),
        name="attend_back",
    )(lo, hi, gh, lse, qa, ka, marks, gains, kv, w, q, ctx, x, tiles, layer_output)


def slot_arrays(segments, live):
    slots = segments.shape[0]
    place = jnp.arange(slots, dtype=jnp.int32)
    first = jnp.sum((segments[None, :] < segments[:, None]).astype(jnp.int32), axis=1)
    position = place - first
    alive = live[:, None] == 1
    is_prompt = alive & (position < PROMPT)[:, None]
    lane = jnp.arange(TILE, dtype=jnp.int32)[None, :]
    marks = ((position[:, None] == lane) & is_prompt).astype(BF)
    same = segments[:, None] == lane
    query_side = jnp.where(lane == ALIVE, alive, same)
    query_side = jnp.where(lane == IS_PROMPT, is_prompt, query_side).astype(BF)
    key_side = jnp.where((lane < 16) & jnp.logical_not(same & alive), MASKED, 0.0).astype(BF)
    by_block = segments.reshape(-1, TILE)
    top = jnp.max(jnp.where(live.reshape(-1, TILE) == 1, by_block, -1), axis=1)
    hi = jnp.sum((segments[None, :] <= top[:, None]) & (live[None, :] == 1), axis=1)
    hi = (hi.astype(jnp.int32) + TILE - 1) // TILE
    lo = jnp.sum((segments[None, :] < by_block[:, :1]).astype(jnp.int32), axis=1) // TILE
    return marks, query_side, key_side, jnp.minimum(lo, hi)[None], hi[None]


def bias_tiles(table):
    place = jnp.arange(TILE, dtype=jnp.int32)
    kinds = jnp.arange(-2, 3, dtype=jnp.int32)[:, None, None] * TILE
    offset = jnp.clip(kinds + place[None, None, :] - place[None, :, None], -TILE, TILE)
    both = []
    for sign in (1, -1):
        both.append(
            table.astype(F32)[bucket_of(sign * offset, BUCKETS // 2)].transpose(3, 0, 1, 2) * LOG2E
        )
    return both


def tiles_of(first, second):
    rows = first.shape[0]
    shaped = [part.reshape(rows, -1, 1, HEAD_DIM) for part in (first, second)]
    return jnp.concatenate(shaped, axis=2).reshape(rows, -1)


def open_plain(
    tok, prompt, seg, live, w_query, w_key, w_value, w_output, w_inner, w_outer, gain_attn,
    gain_ffn, rel_table,
):
    slots, width = tok.shape
    packs = jnp.stack(
        [
            jnp.concatenate([tiles_of(w_key, w_value), tiles_of(w_query, w_output.T)], axis=1),
            w_inner,
            w_outer.T,
        ]
    )
    weights = lax.all_gather(lax.all_gather(packs, "dp", axis=1, tiled=True), "mp", axis=1)
    prompt_all = lax.all_gather(prompt.astype(BF), ("dp", "mp"), tiled=True)
    prompt_all = jnp.pad(prompt_all.reshape(PROMPT, width), ((0, TILE - PROMPT), (0, 0)))
    gains = lax.all_gather(jnp.stack([gain_attn, gain_ffn]), "dp", axis=1, tiled=True)
    gains = jnp.pad(gains.astype(F32), ((8, 6), (0, 0)))
    ahead, behind = bias_tiles(lax.all_gather(rel_table, "mp", axis=1, tiled=True))
    marks, query_side, key_side, lo, hi = slot_arrays(seg, live)
    placed = jnp.dot(marks, prompt_all, preferred_element_type=F32)
    x = jnp.where(query_side[:, IS_PROMPT:] > 0, placed, tok.astype(F32))
    normed = (x * rms_factor(x) * gains[8:9]).astype(BF)
    out = jnp.einsum("sd,mdc->smc", normed, weights[0], preferred_element_type=F32)
    half = out.shape[2] // 2
    kv = out[:, :, :half].astype(BF).reshape(slots, -1)
    q = jnp.where(low_lanes(half), out[:, :, half:] * LOG2E, 0.0).astype(BF).reshape(slots, -1)
    return weights, x, kv, q, ahead, behind, marks, query_side, key_side, gains, lo, hi


def adam_kernel(
    part_ref, state_ref, out_ref, land_one, land_two, mid_ref, send_one, recv_one, send_two,
    recv_two,
):
    dp = lax.axis_index("dp")
    mp = lax.axis_index("mp")
    wide = part_ref.shape[0]
    deep = mid_ref.shape[0]
    width = part_ref.shape[2]
    barrier = pltpu.get_barrier_semaphore()
    peers = [{"dp": lax.rem(dp + s, wide)} for s in range(1, wide)]
    peers += [{"mp": lax.rem(mp + s, deep)} for s in range(1, deep)]
    for peer in peers:
        pl.semaphore_signal(barrier, inc=1, device_id=peer, device_id_type=MESH)
    pl.semaphore_wait(barrier, len(peers))
    first = []
    for s in range(1, wide):
        to = lax.rem(dp + s, wide)
        copy = pltpu.make_async_remote_copy(
            src_ref=part_ref.at[to], dst_ref=land_one.at[s - 1],
            send_sem=send_one.at[s - 1], recv_sem=recv_one.at[s - 1],
            device_id={"dp": to}, device_id_type=MESH,
        )
        copy.start()
        first.append(copy)
    total = part_ref[dp]
    for s, copy in enumerate(first):
        copy.wait_recv()
        total = total + land_one[s]
    for m in range(deep):
        mid_ref[m, 0:4] = total[4 * m : 4 * m + 4]
        mid_ref[m, 4:8] = jnp.zeros((4, width), F32)
    second = []
    for s in range(1, deep):
        to = lax.rem(mp + s, deep)
        copy = pltpu.make_async_remote_copy(
            src_ref=mid_ref.at[to], dst_ref=land_two.at[s - 1],
            send_sem=send_two.at[s - 1], recv_sem=recv_two.at[s - 1],
            device_id={"mp": to}, device_id_type=MESH,
        )
        copy.start()
        second.append(copy)
    window = mid_ref[mp]
    for s, copy in enumerate(second):
        copy.wait_recv()
        window = window + land_two[s]
    begin = width // 8 * lax.rem(dp * deep + mp, 8)
    turned = pltpu.roll(window, lax.rem(width - begin, width), 1)
    lane = lax.broadcasted_iota(jnp.int32, (8, width), 1)
    grad = jnp.where(lane < width - begin, turned, pltpu.roll(turned, 7, 0))
    updated = adam_step(grad, state_ref[0], state_ref[1], state_ref[2])
    for i, value in enumerate(updated):
        out_ref[i] = value
    for copy in first + second:
        copy.wait_send()


def adam_step(grad, prompt, moment_one, moment_two):
    first_new = 0.9 * moment_one + 0.1 * grad
    second_new = 0.999 * moment_two + 0.001 * grad * grad
    correct_one = 1.0 - 0.9**ADAM_STEP
    correct_two = 1.0 - 0.999**ADAM_STEP
    prompt_new = prompt - 0.3 * (first_new / correct_one) / (
        jnp.sqrt(second_new / correct_two) + 1e-08
    )
    return prompt_new, first_new, second_new


def adam_call(part, state, deep):
    wide, rows, width = part.shape
    return pl.pallas_call(
        adam_kernel,
        in_specs=[VMEM_SPEC] * 2,
        out_specs=VMEM_SPEC,
        out_shape=jax.ShapeDtypeStruct(state.shape, F32),
        scratch_shapes=[
            pltpu.VMEM((wide - 1, rows, width), F32),
            pltpu.VMEM((deep - 1, 8, width), F32),
            pltpu.VMEM((deep, 8, width), F32),
            pltpu.SemaphoreType.DMA((wide - 1,)),
            pltpu.SemaphoreType.DMA((wide - 1,)),
            pltpu.SemaphoreType.DMA((deep - 1,)),
            pltpu.SemaphoreType.DMA((deep - 1,)),
        ],
        compiler_params=pltpu.CompilerParams(collective_id=1, has_side_effects=True),
        name="sum_and_step",
    )(part, state)


def body(
    dp, mp, tokens, prompt, moment_one, moment_two, segments, live, out_grad, w_query, w_key,
    w_value, w_output, w_inner, w_outer, gain_attn, gain_ffn, rel_table,
):
    _, slots, width = tokens.shape
    tuned = (dp, mp) == (8, 4)
    share = prompt.shape[0]
    if tuned:
        state = jnp.pad(
            jnp.stack([prompt, moment_one, moment_two]), ((0, 0), (0, 8 * width - share))
        ).reshape(3, 8, width)
        (
            w, own, line, near, x, kv, q, ahead, behind, marks, query_side, key_side, gains, lo,
            hi,
        ) = open_call(
            state, gain_attn[None], gain_ffn[None], rel_table.T, w_query, w_key, w_value,
            w_output, w_inner, w_outer.T, segments, live, tokens[0], dp, mp,
        )
        swap = lambda bit: lax.ppermute(line, "dp", [(i, i ^ bit) for i in range(dp)])
        from_east, from_south, from_sib = swap(2), swap(4), swap(1)
    else:
        (
            weights, x, kv, q, ahead, behind, marks, query_side, key_side, gains, lo, hi,
        ) = open_plain(
            tokens[0], prompt, segments[0], live[0], w_query, w_key, w_value, w_output, w_inner,
            w_outer, gain_attn, gain_ffn, rel_table,
        )
    ctx, lse = attend_call(lo, hi, query_side, key_side, kv, q, ahead)
    if tuned:
        layer_output, grad_hidden = feed_call(
            out_grad[0], query_side, gains, x, ctx, w, own, line, near, from_east, from_south,
            from_sib,
        )
        w = w.reshape(mp, width, -1)
    else:
        w = weights[0]
        layer_output, grad_hidden = feed_local(
            x, out_grad[0], query_side, gains, ctx, w, weights[1], weights[2]
        )
    input_grad, prompt_part, layer_output = backward_call(
        lo, hi, grad_hidden, lse, query_side, key_side, marks, gains, kv, w, q, ctx, x, behind,
        layer_output,
    )
    if tuned:
        stepped = adam_call(prompt_part.reshape(dp, -1, width), state, mp)
        stepped = stepped.reshape(3, -1)[:, :share]
        prompt_new, first_new, second_new = stepped[0], stepped[1], stepped[2]
    else:
        grad = lax.psum_scatter(
            prompt_part[:PROMPT].reshape(-1), ("dp", "mp"), scatter_dimension=0, tiled=True
        )
        prompt_new, first_new, second_new = adam_step(grad, prompt, moment_one, moment_two)
    return (layer_output[None], input_grad[None], prompt_new, first_new, second_new)


def solution(mesh):
    both = ("dp", "mp")
    return jax.shard_map(
        functools.partial(body, mesh.shape["dp"], mesh.shape["mp"]),
        mesh=mesh,
        in_specs=(
            P(both, None, None),
            P(both),
            P(both),
            P(both),
            P(both, None),
            P(both, None),
            P(both, None, None),
            P("dp", "mp"),
            P("dp", "mp"),
            P("dp", "mp"),
            P("mp", "dp"),
            P("dp", "mp"),
            P("mp", "dp"),
            P("dp"),
            P("dp"),
            P(None, "mp"),
        ),
        out_specs=(
            P(both, None, None),
            P(both, None, None),
            P(both),
            P(both),
            P(both),
        ),
        check_vma=False,
    )
```

```python
import functools

import jax
import jax.numpy as jnp
from jax import lax
from jax.experimental import pallas as pl
from jax.experimental.pallas import tpu as pltpu
from jax.sharding import PartitionSpec as P

HEADS = 12
HEAD_DIM = 64
BUCKETS = 32
PROMPT = 100
ADAM_STEP = 10
BOUNDS = (1, 2, 3, 4, 5, 6, 7, 8, 12, 16, 23, 32, 46, 64, 91)
EPSILON = 1e-06
MASKED = -1e30
LOG2E = 1.4426950408889634
LN2 = 0.6931471805599453
GELU_C = 0.7978845608028654

BLK = 256
TILE = 128
GROUP = 12
ALIVE = 126
IS_PROMPT = 127
BF = jnp.bfloat16
F32 = jnp.float32
NN = (((1,), (0,)), ((), ()))
NT = (((1,), (1,)), ((), ()))
TN = (((0,), (0,)), ((), ()))
MESH = pl.DeviceIdType.MESH
VMEM_LIMIT = 62 * 1024 * 1024
SMEM_SPEC = pl.BlockSpec(memory_space=pltpu.SMEM)
VMEM_SPEC = pl.BlockSpec(memory_space=pltpu.VMEM)
ANY_SPEC = pl.BlockSpec(memory_space=pl.ANY)


def mm(left, right, dims):
    return lax.dot_general(left, right, dims, preferred_element_type=F32)


def bucket_of(offset, half):
    distance = jnp.abs(offset)
    counted = sum(((distance >= limit).astype(jnp.int32) for limit in BOUNDS))
    return counted + jnp.where(offset > 0, half, 0).astype(jnp.int32)


def span(block, size=BLK):
    return pl.ds(pl.multiple_of(block * size, size), size)


def low_lanes(width=TILE):
    return lax.rem(lax.broadcasted_iota(jnp.int32, (1, width), 1), TILE) < HEAD_DIM


def fill_bias(line_ref, tiles_ref):
    def one(head, carry):
        row = line_ref[pl.ds(head, 1), :]
        wide = pltpu.roll(
            jnp.broadcast_to(row, (TILE, 4 * TILE)), 0, 1, stride=1, stride_axis=0
        )
        for near in range(1, 4):
            tiles_ref[head, near] = wide[:, near * TILE : (near + 1) * TILE]
        tiles_ref[head, 0] = jnp.broadcast_to(row[:, 0:1], (TILE, TILE))
        tiles_ref[head, 4] = jnp.broadcast_to(row[:, 4 * TILE - 1 :], (TILE, TILE))
        return carry

    lax.fori_loop(0, HEADS, one, 0)


def rms_factor(values):
    return lax.rsqrt(jnp.mean(values * values, axis=-1, keepdims=True) + EPSILON)


def neighbours():
    dp = lax.axis_index("dp")
    core = lax.rem(dp, 2)
    across = lax.rem(lax.div(dp, 2), 2)
    down = lax.div(dp, 4)
    return (
        dp + 1 - 2 * core,
        dp + 2 - 4 * across,
        dp + 4 - 8 * down,
        dp + 6 - 4 * across - 8 * down,
    )


def line_order(z, j):
    upper = lax.div(z, 2)
    return (z, z + 1 - 2 * lax.rem(z, 2), 2 - upper, 3 - 3 * upper)[j]


def flat_shift(rows, shift, width):
    lane = lax.broadcasted_iota(jnp.int32, (8, width), 1)
    turned = pltpu.roll(rows, shift, 1)
    return jnp.where(lane >= shift, turned, pltpu.roll(turned, 1, 0))


def interleave(first, second):
    parts = []
    for at in range(0, first.shape[1], HEAD_DIM):
        parts += [first[:, at : at + HEAD_DIM], second[:, at : at + HEAD_DIM]]
    return jnp.concatenate(parts, axis=1)


def open_kernel(
    state_ref, ga_ref, gf_ref, table_ref, wq_ref, wk_ref, wv_ref, wo_ref, wi_ref, wu_ref,
    seg_ref, live_ref, tok_ref,
    w_out, trio_out, last_out, x_out, kv_out, q_out, ahead_out, behind_out,
    marks_ref, qa_ref, ka_ref, gains_ref, lo_ref, hi_ref,
    small_src, small_v, pack_src, w_v, ff_src, x_v, norm_v, kv_v, q_v, lines_v, ahead_v,
    behind_v,
    own_sem, z_send, z_recv, send, recv, line_send, line_recv, out_sem,
):
    mp = lax.axis_index("mp")
    dp = lax.axis_index("dp")
    depth, wide = w_v.shape[0], w_v.shape[1]
    width = tok_ref.shape[1]
    sib, east, south, corner = neighbours()
    up, down = mp + 1 < depth, mp > 0
    barrier = pltpu.get_barrier_semaphore()

    def greet(peer):
        pl.semaphore_signal(barrier, inc=1, device_id=peer, device_id_type=MESH)

    for peer in (sib, east, south):
        greet({"dp": peer})
    pl.when(up)(lambda: greet({"mp": mp + 1}))
    pl.when(down)(lambda: greet({"mp": mp - 1}))

    share = lax.rem(dp * depth + mp, 8)
    part = ga_ref.shape[1]
    empty = jnp.zeros((1, width - part), F32)
    gain_rows = [
        pltpu.roll(jnp.concatenate([ref[...].astype(F32), empty], axis=1), part * dp, 1)
        for ref in (ga_ref, gf_ref)
    ]
    table_rows = jnp.concatenate(
        [table_ref[...].astype(F32), jnp.zeros((HEADS // depth, width - BUCKETS), F32)], axis=1
    )
    small_src[...] = jnp.concatenate(
        [flat_shift(state_ref[0], part * share, width)]
        + gain_rows
        + [table_rows, jnp.zeros((6 - HEADS // depth, width), F32)],
        axis=0,
    ).astype(BF)
    pack_src[...] = jnp.concatenate(
        [interleave(wk_ref[...], wv_ref[...]), interleave(wq_ref[...], wo_ref[...].T)], axis=1
    )
    ff_src[0] = wi_ref[...]
    ff_src[1] = wu_ref[...]
    pl.semaphore_wait(barrier, 3 + up.astype(jnp.int32) + down.astype(jnp.int32))

    def remote(src, dst, send_sem, recv_sem, peer):
        return pltpu.make_async_remote_copy(
            src_ref=src, dst_ref=dst, send_sem=send_sem, recv_sem=recv_sem,
            device_id=peer, device_id_type=MESH,
        )

    started = []
    local = []
    units = [(small_src, small_v), (pack_src, w_v)]

    def along(u, j, src):
        dst = units[u][1]
        z = line_order(mp, j)
        copies = []
        for at, (ahead, there, move) in enumerate(((up, z <= mp, 1), (down, z >= mp, -1))):
            copy = remote(
                src, dst.at[z, dp], z_send.at[u, j, at], z_recv.at[u, z], {"mp": mp + move}
            )
            copies.append((jnp.logical_and(ahead, there), copy))
        return copies

    lined = []

    def launch(copies):
        for condition, copy in copies:
            pl.when(condition)(copy.start)
        lined.extend(copies)

    def push(u, o, kind, src, dst, peer):
        copy = remote(src, dst, send.at[u, o, kind], recv.at[u, o, kind], peer)
        copy.start()
        started.append(copy)

    def landed(u, o, kind, dst):
        remote(dst, dst, send.at[u, o, kind], recv.at[u, o, kind], {"dp": sib}).wait_recv()

    def step(u, o):
        src, dst = units[u]
        z = line_order(mp, o)
        block = dst.at[z, dp]
        if o:
            remote(block, block, z_send.at[u, o, 0], z_recv.at[u, z], {"dp": sib}).wait_recv()
            src = block
        launch(along(u, o, src))
        push(u, o, 0, src, block, {"dp": east})
        push(u, o, 1, src, block, {"dp": south})
        push(u, o, 2, src, block, {"dp": sib})

    def forward(u, o):
        dst = units[u][1]
        z = line_order(mp, o)
        rows = dst.shape[2] // 2 if u else dst.shape[2]
        landed(u, o, 0, dst.at[z, east])
        push(u, o, 3, dst.at[z, east, 0:rows], dst.at[z, east, 0:rows], {"dp": south})
        push(u, o, 4, dst.at[z, east], dst.at[z, east], {"dp": sib})
        landed(u, o, 1, dst.at[z, south])
        if u:
            push(u, o, 5, dst.at[z, south, rows:], dst.at[z, south, rows:], {"dp": east})
        push(u, o, 6, dst.at[z, south], dst.at[z, south], {"dp": sib})

    def finish(u, o):
        dst = units[u][1]
        z = line_order(mp, o)
        rows = dst.shape[2] // 2 if u else dst.shape[2]
        landed(u, o, 3, dst.at[z, corner, 0:rows])
        if u:
            landed(u, o, 5, dst.at[z, corner, rows:])
        push(u, o, 7, dst.at[z, corner], dst.at[z, corner], {"dp": sib})

    flip = 1 - 2 * lax.rem(dp, 2)

    def complete(u, o):
        dst = units[u][1]
        z = line_order(mp, o)
        landed(u, o, 2, dst.at[z, sib])
        landed(u, o, 4, dst.at[z, east + flip])
        landed(u, o, 6, dst.at[z, south + flip])
        landed(u, o, 7, dst.at[z, corner + flip])

    for u in range(2):
        step(u, 0)
        src, dst = units[u]
        copy = pltpu.make_async_copy(src, dst.at[mp, dp], own_sem.at[u])
        copy.start()
        local.append(copy)
    own_copy = pltpu.make_async_copy(ff_src, trio_out.at[0], own_sem.at[2])
    own_copy.start()
    partner = line_order(mp, 1)
    across = depth - 1 - mp
    inside = lax.rem(lax.div(mp + 1, 2), 2) == 1
    at_end = jnp.logical_not(inside)

    def line_copy(src, dst, at, at_recv, to):
        return remote(src, dst, line_send.at[at], line_recv.at[at_recv], {"mp": to})

    pair_copy = line_copy(ff_src, trio_out.at[1], 0, 0, partner)
    over_copy = line_copy(ff_src, trio_out.at[2], 1, 1, across)
    far_copy = line_copy(trio_out.at[1], last_out, 2, 2, across)
    back_copy = line_copy(trio_out.at[2], trio_out.at[2], 3, 1, partner)
    pl.when(at_end)(pair_copy.start)
    pl.when(inside)(over_copy.start)

    slots = tok_ref.shape[0]
    segment_row = seg_ref[...].astype(F32)
    live_row = live_ref[...].astype(F32)
    lane = lax.broadcasted_iota(jnp.int32, (slots, TILE), 1)
    lane_f = lane.astype(F32)
    segment = jnp.broadcast_to(segment_row, (TILE, slots)).T
    alive = jnp.broadcast_to(live_row, (TILE, slots)).T
    same = segment == lane_f
    start = jnp.sum((segment < lane_f).astype(F32), axis=0, keepdims=True)
    first = jnp.sum(jnp.where(same, start, 0.0), axis=1, keepdims=True)
    position = lax.broadcasted_iota(jnp.int32, (slots, 1), 0).astype(F32) - first
    prompt_slot = (alive > 0) & (position < PROMPT)
    sides = jnp.where(lane == ALIVE, alive, same.astype(F32))
    qa_ref[...] = jnp.where(lane == IS_PROMPT, prompt_slot.astype(F32), sides).astype(BF)
    ka_ref[...] = jnp.where(
        (lane < 16) & jnp.logical_not(same & (alive > 0)), MASKED, 0.0
    ).astype(BF)
    step(0, 1)
    forward(0, 0)
    step(0, 2)
    step(1, 1)
    forward(1, 0)
    forward(0, 1)
    finish(0, 0)
    step(0, 3)
    forward(0, 2)
    finish(0, 1)

    def window_rows(device, inside):
        target = 25 * lax.div(device, 8) + 3 * lax.rem(device, 8) + inside
        return jnp.where(inside < 4, target, -1).astype(F32)

    at = lax.broadcasted_iota(jnp.int32, (1, TILE), 1)
    target = window_rows(lax.div(at, 4), lax.rem(at, 4))
    marks_ref[...] = jnp.where((position == target) & prompt_slot, 1.0, 0.0).astype(BF)
    forward(0, 3)
    finish(0, 2)
    step(1, 2)
    forward(1, 1)
    finish(0, 3)
    finish(1, 0)
    block_lane = lax.broadcasted_iota(jnp.int32, (8, TILE), 1)
    lows = jnp.zeros((8, TILE), F32)
    highs = jnp.zeros((8, TILE), F32)
    for block in range(slots // TILE):
        here = segment_row[:, block * TILE : (block + 1) * TILE]
        lives = live_row[:, block * TILE : (block + 1) * TILE] > 0
        top = jnp.max(jnp.where(lives, here, -1.0), axis=1, keepdims=True)
        bottom = jnp.min(here, axis=1, keepdims=True)
        before = jnp.sum((segment_row < bottom).astype(F32), axis=1, keepdims=True)
        through = (segment_row <= top) & (live_row > 0)
        through = jnp.sum(through.astype(F32), axis=1, keepdims=True)
        lows = jnp.where(block_lane == block, before, lows)
        highs = jnp.where(block_lane == block, through, highs)
    highs = lax.div(highs.astype(jnp.int32) + TILE - 1, TILE)
    hi_ref[...] = highs
    lo_ref[...] = jnp.minimum(lax.div(lows.astype(jnp.int32), TILE), highs)
    for o in range(depth):
        complete(0, o)
    local[0].wait()

    gains = functools.reduce(jnp.add, [small_v[0, d].astype(F32) for d in range(wide)])
    gains_ref[...] = gains
    rows_all = depth * wide * 16
    at = lax.broadcasted_iota(jnp.int32, (1, rows_all), 1)
    holder = lax.div(at, 16)
    target = window_rows(
        lax.rem(holder, wide) * depth + lax.div(holder, wide), lax.rem(at, 16)
    )
    windows = small_v[...].reshape(rows_all, width)
    gain = gains[8:9]

    def embed(f):
        rows = slice(f, f + BLK)
        hot = (position[rows] == target).astype(F32).astype(BF)
        placed = mm(hot, windows, NN)
        value = jnp.where(prompt_slot[rows, 0:1], placed, tok_ref[rows, :].astype(F32))
        x_v[rows, :] = value
        norm_v[rows, :] = (value * rms_factor(value) * gain).astype(BF)

    for f in range(0, slots, BLK):
        embed(f)
        if f == slots // 2 - BLK:
            step(1, 3)
            forward(1, 2)
            finish(1, 1)
    copy = pltpu.make_async_copy(x_v, x_out, out_sem.at[0])
    copy.start()
    local.append(copy)

    @pl.when(inside)
    def _():
        pair_copy.start()
        pair_copy.wait_recv()
        far_copy.start()
        over_copy.wait_recv()
        back_copy.start()

    half = w_v.shape[3] // 2
    low = low_lanes(half)

    def project(o):
        complete(1, o)
        if o == 0:
            local[1].wait()
        z = line_order(mp, o)
        copy = pltpu.make_async_copy(w_v.at[z], w_out.at[z], out_sem.at[1 + o])
        copy.start()
        local.append(copy)
        weight = w_v[z].reshape(wide * w_v.shape[2], 2 * half)
        cols = span(z, half)
        parts = [mm(norm_v[f : f + BLK, :], weight, NN) for f in range(0, slots, BLK)]
        for i, piece in enumerate(parts):
            rows = slice(i * BLK, (i + 1) * BLK)
            kv_v[rows, cols] = piece[:, :half].astype(BF)
            q_v[rows, cols] = jnp.where(low, piece[:, half:] * LOG2E, 0.0).astype(BF)
        for at_sem, (src, dst) in enumerate(((kv_v, kv_out), (q_v, q_out))):
            copy = pltpu.make_async_copy(
                src.at[:, cols], dst.at[:, cols], out_sem.at[1 + depth + 2 * o + at_sem]
            )
            copy.start()
            local.append(copy)

    table = jnp.concatenate(
        [small_v[m, 0].astype(F32)[10 : 10 + HEADS // depth, 0:TILE] for m in range(depth)]
        + [jnp.zeros((16 - HEADS, TILE), F32)],
        axis=0,
    ).astype(BF)
    offset = lax.broadcasted_iota(jnp.int32, (1, 4 * TILE), 1) - 2 * TILE
    code = lax.broadcasted_iota(jnp.int32, (TILE, 4 * TILE), 0)
    def bias_out(at_sem, sign, tiles, out):
        hot = (code == bucket_of(sign * offset, BUCKETS // 2)).astype(F32).astype(BF)
        lines_v[...] = mm(table, hot, NN) * LOG2E
        fill_bias(lines_v, tiles)
        copy = pltpu.make_async_copy(tiles, out, out_sem.at[1 + 3 * depth + at_sem])
        copy.start()
        local.append(copy)

    bias_out(0, 1, ahead_v, ahead_out)
    forward(1, 3)
    finish(1, 2)
    project(0)
    finish(1, 3)
    project(1)
    project(2)
    bias_out(1, -1, behind_v, behind_out)
    project(3)
    own_copy.wait()
    pair_copy.wait_send()

    @pl.when(at_end)
    def _():
        pair_copy.wait_recv()
        back_copy.wait_recv()

    @pl.when(inside)
    def _():
        over_copy.wait_send()
        far_copy.wait()
        back_copy.wait_send()

    for copy in local[2:]:
        copy.wait()
    for copy in started:
        copy.wait_send()
    for condition, copy in lined:
        pl.when(condition)(copy.wait_send)


def open_call(state, ga, gf, table, wq, wk, wv, wo, wi, wu, seg, live, tok, dp, mp):
    slots, width = tok.shape
    rows = wi.shape[0]
    wide = HEADS * TILE
    pack = (rows, width)
    shape = jax.ShapeDtypeStruct
    dma = pltpu.SemaphoreType.DMA
    tiles = (HEADS, 5, TILE, TILE)
    return pl.pallas_call(
        open_kernel,
        in_specs=[VMEM_SPEC] * 13,
        out_specs=[ANY_SPEC] * 8 + [VMEM_SPEC] * 6,
        out_shape=[
            shape((mp, dp) + pack, BF),
            shape((3, 2) + pack, BF),
            shape((2,) + pack, BF),
            shape((slots, width), F32),
            shape((slots, wide), BF),
            shape((slots, wide), BF),
            shape(tiles, F32),
            shape(tiles, F32),
            shape((slots, TILE), BF),
            shape((slots, TILE), BF),
            shape((slots, TILE), BF),
            shape((16, width), F32),
            shape((8, TILE), jnp.int32),
            shape((8, TILE), jnp.int32),
        ],
        scratch_shapes=[
            pltpu.VMEM((16, width), BF),
            pltpu.VMEM((mp, dp, 16, width), BF),
            pltpu.VMEM(pack, BF),
            pltpu.VMEM((mp, dp) + pack, BF),
            pltpu.VMEM((2,) + pack, BF),
            pltpu.VMEM((slots, width), F32),
            pltpu.VMEM((slots, width), BF),
            pltpu.VMEM((slots, wide), BF),
            pltpu.VMEM((slots, wide), BF),
            pltpu.VMEM((16, 4 * TILE), F32),
            pltpu.VMEM(tiles, F32),
            pltpu.VMEM(tiles, F32),
            dma((3,)),
            dma((2, mp, 2)),
            dma((2, mp)),
            dma((2, mp, 8)),
            dma((2, mp, 8)),
            dma((4,)),
            dma((3,)),
            dma((3 + 3 * mp,)),
        ],
        compiler_params=pltpu.CompilerParams(
            collective_id=0, has_side_effects=True, vmem_limit_bytes=VMEM_LIMIT
        ),
        cost_estimate=pl.CostEstimate(
            flops=16 * 10**9, bytes_accessed=40 * 10**6, transcendentals=0
        ),
        name="open_layer",
    )(state, ga, gf, table, wq, wk, wv, wo, wi, wu, seg, live, tok)


def window_of(lo_ref, hi_ref, block, blocks):
    lo = lo_ref[0, block]
    pairs = lax.div(hi_ref[0, block] - lo + 1, 2)
    return jnp.minimum(lo, blocks - 2 * pairs), pairs


def bias_row(tiles_ref, head, first, block, pairs):
    return jnp.concatenate(
        [
            tiles_ref[head, jnp.clip(first + j - block, -2, 2) + 2]
            for j in range(2 * pairs)
        ],
        axis=1,
    )


def attend_kernel(
    lo_ref, hi_ref, qa_ref, ka_ref, kv_hbm, q_hbm, tiles_hbm,
    ctx_out, lse_ref,
    kv_ref, val_ref, q_ref, ctx_ref, tiles_ref, lsem_ref, mean_ref, sems, ctx_sems,
):
    slots = qa_ref.shape[0]
    blocks = slots // TILE
    copies = [
        pltpu.make_async_copy(src, dst, sems.at[i])
        for i, (src, dst) in enumerate(
            ((kv_hbm, kv_ref), (q_hbm, q_ref), (tiles_hbm, tiles_ref))
        )
    ]
    for copy in copies:
        copy.start()
    copies[0].wait()
    mean_ref[...] = mm(jnp.full((8, slots), 1.0 / slots, BF), kv_ref[...], NN)
    high = jnp.logical_not(low_lanes())
    ones = jnp.ones((slots, TILE), BF)
    for h in range(HEADS):
        cols = slice(h * TILE, (h + 1) * TILE)
        val_ref[:, cols] = jnp.where(high, kv_ref[:, cols], ones)
    lane = lax.broadcasted_iota(jnp.int32, (1, TILE), 1)
    copies[1].wait()
    copies[2].wait()

    def query_block(qb, carry):
        qs = span(qb, TILE)
        first, count = window_of(lo_ref, hi_ref, qb, blocks)
        alive = qa_ref[qs, ALIVE : ALIVE + 1].astype(F32) > 0
        lsem_ref[...] = jnp.zeros_like(lsem_ref)

        def attend(pairs):
            size = 2 * pairs * TILE
            ks = pl.ds(pl.multiple_of(first * TILE, TILE), size)
            mask = mm(qa_ref[qs, :], ka_ref[ks, :], NT)

            def group_body(g, inner):
                heads = [g * GROUP + i for i in range(GROUP)]
                cols = [span(h, TILE) for h in heads]
                scores = [
                    mm(q_ref[qs, c], kv_ref[ks, c], NT)
                    + (bias_row(tiles_ref, h, first, qb, pairs) + mask)
                    for h, c in zip(heads, cols)
                ]
                tops = [jnp.max(row, axis=1, keepdims=True) for row in scores]
                weights = [jnp.exp2(row - top).astype(BF) for row, top in zip(scores, tops)]
                for h, c, top, weight in zip(heads, cols, tops, weights):
                    both = mm(weight, val_ref[ks, c], NN)
                    context = both / pltpu.roll(both, HEAD_DIM, 1)
                    context = jnp.where(alive, context, mean_ref[0:1, c])
                    ctx_ref[qs, c] = jnp.where(high, context, 0.0).astype(BF)
                    lsem_ref[...] = jnp.where(
                        (lane == h) & alive, top + jnp.log2(both), lsem_ref[...]
                    )
                return inner

            lax.fori_loop(0, HEADS // GROUP, group_body, 0)

        for pairs in range(1, blocks // 2 + 1):
            pl.when(count == pairs)(functools.partial(attend, pairs))

        @pl.when(count == 0)
        def _():
            every = jnp.logical_not(low_lanes(HEADS * TILE))
            ctx_ref[qs, :] = jnp.broadcast_to(
                jnp.where(every, mean_ref[0:1, :], 0.0), (TILE, HEADS * TILE)
            ).astype(BF)

        lse_ref[:, qs] = lsem_ref[...].T[0:16]
        pltpu.make_async_copy(ctx_ref.at[qs], ctx_out.at[qs], ctx_sems.at[qb]).start()
        return carry

    lax.fori_loop(0, blocks, query_block, 0)
    for b in range(blocks):
        rows = slice(b * TILE, (b + 1) * TILE)
        pltpu.make_async_copy(ctx_ref.at[rows], ctx_out.at[rows], ctx_sems.at[b]).wait()


def attend_call(lo, hi, qa, ka, kv, q, tiles):
    slots, wide = kv.shape
    return pl.pallas_call(
        attend_kernel,
        in_specs=[SMEM_SPEC] * 2 + [VMEM_SPEC] * 2 + [ANY_SPEC] * 3,
        out_specs=[ANY_SPEC, VMEM_SPEC],
        out_shape=[
            jax.ShapeDtypeStruct((slots, wide), BF),
            jax.ShapeDtypeStruct((16, slots), F32),
        ],
        scratch_shapes=[
            pltpu.VMEM((slots, wide), BF),
            pltpu.VMEM((slots, wide), BF),
            pltpu.VMEM((slots, wide), BF),
            pltpu.VMEM((slots, wide), BF),
            pltpu.VMEM(tiles.shape, F32),
            pltpu.VMEM((TILE, TILE), F32),
            pltpu.VMEM((8, wide), F32),
            pltpu.SemaphoreType.DMA((3,)),
            pltpu.SemaphoreType.DMA((slots // TILE,)),
        ],
        compiler_params=pltpu.CompilerParams(vmem_limit_bytes=VMEM_LIMIT),
        cost_estimate=pl.CostEstimate(
            flops=25 * 10**9, bytes_accessed=10**7, transcendentals=10**7
        ),
        name="attend",
    )(lo, hi, qa, ka, kv, q, tiles)


def gelu_both(inner, upstream):
    square = inner * inner
    bent = jnp.tanh(inner * (GELU_C + (GELU_C * 0.044715) * square))
    half = 0.5 + 0.5 * bent
    activated = inner * half
    slope = half + activated * ((1.0 - half) * (2 * GELU_C + (6 * GELU_C * 0.044715) * square))
    return activated.astype(BF), (upstream * slope).astype(BF)


def feed_kernel(
    og_ref, qa_ref, gains_ref, x_hbm, ctx_hbm, w_hbm, trio_hbm, east_hbm, south_hbm, sib_hbm,
    last_hbm, lasted_hbm,
    out_ref, gh_ref,
    ff_v, ctx_ref, w_ref, norm_ref, gb_ref, hid_ref, br_ref, dn_ref,
    sems, fill, send, recv,
):
    dp = lax.axis_index("dp")
    mp = lax.axis_index("mp")
    depth, wide = ff_v.shape[0], ff_v.shape[1]
    half = w_hbm.shape[3] // 2
    rows_half = ff_v.shape[3] // 2
    sib, east, south, corner = neighbours()
    flip = 1 - 2 * lax.rem(dp, 2)
    upper, lower = pl.ds(0, rows_half), pl.ds(rows_half, rows_half)
    inside = lax.rem(lax.div(mp + 1, 2), 2) == 1
    barrier = pltpu.get_barrier_semaphore()
    for peer in (sib, east, south):
        pl.semaphore_signal(barrier, inc=1, device_id={"dp": peer}, device_id_type=MESH)
    first = [
        pltpu.make_async_copy(ctx_hbm, ctx_ref, sems.at[0]),
        pltpu.make_async_copy(x_hbm, hid_ref, sems.at[1]),
    ]
    for m in range(depth):
        first.append(
            pltpu.make_async_copy(w_hbm.at[m, :, :, half:], w_ref.at[m], sems.at[2 + m])
        )
    end = depth - 1
    for here, source in ((inside, last_hbm), (jnp.logical_not(inside), lasted_hbm)):
        pl.when(here)(pltpu.make_async_copy(source, ff_v.at[end, dp], fill.at[end, 0]).start)
    for copy in first:
        copy.start()
    pl.semaphore_wait(barrier, 3)

    def remote(src, dst, j, kind, peer):
        return pltpu.make_async_remote_copy(
            src_ref=src, dst_ref=dst, send_sem=send.at[j, kind], recv_sem=recv.at[j, kind],
            device_id={"dp": peer}, device_id_type=MESH,
        )

    sent = []

    def push(src, dst, j, kind, peer):
        copy = remote(src, dst, j, kind, peer)
        copy.start()
        sent.append(copy)

    def awaited(block, j, kind):
        remote(block, block, j, kind, sib).wait_recv()

    def relay(j, from_east, from_south):
        push(from_east.at[:, upper], ff_v.at[j, east, :, upper], j, 0, south)
        push(from_south.at[:, lower], ff_v.at[j, south, :, lower], j, 1, east)
        push(from_east, ff_v.at[j, east], j, 2, sib)
        push(from_south, ff_v.at[j, south], j, 3, sib)

    for j in range(end):
        relay(j, east_hbm.at[j], south_hbm.at[j])
        for kind, (src, place) in enumerate(
            ((trio_hbm, dp), (east_hbm, east), (south_hbm, south), (sib_hbm, sib))
        ):
            pltpu.make_async_copy(src.at[j], ff_v.at[j, place], fill.at[j, kind]).start()

    def spread(j):
        block = ff_v.at[j, dp]
        pltpu.make_async_copy(block, block, fill.at[j, 0]).wait()
        for kind, peer in ((5, east), (6, south), (7, sib)):
            push(block, block, j, kind, peer)

    spread(end)

    def pass_on(j):
        awaited(ff_v.at[j, east], j, 5)
        awaited(ff_v.at[j, south], j, 6)
        relay(j, ff_v.at[j, east], ff_v.at[j, south])

    def corners(j):
        block = ff_v.at[j, corner]
        awaited(ff_v.at[j, corner, :, upper], j, 0)
        awaited(ff_v.at[j, corner, :, lower], j, 1)
        push(block, block, j, 4, sib)

    def landed(j):
        for kind, place in ((2, east + flip), (3, south + flip), (4, corner + flip)):
            awaited(ff_v.at[j, place], j, kind)
        if j < end:
            for kind, place in enumerate((dp, east, south, sib)):
                block = ff_v.at[j, place]
                pltpu.make_async_copy(block, block, fill.at[j, kind]).wait()
        else:
            awaited(ff_v.at[j, sib], j, 7)

    slots = og_ref.shape[0]
    gain = gains_ref[9:10]
    blocks = [slice(f, f + BLK) for f in range(0, slots, BLK)]
    for rows in blocks:
        gb_ref[rows, :] = (
            og_ref[rows, :].astype(F32) * qa_ref[rows, ALIVE : ALIVE + 1].astype(F32)
        ).astype(BF)
    br_ref[...] = jnp.zeros_like(br_ref)
    dn_ref[...] = jnp.zeros_like(dn_ref)
    for copy in first:
        copy.wait()
    for m in range(depth):
        cols = slice(m * half, (m + 1) * half)
        weight = w_ref[m].reshape(-1, half)
        for rows in blocks:
            hid_ref[rows, :] += mm(ctx_ref[rows, cols], weight, NT)
        if m == 1:
            corners(0)
    corners(1)
    for rows in blocks:
        hidden = hid_ref[rows, :]
        norm_ref[rows, :] = (hidden * rms_factor(hidden) * gain).astype(BF)

    def unit_block(j, chosen):
        wi = ff_v[j, :, 0].reshape(-1, ff_v.shape[4])
        wo = ff_v[j, :, 1].reshape(-1, ff_v.shape[4])
        inner = [mm(norm_ref[rows, :], wi, NN) for rows in chosen]
        upstream = [mm(gb_ref[rows, :], wo, NN) for rows in chosen]
        pairs = [gelu_both(a, b) for a, b in zip(inner, upstream)]
        for rows, (activated, grad_inner) in zip(chosen, pairs):
            br_ref[rows, :] += mm(activated, wo, NT)
            dn_ref[rows, :] += mm(grad_inner, wi, NT)

    landed(0)
    unit_block(0, blocks)
    corners(2)
    pass_on(3)
    landed(1)
    unit_block(1, blocks)
    corners(3)
    landed(2)
    unit_block(2, blocks)
    landed(3)
    unit_block(3, blocks)
    for rows in blocks:
        hidden = hid_ref[rows, :]
        alive = qa_ref[rows, ALIVE : ALIVE + 1].astype(F32)
        out_ref[rows, :] = (alive * (hidden + br_ref[rows, :])).astype(BF)
        factor = rms_factor(hidden)
        weighted = dn_ref[rows, :] * gain
        gh_ref[rows, :] = og_ref[rows, :].astype(F32) * alive + (
            factor * weighted
            - hidden
            * (factor * factor * factor)
            * jnp.mean(weighted * hidden, axis=-1, keepdims=True)
        )
    for copy in sent:
        copy.wait_send()


def feed_call(
    og, qa, gains, x, ctx, w, trio, from_east, from_south, from_sib, last, lasted
):
    slots, width = x.shape
    depth, wide, rows, units = w.shape
    dma = pltpu.SemaphoreType.DMA
    return pl.pallas_call(
        feed_kernel,
        in_specs=[VMEM_SPEC] * 3 + [ANY_SPEC] * 9,
        out_specs=[VMEM_SPEC] * 2,
        out_shape=[
            jax.ShapeDtypeStruct((slots, width), BF),
            jax.ShapeDtypeStruct((slots, width), F32),
        ],
        scratch_shapes=[
            pltpu.VMEM((depth, wide) + trio.shape[1:], BF),
            pltpu.VMEM(ctx.shape, BF),
            pltpu.VMEM((depth, wide, rows, units // 2), BF),
            pltpu.VMEM((slots, width), BF),
            pltpu.VMEM((slots, width), BF),
            pltpu.VMEM((slots, width), F32),
            pltpu.VMEM((slots, width), F32),
            pltpu.VMEM((slots, width), F32),
            dma((2 + depth,)),
            dma((depth, 4)),
            dma((depth, 8)),
            dma((depth, 8)),
        ],
        compiler_params=pltpu.CompilerParams(
            collective_id=2, has_side_effects=True, vmem_limit_bytes=VMEM_LIMIT
        ),
        name="feed_forward",
    )(og, qa, gains, x, ctx, w, trio, from_east, from_south, from_sib, last, lasted)


def feed_local_kernel(
    x_ref, og_ref, qa_ref, gain_ref, ctx_hbm, w_hbm, wi_hbm, wo_hbm,
    out_ref, gh_ref,
    ctx_ref, w_ref, wi_ref, wo_ref, norm_ref, gb_ref, hid_ref, br_ref, dn_ref, sems,
):
    slots = x_ref.shape[0]
    groups = w_hbm.shape[0]
    half = w_hbm.shape[2] // 2
    first = [pltpu.make_async_copy(ctx_hbm, ctx_ref, sems.at[0])]
    for m in range(groups):
        first.append(
            pltpu.make_async_copy(w_hbm.at[m, :, half:], w_ref.at[m], sems.at[1 + m])
        )
    later = []
    for m in range(groups):
        later.append(
            (
                pltpu.make_async_copy(wi_hbm.at[m], wi_ref.at[m], sems.at[1 + groups + 2 * m]),
                pltpu.make_async_copy(wo_hbm.at[m], wo_ref.at[m], sems.at[2 + groups + 2 * m]),
            )
        )
    for copy in first:
        copy.start()
    for pair in later:
        pair[0].start()
        pair[1].start()
    for copy in first:
        copy.wait()
    gain = gain_ref[9:10]
    blocks = [slice(f, f + BLK) for f in range(0, slots, BLK)]
    for rows in blocks:
        hid_ref[rows, :] = x_ref[rows, :]
    for m in range(groups):
        cols = slice(m * half, (m + 1) * half)
        for rows in blocks:
            hid_ref[rows, :] += mm(ctx_ref[rows, cols], w_ref[m], NT)
    for rows in blocks:
        hidden = hid_ref[rows, :]
        norm_ref[rows, :] = (hidden * rms_factor(hidden) * gain).astype(BF)
        gb_ref[rows, :] = (
            og_ref[rows, :].astype(F32) * qa_ref[rows, ALIVE : ALIVE + 1].astype(F32)
        ).astype(BF)
    br_ref[...] = jnp.zeros_like(br_ref)
    dn_ref[...] = jnp.zeros_like(dn_ref)
    for m in range(groups):
        later[m][0].wait()
        later[m][1].wait()
    def unit_block(m, carry):
        inner = [mm(norm_ref[rows, :], wi_ref[m], NN) for rows in blocks]
        upstream = [mm(gb_ref[rows, :], wo_ref[m], NN) for rows in blocks]
        pairs = [gelu_both(a, b) for a, b in zip(inner, upstream)]
        for rows, (activated, grad_inner) in zip(blocks, pairs):
            br_ref[rows, :] += mm(activated, wo_ref[m], NT)
            dn_ref[rows, :] += mm(grad_inner, wi_ref[m], NT)
        return carry

    lax.fori_loop(0, groups, unit_block, 0)
    for rows in blocks:
        hidden = hid_ref[rows, :]
        alive = qa_ref[rows, ALIVE : ALIVE + 1].astype(F32)
        out_ref[rows, :] = (alive * (hidden + br_ref[rows, :])).astype(BF)
        factor = rms_factor(hidden)
        weighted = dn_ref[rows, :] * gain
        gh_ref[rows, :] = og_ref[rows, :].astype(F32) * alive + (
            factor * weighted
            - hidden
            * (factor * factor * factor)
            * jnp.mean(weighted * hidden, axis=-1, keepdims=True)
        )


def feed_local(x, og, qa, gain, ctx, w, wi, wo):
    slots, width = x.shape
    groups = w.shape[0]
    return pl.pallas_call(
        feed_local_kernel,
        in_specs=[VMEM_SPEC] * 4 + [ANY_SPEC] * 4,
        out_specs=[VMEM_SPEC] * 2,
        out_shape=[
            jax.ShapeDtypeStruct((slots, width), BF),
            jax.ShapeDtypeStruct((slots, width), F32),
        ],
        scratch_shapes=[
            pltpu.VMEM(ctx.shape, BF),
            pltpu.VMEM((groups, w.shape[1], w.shape[2] // 2), BF),
            pltpu.VMEM(wi.shape, BF),
            pltpu.VMEM(wo.shape, BF),
            pltpu.VMEM((slots, width), BF),
            pltpu.VMEM((slots, width), BF),
            pltpu.VMEM((slots, width), F32),
            pltpu.VMEM((slots, width), F32),
            pltpu.VMEM((slots, width), F32),
            pltpu.SemaphoreType.DMA((1 + 3 * groups,)),
        ],
        compiler_params=pltpu.CompilerParams(vmem_limit_bytes=VMEM_LIMIT),
        name="feed_forward_local",
    )(x, og, qa, gain, ctx, w, wi, wo)


def backward_kernel(
    lo_ref, hi_ref, gh_ref, lse_ref, qa_ref, ka_ref, marks_ref, gains_ref, kv_hbm, w_hbm, q_hbm,
    ctx_hbm, x_hbm, tiles_hbm, layer_hbm,
    ig_ref, pg_ref, layer_out,
    kv_ref, w_ref, q_ref, ctx_ref, x_ref, tiles_ref, layer_ref, all_ref, kt_ref, dsum_ref,
    dqt_ref, sems,
):
    slots = gh_ref.shape[0]
    count_blocks = slots // TILE
    groups = w_hbm.shape[0]
    half = w_hbm.shape[2] // 2
    per = HEADS // groups
    weights = [pltpu.make_async_copy(w_hbm.at[m], w_ref.at[m], sems.at[m]) for m in range(groups)]
    q_copy, ctx_copy, kv_copy, tiles_copy, x_copy, layer_copy = [
        pltpu.make_async_copy(src, dst, sems.at[groups + i])
        for i, (src, dst) in enumerate(
            (
                (q_hbm, q_ref),
                (ctx_hbm, ctx_ref),
                (kv_hbm, kv_ref),
                (tiles_hbm, tiles_ref),
                (x_hbm, x_ref),
                (layer_hbm, layer_ref),
            )
        )
    ]
    for copy in [q_copy] + weights + [ctx_copy, kv_copy, tiles_copy, x_copy, layer_copy]:
        copy.start()
    dqt_ref[...] = jnp.zeros_like(dqt_ref)
    blocks = [slice(f, f + BLK) for f in range(0, slots, BLK)]
    low_half = low_lanes(half)
    q_copy.wait()
    grads_low = [gh_ref[rows, :].astype(BF) for rows in blocks]
    for m in range(groups):
        weights[m].wait()
        cols = slice(m * half, (m + 1) * half)
        parts = [mm(grad, w_ref[m, :, half:], NN) for grad in grads_low]
        for rows, part in zip(blocks, parts):
            q_ref[rows, cols] = jnp.where(low_half, q_ref[rows, cols], part.astype(BF))
    ctx_copy.wait()
    wide = HEADS * TILE
    pick = (
        lax.broadcasted_iota(jnp.int32, (wide, TILE), 0) // TILE
        == lax.broadcasted_iota(jnp.int32, (wide, TILE), 1)
    ).astype(F32).astype(BF)
    sums = []
    for rows in blocks:
        product = q_ref[rows, :].astype(F32) * ctx_ref[rows, :].astype(F32)
        upper = product.astype(BF)
        lower = (product - upper.astype(F32)).astype(BF)
        sums.append(mm(upper, pick, NN) + mm(lower, pick, NN))
    for rows, value in zip(blocks, sums):
        dsum_ref[:, rows] = value.T[0:16]
    kv_copy.wait()
    for h in range(HEADS):
        kt_ref[h] = kv_ref[:, h * TILE : (h + 1) * TILE].T[0:HEAD_DIM]
    tiles_copy.wait()
    low = low_lanes()

    def place_of(h, second):
        place = lax.div(h, per) * (2 * half) + second * half + lax.rem(h, per) * TILE
        return pl.ds(pl.multiple_of(place, TILE), TILE)

    def key_block(kb, carry):
        ks = span(kb, TILE)
        first, count = window_of(lo_ref, hi_ref, kb, count_blocks)

        def attend(pairs):
            size = 2 * pairs * TILE
            qs = pl.ds(pl.multiple_of(first * TILE, TILE), size)
            mask = mm(ka_ref[ks, :], qa_ref[qs, :], NT)

            def group_body(g, inner):
                heads = [g * GROUP + i for i in range(GROUP)]
                cols = [span(h, TILE) for h in heads]
                zero = jnp.zeros((TILE, TILE), BF)
                keys = [kv_ref[ks, c] for c in cols]
                raw = [
                    mm(
                        jnp.concatenate(
                            [jnp.where(low, key, zero), jnp.where(low, zero, key)], axis=0
                        ),
                        q_ref[qs, c],
                        NT,
                    )
                    for key, c in zip(keys, cols)
                ]
                probs = [
                    jnp.exp2(
                        both[:TILE]
                        + (bias_row(tiles_ref, h, first, kb, pairs) + mask)
                        - lse_ref[pl.ds(h, 1), qs]
                    )
                    for h, both in zip(heads, raw)
                ]
                outs = [
                    (p * (both[TILE:] - dsum_ref[pl.ds(h, 1), qs])).astype(BF)
                    for h, p, both in zip(heads, probs, raw)
                ]
                sides = [
                    jnp.concatenate([out, p.astype(BF)], axis=0) for out, p in zip(outs, probs)
                ]
                for h, c, out, side in zip(heads, cols, outs, sides):
                    both = mm(side, q_ref[qs, c], NN)
                    all_ref[ks, place_of(h, 0)] = jnp.where(
                        low, both[:TILE] * LN2, both[TILE:]
                    ).astype(BF)
                    dqt_ref[h, :, qs] += mm(kt_ref[h, :, ks], out, NN)
                return inner

            lax.fori_loop(0, HEADS // GROUP, group_body, 0)

        for pairs in range(1, count_blocks // 2 + 1):
            pl.when(count == pairs)(functools.partial(attend, pairs))

        @pl.when(count == 0)
        def _():
            all_ref[ks, :] = jnp.zeros((TILE, all_ref.shape[1]), BF)

        return carry

    lax.fori_loop(0, count_blocks, key_block, 0)
    rest = jnp.zeros((TILE - HEAD_DIM, slots), BF)
    for h in range(HEADS):
        place = (h // per) * (2 * half) + half + (h % per) * TILE
        all_ref[:, place : place + TILE] = jnp.concatenate(
            [dqt_ref[h].astype(BF), rest], axis=0
        ).T
    x_copy.wait()
    layer_copy.wait()
    layer_copy = pltpu.make_async_copy(layer_ref, layer_out, sems.at[groups + 5])
    layer_copy.start()
    gain = gains_ref[8:9]
    backs = [
        functools.reduce(
            jnp.add,
            [
                mm(all_ref[rows, m * 2 * half : (m + 1) * 2 * half], w_ref[m], NT)
                for m in range(groups)
            ],
        )
        for rows in blocks
    ]
    total = None
    for rows, back in zip(blocks, backs):
        value = x_ref[rows, :]
        factor = rms_factor(value)
        weighted = back * gain
        grad = gh_ref[rows, :] + (
            factor * weighted
            - value
            * (factor * factor * factor)
            * jnp.mean(weighted * value, axis=-1, keepdims=True)
        )
        ig_ref[rows, :] = jnp.where(
            qa_ref[rows, IS_PROMPT : IS_PROMPT + 1].astype(F32) > 0, 0.0, grad
        )
        upper = grad.astype(BF)
        lower = (grad - upper.astype(F32)).astype(BF)
        hot = marks_ref[rows, :]
        part = mm(hot, upper, TN) + mm(hot, lower, TN)
        total = part if total is None else total + part
    pg_ref[...] = total
    layer_copy.wait()


def backward_call(
    lo, hi, gh, lse, qa, ka, marks, gains, kv, w, q, ctx, x, tiles, layer_output
):
    slots, width = gh.shape
    groups = w.shape[0]
    return pl.pallas_call(
        backward_kernel,
        in_specs=[SMEM_SPEC] * 2 + [VMEM_SPEC] * 6 + [ANY_SPEC] * 7,
        out_specs=[VMEM_SPEC] * 2 + [ANY_SPEC],
        out_shape=[
            jax.ShapeDtypeStruct((slots, width), F32),
            jax.ShapeDtypeStruct((TILE, width), F32),
            jax.ShapeDtypeStruct((slots, width), BF),
        ],
        scratch_shapes=[
            pltpu.VMEM(kv.shape, BF),
            pltpu.VMEM(w.shape, BF),
            pltpu.VMEM(q.shape, BF),
            pltpu.VMEM(ctx.shape, BF),
            pltpu.VMEM(x.shape, F32),
            pltpu.VMEM(tiles.shape, F32),
            pltpu.VMEM(layer_output.shape, BF),
            pltpu.VMEM((slots, 2 * HEADS * TILE), BF),
            pltpu.VMEM((HEADS, HEAD_DIM, slots), BF),
            pltpu.VMEM((16, slots), F32),
            pltpu.VMEM((HEADS, HEAD_DIM, slots), F32),
            pltpu.SemaphoreType.DMA((groups + 6,)),
        ],
        compiler_params=pltpu.CompilerParams(vmem_limit_bytes=VMEM_LIMIT),
        name="attend_back",
    )(lo, hi, gh, lse, qa, ka, marks, gains, kv, w, q, ctx, x, tiles, layer_output)


def slot_arrays(segments, live):
    slots = segments.shape[0]
    place = jnp.arange(slots, dtype=jnp.int32)
    first = jnp.sum((segments[None, :] < segments[:, None]).astype(jnp.int32), axis=1)
    position = place - first
    alive = live[:, None] == 1
    is_prompt = alive & (position < PROMPT)[:, None]
    lane = jnp.arange(TILE, dtype=jnp.int32)[None, :]
    marks = ((position[:, None] == lane) & is_prompt).astype(BF)
    same = segments[:, None] == lane
    query_side = jnp.where(lane == ALIVE, alive, same)
    query_side = jnp.where(lane == IS_PROMPT, is_prompt, query_side).astype(BF)
    key_side = jnp.where((lane < 16) & jnp.logical_not(same & alive), MASKED, 0.0).astype(BF)
    by_block = segments.reshape(-1, TILE)
    top = jnp.max(jnp.where(live.reshape(-1, TILE) == 1, by_block, -1), axis=1)
    hi = jnp.sum((segments[None, :] <= top[:, None]) & (live[None, :] == 1), axis=1)
    hi = (hi.astype(jnp.int32) + TILE - 1) // TILE
    lo = jnp.sum((segments[None, :] < by_block[:, :1]).astype(jnp.int32), axis=1) // TILE
    return marks, query_side, key_side, jnp.minimum(lo, hi)[None], hi[None]


def bias_tiles(table):
    place = jnp.arange(TILE, dtype=jnp.int32)
    kinds = jnp.arange(-2, 3, dtype=jnp.int32)[:, None, None] * TILE
    offset = jnp.clip(kinds + place[None, None, :] - place[None, :, None], -TILE, TILE)
    both = []
    for sign in (1, -1):
        both.append(
            table.astype(F32)[bucket_of(sign * offset, BUCKETS // 2)].transpose(3, 0, 1, 2) * LOG2E
        )
    return both


def tiles_of(first, second):
    rows = first.shape[0]
    shaped = [part.reshape(rows, -1, 1, HEAD_DIM) for part in (first, second)]
    return jnp.concatenate(shaped, axis=2).reshape(rows, -1)


def open_plain(
    tok, prompt, seg, live, w_query, w_key, w_value, w_output, w_inner, w_outer, gain_attn,
    gain_ffn, rel_table,
):
    slots, width = tok.shape
    packs = jnp.stack(
        [
            jnp.concatenate([tiles_of(w_key, w_value), tiles_of(w_query, w_output.T)], axis=1),
            w_inner,
            w_outer.T,
        ]
    )
    weights = lax.all_gather(lax.all_gather(packs, "dp", axis=1, tiled=True), "mp", axis=1)
    prompt_all = lax.all_gather(prompt.astype(BF), ("dp", "mp"), tiled=True)
    prompt_all = jnp.pad(prompt_all.reshape(PROMPT, width), ((0, TILE - PROMPT), (0, 0)))
    gains = lax.all_gather(jnp.stack([gain_attn, gain_ffn]), "dp", axis=1, tiled=True)
    gains = jnp.pad(gains.astype(F32), ((8, 6), (0, 0)))
    ahead, behind = bias_tiles(lax.all_gather(rel_table, "mp", axis=1, tiled=True))
    marks, query_side, key_side, lo, hi = slot_arrays(seg, live)
    placed = jnp.dot(marks, prompt_all, preferred_element_type=F32)
    x = jnp.where(query_side[:, IS_PROMPT:] > 0, placed, tok.astype(F32))
    normed = (x * rms_factor(x) * gains[8:9]).astype(BF)
    out = jnp.einsum("sd,mdc->smc", normed, weights[0], preferred_element_type=F32)
    half = out.shape[2] // 2
    kv = out[:, :, :half].astype(BF).reshape(slots, -1)
    q = jnp.where(low_lanes(half), out[:, :, half:] * LOG2E, 0.0).astype(BF).reshape(slots, -1)
    return weights, x, kv, q, ahead, behind, marks, query_side, key_side, gains, lo, hi


def adam_kernel(
    part_ref, state_ref, out_ref, land_one, land_two, mid_ref, send_one, recv_one, send_two,
    recv_two,
):
    dp = lax.axis_index("dp")
    mp = lax.axis_index("mp")
    wide = part_ref.shape[0]
    deep = mid_ref.shape[0]
    width = part_ref.shape[2]
    barrier = pltpu.get_barrier_semaphore()
    peers = [{"dp": lax.rem(dp + s, wide)} for s in range(1, wide)]
    peers += [{"mp": lax.rem(mp + s, deep)} for s in range(1, deep)]
    for peer in peers:
        pl.semaphore_signal(barrier, inc=1, device_id=peer, device_id_type=MESH)
    pl.semaphore_wait(barrier, len(peers))
    first = []
    for s in range(1, wide):
        to = lax.rem(dp + s, wide)
        copy = pltpu.make_async_remote_copy(
            src_ref=part_ref.at[to], dst_ref=land_one.at[s - 1],
            send_sem=send_one.at[s - 1], recv_sem=recv_one.at[s - 1],
            device_id={"dp": to}, device_id_type=MESH,
        )
        copy.start()
        first.append(copy)
    total = part_ref[dp]
    for s, copy in enumerate(first):
        copy.wait_recv()
        total = total + land_one[s]
    for m in range(deep):
        mid_ref[m, 0:4] = total[4 * m : 4 * m + 4]
        mid_ref[m, 4:8] = jnp.zeros((4, width), F32)
    second = []
    for s in range(1, deep):
        to = lax.rem(mp + s, deep)
        copy = pltpu.make_async_remote_copy(
            src_ref=mid_ref.at[to], dst_ref=land_two.at[s - 1],
            send_sem=send_two.at[s - 1], recv_sem=recv_two.at[s - 1],
            device_id={"mp": to}, device_id_type=MESH,
        )
        copy.start()
        second.append(copy)
    window = mid_ref[mp]
    for s, copy in enumerate(second):
        copy.wait_recv()
        window = window + land_two[s]
    begin = width // 8 * lax.rem(dp * deep + mp, 8)
    turned = pltpu.roll(window, lax.rem(width - begin, width), 1)
    lane = lax.broadcasted_iota(jnp.int32, (8, width), 1)
    grad = jnp.where(lane < width - begin, turned, pltpu.roll(turned, 7, 0))
    updated = adam_step(grad, state_ref[0], state_ref[1], state_ref[2])
    for i, value in enumerate(updated):
        out_ref[i] = value
    for copy in first + second:
        copy.wait_send()


def adam_step(grad, prompt, moment_one, moment_two):
    first_new = 0.9 * moment_one + 0.1 * grad
    second_new = 0.999 * moment_two + 0.001 * grad * grad
    correct_one = 1.0 - 0.9**ADAM_STEP
    correct_two = 1.0 - 0.999**ADAM_STEP
    prompt_new = prompt - 0.3 * (first_new / correct_one) / (
        jnp.sqrt(second_new / correct_two) + 1e-08
    )
    return prompt_new, first_new, second_new


def adam_call(part, state, deep):
    wide, rows, width = part.shape
    return pl.pallas_call(
        adam_kernel,
        in_specs=[VMEM_SPEC] * 2,
        out_specs=VMEM_SPEC,
        out_shape=jax.ShapeDtypeStruct(state.shape, F32),
        scratch_shapes=[
            pltpu.VMEM((wide - 1, rows, width), F32),
            pltpu.VMEM((deep - 1, 8, width), F32),
            pltpu.VMEM((deep, 8, width), F32),
            pltpu.SemaphoreType.DMA((wide - 1,)),
            pltpu.SemaphoreType.DMA((wide - 1,)),
            pltpu.SemaphoreType.DMA((deep - 1,)),
            pltpu.SemaphoreType.DMA((deep - 1,)),
        ],
        compiler_params=pltpu.CompilerParams(collective_id=1, has_side_effects=True),
        name="sum_and_step",
    )(part, state)


def body(
    dp, mp, tokens, prompt, moment_one, moment_two, segments, live, out_grad, w_query, w_key,
    w_value, w_output, w_inner, w_outer, gain_attn, gain_ffn, rel_table,
):
    _, slots, width = tokens.shape
    tuned = (dp, mp) == (8, 4)
    share = prompt.shape[0]
    if tuned:
        line = 8 * width
        state = functools.reduce(
            jnp.add,
            [
                jnp.pad(part, (i * line, (3 - i) * line - share))
                for i, part in enumerate((prompt, moment_one, moment_two))
            ],
        ).reshape(3, 8, width)
        (
            w, trio, last, x, kv, q, ahead, behind, marks, query_side, key_side, gains, lo, hi,
        ) = open_call(
            state, gain_attn[None], gain_ffn[None], rel_table.T, w_query, w_key, w_value,
            w_output, w_inner, w_outer.T, segments, live, tokens[0], dp, mp,
        )
        swap = lambda bit: lax.ppermute(trio, "dp", [(i, i ^ bit) for i in range(dp)])
        from_east, from_south, from_sib = swap(2), swap(4), swap(1)
        lasted = lax.ppermute(last, "mp", [(1, 0), (2, 3)])
    else:
        (
            weights, x, kv, q, ahead, behind, marks, query_side, key_side, gains, lo, hi,
        ) = open_plain(
            tokens[0], prompt, segments[0], live[0], w_query, w_key, w_value, w_output, w_inner,
            w_outer, gain_attn, gain_ffn, rel_table,
        )
    ctx, lse = attend_call(lo, hi, query_side, key_side, kv, q, ahead)
    if tuned:
        layer_output, grad_hidden = feed_call(
            out_grad[0], query_side, gains, x, ctx, w, trio, from_east, from_south, from_sib,
            last, lasted,
        )
        w = w.reshape(mp, width, -1)
    else:
        w = weights[0]
        layer_output, grad_hidden = feed_local(
            x, out_grad[0], query_side, gains, ctx, w, weights[1], weights[2]
        )
    input_grad, prompt_part, layer_output = backward_call(
        lo, hi, grad_hidden, lse, query_side, key_side, marks, gains, kv, w, q, ctx, x, behind,
        layer_output,
    )
    if tuned:
        stepped = adam_call(prompt_part.reshape(dp, -1, width), state, mp)
        stepped = stepped.reshape(3, -1)[:, :share]
        prompt_new, first_new, second_new = stepped[0], stepped[1], stepped[2]
    else:
        grad = lax.psum_scatter(
            prompt_part[:PROMPT].reshape(-1), ("dp", "mp"), scatter_dimension=0, tiled=True
        )
        prompt_new, first_new, second_new = adam_step(grad, prompt, moment_one, moment_two)
    return (layer_output[None], input_grad[None], prompt_new, first_new, second_new)


def solution(mesh):
    both = ("dp", "mp")
    return jax.shard_map(
        functools.partial(body, mesh.shape["dp"], mesh.shape["mp"]),
        mesh=mesh,
        in_specs=(
            P(both, None, None),
            P(both),
            P(both),
            P(both),
            P(both, None),
            P(both, None),
            P(both, None, None),
            P("dp", "mp"),
            P("dp", "mp"),
            P("dp", "mp"),
            P("mp", "dp"),
            P("dp", "mp"),
            P("mp", "dp"),
            P("dp"),
            P("dp"),
            P(None, "mp"),
        ),
        out_specs=(
            P(both, None, None),
            P(both, None, None),
            P(both),
            P(both),
            P(both),
        ),
        check_vma=False,
    )
```

```python
import functools

import jax
import jax.numpy as jnp
from jax import lax
from jax.experimental import pallas as pl
from jax.experimental.pallas import tpu as pltpu
from jax.sharding import PartitionSpec as P

HEADS = 12
HEAD_DIM = 64
BUCKETS = 32
PROMPT = 100
ADAM_STEP = 10
BOUNDS = (1, 2, 3, 4, 5, 6, 7, 8, 12, 16, 23, 32, 46, 64, 91)
EPSILON = 1e-06
MASKED = -1e30
LOG2E = 1.4426950408889634
LN2 = 0.6931471805599453
GELU_C = 0.7978845608028654

BLK = 256
TILE = 128
GROUP = 12
ALIVE = 126
IS_PROMPT = 127
BF = jnp.bfloat16
F32 = jnp.float32
NN = (((1,), (0,)), ((), ()))
NT = (((1,), (1,)), ((), ()))
TN = (((0,), (0,)), ((), ()))
MESH = pl.DeviceIdType.MESH
VMEM_LIMIT = 62 * 1024 * 1024
SMEM_SPEC = pl.BlockSpec(memory_space=pltpu.SMEM)
VMEM_SPEC = pl.BlockSpec(memory_space=pltpu.VMEM)
ANY_SPEC = pl.BlockSpec(memory_space=pl.ANY)


def mm(left, right, dims):
    return lax.dot_general(left, right, dims, preferred_element_type=F32)


def bucket_of(offset, half):
    distance = jnp.abs(offset)
    counted = sum(((distance >= limit).astype(jnp.int32) for limit in BOUNDS))
    return counted + jnp.where(offset > 0, half, 0).astype(jnp.int32)


def span(block, size=BLK):
    return pl.ds(pl.multiple_of(block * size, size), size)


def low_lanes(width=TILE):
    return lax.rem(lax.broadcasted_iota(jnp.int32, (1, width), 1), TILE) < HEAD_DIM


def fill_bias(line_ref, tiles_ref):
    def one(head, carry):
        row = line_ref[pl.ds(head, 1), :]
        wide = pltpu.roll(
            jnp.broadcast_to(row, (TILE, 4 * TILE)), 0, 1, stride=1, stride_axis=0
        )
        for near in range(1, 4):
            tiles_ref[head, near] = wide[:, near * TILE : (near + 1) * TILE]
        tiles_ref[head, 0] = jnp.broadcast_to(row[:, 0:1], (TILE, TILE))
        tiles_ref[head, 4] = jnp.broadcast_to(row[:, 4 * TILE - 1 :], (TILE, TILE))
        return carry

    lax.fori_loop(0, HEADS, one, 0)


def rms_factor(values):
    return lax.rsqrt(jnp.mean(values * values, axis=-1, keepdims=True) + EPSILON)


def neighbours():
    dp = lax.axis_index("dp")
    core = lax.rem(dp, 2)
    across = lax.rem(lax.div(dp, 2), 2)
    down = lax.div(dp, 4)
    return (
        dp + 1 - 2 * core,
        dp + 2 - 4 * across,
        dp + 4 - 8 * down,
        dp + 6 - 4 * across - 8 * down,
    )


def line_order(z, j):
    upper = lax.div(z, 2)
    return (z, z + 1 - 2 * lax.rem(z, 2), 2 - upper, 3 - 3 * upper)[j]


def flat_shift(rows, shift, width):
    lane = lax.broadcasted_iota(jnp.int32, (8, width), 1)
    turned = pltpu.roll(rows, shift, 1)
    return jnp.where(lane >= shift, turned, pltpu.roll(turned, 1, 0))


def interleave(first, second):
    parts = []
    for at in range(0, first.shape[1], HEAD_DIM):
        parts += [first[:, at : at + HEAD_DIM], second[:, at : at + HEAD_DIM]]
    return jnp.concatenate(parts, axis=1)


def open_kernel(
    state_ref, ga_ref, gf_ref, table_ref, wq_ref, wk_ref, wv_ref, wo_ref, wi_ref, wu_ref,
    seg_ref, live_ref, tok_ref,
    w_out, trio_out, last_out, x_out, kv_out, q_out, ahead_out, behind_out,
    marks_ref, qa_ref, ka_ref, gains_ref, lo_ref, hi_ref,
    small_src, small_v, pack_src, w_v, ff_src, x_v, norm_v, kv_v, q_v, lines_v, ahead_v,
    behind_v,
    own_sem, z_send, z_recv, send, recv, line_send, line_recv, out_sem,
):
    mp = lax.axis_index("mp")
    dp = lax.axis_index("dp")
    depth, wide = w_v.shape[0], w_v.shape[1]
    width = tok_ref.shape[1]
    sib, east, south, corner = neighbours()
    up, down = mp + 1 < depth, mp > 0
    barrier = pltpu.get_barrier_semaphore()

    def greet(peer):
        pl.semaphore_signal(barrier, inc=1, device_id=peer, device_id_type=MESH)

    for peer in (sib, east, south):
        greet({"dp": peer})
    pl.when(up)(lambda: greet({"mp": mp + 1}))
    pl.when(down)(lambda: greet({"mp": mp - 1}))

    share = lax.rem(dp * depth + mp, 8)
    part = ga_ref.shape[1]
    empty = jnp.zeros((1, width - part), F32)
    gain_rows = [
        pltpu.roll(jnp.concatenate([ref[...].astype(F32), empty], axis=1), part * dp, 1)
        for ref in (ga_ref, gf_ref)
    ]
    table_rows = jnp.concatenate(
        [table_ref[...].astype(F32), jnp.zeros((HEADS // depth, width - BUCKETS), F32)], axis=1
    )
    small_src[...] = jnp.concatenate(
        [flat_shift(state_ref[0], part * share, width)]
        + gain_rows
        + [table_rows, jnp.zeros((6 - HEADS // depth, width), F32)],
        axis=0,
    ).astype(BF)
    pack_src[...] = jnp.concatenate(
        [interleave(wk_ref[...], wv_ref[...]), interleave(wq_ref[...], wo_ref[...].T)], axis=1
    )
    ff_src[0] = wi_ref[...]
    ff_src[1] = wu_ref[...]
    pl.semaphore_wait(barrier, 3 + up.astype(jnp.int32) + down.astype(jnp.int32))

    def remote(src, dst, send_sem, recv_sem, peer):
        return pltpu.make_async_remote_copy(
            src_ref=src, dst_ref=dst, send_sem=send_sem, recv_sem=recv_sem,
            device_id=peer, device_id_type=MESH,
        )

    started = []
    local = []
    units = [(small_src, small_v), (pack_src, w_v)]

    def along(u, j, src):
        dst = units[u][1]
        z = line_order(mp, j)
        copies = []
        for at, (ahead, there, move) in enumerate(((up, z <= mp, 1), (down, z >= mp, -1))):
            copy = remote(
                src, dst.at[z, dp], z_send.at[u, j, at], z_recv.at[u, z], {"mp": mp + move}
            )
            copies.append((jnp.logical_and(ahead, there), copy))
        return copies

    lined = []

    def launch(copies):
        for condition, copy in copies:
            pl.when(condition)(copy.start)
        lined.extend(copies)

    def push(u, o, kind, src, dst, peer):
        copy = remote(src, dst, send.at[u, o, kind], recv.at[u, o, kind], peer)
        copy.start()
        started.append(copy)

    def landed(u, o, kind, dst):
        remote(dst, dst, send.at[u, o, kind], recv.at[u, o, kind], {"dp": sib}).wait_recv()

    def step(u, o):
        src, dst = units[u]
        z = line_order(mp, o)
        block = dst.at[z, dp]
        if o:
            remote(block, block, z_send.at[u, o, 0], z_recv.at[u, z], {"dp": sib}).wait_recv()
            src = block
        launch(along(u, o, src))
        push(u, o, 0, src, block, {"dp": east})
        push(u, o, 1, src, block, {"dp": south})
        push(u, o, 2, src, block, {"dp": sib})

    def forward(u, o):
        dst = units[u][1]
        z = line_order(mp, o)
        rows = dst.shape[2] // 2 if u else dst.shape[2]
        landed(u, o, 0, dst.at[z, east])
        push(u, o, 3, dst.at[z, east, 0:rows], dst.at[z, east, 0:rows], {"dp": south})
        push(u, o, 4, dst.at[z, east], dst.at[z, east], {"dp": sib})
        landed(u, o, 1, dst.at[z, south])
        if u:
            push(u, o, 5, dst.at[z, south, rows:], dst.at[z, south, rows:], {"dp": east})
        push(u, o, 6, dst.at[z, south], dst.at[z, south], {"dp": sib})

    def finish(u, o):
        dst = units[u][1]
        z = line_order(mp, o)
        rows = dst.shape[2] // 2 if u else dst.shape[2]
        landed(u, o, 3, dst.at[z, corner, 0:rows])
        if u:
            landed(u, o, 5, dst.at[z, corner, rows:])
        push(u, o, 7, dst.at[z, corner], dst.at[z, corner], {"dp": sib})

    flip = 1 - 2 * lax.rem(dp, 2)

    def complete(u, o):
        dst = units[u][1]
        z = line_order(mp, o)
        landed(u, o, 2, dst.at[z, sib])
        landed(u, o, 4, dst.at[z, east + flip])
        landed(u, o, 6, dst.at[z, south + flip])
        landed(u, o, 7, dst.at[z, corner + flip])

    for u in range(2):
        step(u, 0)
        src, dst = units[u]
        copy = pltpu.make_async_copy(src, dst.at[mp, dp], own_sem.at[u])
        copy.start()
        local.append(copy)
    own_copy = pltpu.make_async_copy(ff_src, trio_out.at[0], own_sem.at[2])
    own_copy.start()
    partner = line_order(mp, 1)
    across = depth - 1 - mp
    inside = lax.rem(lax.div(mp + 1, 2), 2) == 1
    at_end = jnp.logical_not(inside)

    def line_copy(src, dst, at, at_recv, to):
        return remote(src, dst, line_send.at[at], line_recv.at[at_recv], {"mp": to})

    pair_copy = line_copy(ff_src, trio_out.at[1], 0, 0, partner)
    over_copy = line_copy(ff_src, trio_out.at[2], 1, 1, across)
    far_copy = line_copy(trio_out.at[1], last_out, 2, 2, across)
    back_copy = line_copy(trio_out.at[2], trio_out.at[2], 3, 1, partner)

    slots = tok_ref.shape[0]
    segment_row = seg_ref[...].astype(F32)
    live_row = live_ref[...].astype(F32)
    lane = lax.broadcasted_iota(jnp.int32, (slots, TILE), 1)
    lane_f = lane.astype(F32)
    segment = jnp.broadcast_to(segment_row, (TILE, slots)).T
    alive = jnp.broadcast_to(live_row, (TILE, slots)).T
    same = segment == lane_f
    start = jnp.sum((segment < lane_f).astype(F32), axis=0, keepdims=True)
    first = jnp.sum(jnp.where(same, start, 0.0), axis=1, keepdims=True)
    position = lax.broadcasted_iota(jnp.int32, (slots, 1), 0).astype(F32) - first
    prompt_slot = (alive > 0) & (position < PROMPT)
    sides = jnp.where(lane == ALIVE, alive, same.astype(F32))
    qa_ref[...] = jnp.where(lane == IS_PROMPT, prompt_slot.astype(F32), sides).astype(BF)
    ka_ref[...] = jnp.where(
        (lane < 16) & jnp.logical_not(same & (alive > 0)), MASKED, 0.0
    ).astype(BF)
    step(0, 1)
    forward(0, 0)
    step(0, 2)
    step(1, 1)
    forward(1, 0)
    forward(0, 1)
    finish(0, 0)
    step(0, 3)
    forward(0, 2)
    finish(0, 1)

    def window_rows(device, inside):
        target = 25 * lax.div(device, 8) + 3 * lax.rem(device, 8) + inside
        return jnp.where(inside < 4, target, -1).astype(F32)

    at = lax.broadcasted_iota(jnp.int32, (1, TILE), 1)
    target = window_rows(lax.div(at, 4), lax.rem(at, 4))
    marks_ref[...] = jnp.where((position == target) & prompt_slot, 1.0, 0.0).astype(BF)
    forward(0, 3)
    finish(0, 2)
    step(1, 2)
    forward(1, 1)
    finish(0, 3)
    finish(1, 0)
    block_lane = lax.broadcasted_iota(jnp.int32, (8, TILE), 1)
    lows = jnp.zeros((8, TILE), F32)
    highs = jnp.zeros((8, TILE), F32)
    for block in range(slots // TILE):
        here = segment_row[:, block * TILE : (block + 1) * TILE]
        lives = live_row[:, block * TILE : (block + 1) * TILE] > 0
        top = jnp.max(jnp.where(lives, here, -1.0), axis=1, keepdims=True)
        bottom = jnp.min(here, axis=1, keepdims=True)
        before = jnp.sum((segment_row < bottom).astype(F32), axis=1, keepdims=True)
        through = (segment_row <= top) & (live_row > 0)
        through = jnp.sum(through.astype(F32), axis=1, keepdims=True)
        lows = jnp.where(block_lane == block, before, lows)
        highs = jnp.where(block_lane == block, through, highs)
    highs = lax.div(highs.astype(jnp.int32) + TILE - 1, TILE)
    hi_ref[...] = highs
    lo_ref[...] = jnp.minimum(lax.div(lows.astype(jnp.int32), TILE), highs)
    for o in range(depth):
        complete(0, o)
    local[0].wait()

    gains = functools.reduce(jnp.add, [small_v[0, d].astype(F32) for d in range(wide)])
    gains_ref[...] = gains
    rows_all = depth * wide * 16
    at = lax.broadcasted_iota(jnp.int32, (1, rows_all), 1)
    holder = lax.div(at, 16)
    target = window_rows(
        lax.rem(holder, wide) * depth + lax.div(holder, wide), lax.rem(at, 16)
    )
    windows = small_v[...].reshape(rows_all, width)
    gain = gains[8:9]

    def embed(f):
        rows = slice(f, f + BLK)
        hot = (position[rows] == target).astype(F32).astype(BF)
        placed = mm(hot, windows, NN)
        value = jnp.where(prompt_slot[rows, 0:1], placed, tok_ref[rows, :].astype(F32))
        x_v[rows, :] = value
        norm_v[rows, :] = (value * rms_factor(value) * gain).astype(BF)

    for f in range(0, slots, BLK):
        embed(f)
        if f == slots // 2 - BLK:
            step(1, 3)
            pair_copy.start()
            pl.when(inside)(over_copy.start)
            forward(1, 2)
            finish(1, 1)
    copy = pltpu.make_async_copy(x_v, x_out, out_sem.at[0])
    copy.start()
    local.append(copy)

    half = w_v.shape[3] // 2
    low = low_lanes(half)

    def project(o):
        complete(1, o)
        if o == 0:
            local[1].wait()
        z = line_order(mp, o)
        copy = pltpu.make_async_copy(w_v.at[z], w_out.at[z], out_sem.at[1 + o])
        copy.start()
        local.append(copy)
        weight = w_v[z].reshape(wide * w_v.shape[2], 2 * half)
        cols = span(z, half)
        parts = [mm(norm_v[f : f + BLK, :], weight, NN) for f in range(0, slots, BLK)]
        for i, piece in enumerate(parts):
            rows = slice(i * BLK, (i + 1) * BLK)
            kv_v[rows, cols] = piece[:, :half].astype(BF)
            q_v[rows, cols] = jnp.where(low, piece[:, half:] * LOG2E, 0.0).astype(BF)
        for at_sem, (src, dst) in enumerate(((kv_v, kv_out), (q_v, q_out))):
            copy = pltpu.make_async_copy(
                src.at[:, cols], dst.at[:, cols], out_sem.at[1 + depth + 2 * o + at_sem]
            )
            copy.start()
            local.append(copy)

    table = jnp.concatenate(
        [small_v[m, 0].astype(F32)[10 : 10 + HEADS // depth, 0:TILE] for m in range(depth)]
        + [jnp.zeros((16 - HEADS, TILE), F32)],
        axis=0,
    ).astype(BF)
    offset = lax.broadcasted_iota(jnp.int32, (1, 4 * TILE), 1) - 2 * TILE
    code = lax.broadcasted_iota(jnp.int32, (TILE, 4 * TILE), 0)
    def bias_out(at_sem, sign, tiles, out):
        hot = (code == bucket_of(sign * offset, BUCKETS // 2)).astype(F32).astype(BF)
        lines_v[...] = mm(table, hot, NN) * LOG2E
        fill_bias(lines_v, tiles)
        copy = pltpu.make_async_copy(tiles, out, out_sem.at[1 + 3 * depth + at_sem])
        copy.start()
        local.append(copy)

    bias_out(0, 1, ahead_v, ahead_out)
    forward(1, 3)
    finish(1, 2)
    @pl.when(inside)
    def _():
        pair_copy.wait_recv()
        far_copy.start()
        over_copy.wait_recv()
        back_copy.start()

    project(0)
    finish(1, 3)
    project(1)
    project(2)
    bias_out(1, -1, behind_v, behind_out)
    project(3)
    own_copy.wait()
    pair_copy.wait_send()

    @pl.when(at_end)
    def _():
        pair_copy.wait_recv()
        back_copy.wait_recv()

    @pl.when(inside)
    def _():
        over_copy.wait_send()
        far_copy.wait()
        back_copy.wait_send()

    for copy in local[2:]:
        copy.wait()
    for copy in started:
        copy.wait_send()
    for condition, copy in lined:
        pl.when(condition)(copy.wait_send)


def open_call(state, ga, gf, table, wq, wk, wv, wo, wi, wu, seg, live, tok, dp, mp):
    slots, width = tok.shape
    rows = wi.shape[0]
    wide = HEADS * TILE
    pack = (rows, width)
    shape = jax.ShapeDtypeStruct
    dma = pltpu.SemaphoreType.DMA
    tiles = (HEADS, 5, TILE, TILE)
    return pl.pallas_call(
        open_kernel,
        in_specs=[VMEM_SPEC] * 13,
        out_specs=[ANY_SPEC] * 8 + [VMEM_SPEC] * 6,
        out_shape=[
            shape((mp, dp) + pack, BF),
            shape((3, 2) + pack, BF),
            shape((2,) + pack, BF),
            shape((slots, width), F32),
            shape((slots, wide), BF),
            shape((slots, wide), BF),
            shape(tiles, F32),
            shape(tiles, F32),
            shape((slots, TILE), BF),
            shape((slots, TILE), BF),
            shape((slots, TILE), BF),
            shape((16, width), F32),
            shape((8, TILE), jnp.int32),
            shape((8, TILE), jnp.int32),
        ],
        scratch_shapes=[
            pltpu.VMEM((16, width), BF),
            pltpu.VMEM((mp, dp, 16, width), BF),
            pltpu.VMEM(pack, BF),
            pltpu.VMEM((mp, dp) + pack, BF),
            pltpu.VMEM((2,) + pack, BF),
            pltpu.VMEM((slots, width), F32),
            pltpu.VMEM((slots, width), BF),
            pltpu.VMEM((slots, wide), BF),
            pltpu.VMEM((slots, wide), BF),
            pltpu.VMEM((16, 4 * TILE), F32),
            pltpu.VMEM(tiles, F32),
            pltpu.VMEM(tiles, F32),
            dma((3,)),
            dma((2, mp, 2)),
            dma((2, mp)),
            dma((2, mp, 8)),
            dma((2, mp, 8)),
            dma((4,)),
            dma((3,)),
            dma((3 + 3 * mp,)),
        ],
        compiler_params=pltpu.CompilerParams(
            collective_id=0, has_side_effects=True, vmem_limit_bytes=VMEM_LIMIT
        ),
        cost_estimate=pl.CostEstimate(
            flops=16 * 10**9, bytes_accessed=40 * 10**6, transcendentals=0
        ),
        name="open_layer",
    )(state, ga, gf, table, wq, wk, wv, wo, wi, wu, seg, live, tok)


def window_of(lo_ref, hi_ref, block, blocks):
    lo = lo_ref[0, block]
    pairs = lax.div(hi_ref[0, block] - lo + 1, 2)
    return jnp.minimum(lo, blocks - 2 * pairs), pairs


def bias_row(tiles_ref, head, first, block, pairs):
    return jnp.concatenate(
        [
            tiles_ref[head, jnp.clip(first + j - block, -2, 2) + 2]
            for j in range(2 * pairs)
        ],
        axis=1,
    )


def attend_kernel(
    lo_ref, hi_ref, qa_ref, ka_ref, kv_hbm, q_hbm, tiles_hbm,
    ctx_out, lse_ref,
    kv_ref, val_ref, q_ref, ctx_ref, tiles_ref, lsem_ref, mean_ref, sems, ctx_sems,
):
    slots = qa_ref.shape[0]
    blocks = slots // TILE
    copies = [
        pltpu.make_async_copy(src, dst, sems.at[i])
        for i, (src, dst) in enumerate(
            ((kv_hbm, kv_ref), (q_hbm, q_ref), (tiles_hbm, tiles_ref))
        )
    ]
    for copy in copies:
        copy.start()
    copies[0].wait()
    mean_ref[...] = mm(jnp.full((8, slots), 1.0 / slots, BF), kv_ref[...], NN)
    high = jnp.logical_not(low_lanes())
    ones = jnp.ones((slots, TILE), BF)
    for h in range(HEADS):
        cols = slice(h * TILE, (h + 1) * TILE)
        val_ref[:, cols] = jnp.where(high, kv_ref[:, cols], ones)
    lane = lax.broadcasted_iota(jnp.int32, (1, TILE), 1)
    copies[1].wait()
    copies[2].wait()

    def query_block(qb, carry):
        qs = span(qb, TILE)
        first, count = window_of(lo_ref, hi_ref, qb, blocks)
        alive = qa_ref[qs, ALIVE : ALIVE + 1].astype(F32) > 0
        lsem_ref[...] = jnp.zeros_like(lsem_ref)

        def attend(pairs):
            size = 2 * pairs * TILE
            ks = pl.ds(pl.multiple_of(first * TILE, TILE), size)
            mask = mm(qa_ref[qs, :], ka_ref[ks, :], NT)

            def group_body(g, inner):
                heads = [g * GROUP + i for i in range(GROUP)]
                cols = [span(h, TILE) for h in heads]
                scores = [
                    mm(q_ref[qs, c], kv_ref[ks, c], NT)
                    + (bias_row(tiles_ref, h, first, qb, pairs) + mask)
                    for h, c in zip(heads, cols)
                ]
                tops = [jnp.max(row, axis=1, keepdims=True) for row in scores]
                weights = [jnp.exp2(row - top).astype(BF) for row, top in zip(scores, tops)]
                for h, c, top, weight in zip(heads, cols, tops, weights):
                    both = mm(weight, val_ref[ks, c], NN)
                    context = both / pltpu.roll(both, HEAD_DIM, 1)
                    context = jnp.where(alive, context, mean_ref[0:1, c])
                    ctx_ref[qs, c] = jnp.where(high, context, 0.0).astype(BF)
                    lsem_ref[...] = jnp.where(
                        (lane == h) & alive, top + jnp.log2(both), lsem_ref[...]
                    )
                return inner

            lax.fori_loop(0, HEADS // GROUP, group_body, 0)

        for pairs in range(1, blocks // 2 + 1):
            pl.when(count == pairs)(functools.partial(attend, pairs))

        @pl.when(count == 0)
        def _():
            every = jnp.logical_not(low_lanes(HEADS * TILE))
            ctx_ref[qs, :] = jnp.broadcast_to(
                jnp.where(every, mean_ref[0:1, :], 0.0), (TILE, HEADS * TILE)
            ).astype(BF)

        lse_ref[:, qs] = lsem_ref[...].T[0:16]
        pltpu.make_async_copy(ctx_ref.at[qs], ctx_out.at[qs], ctx_sems.at[qb]).start()
        return carry

    lax.fori_loop(0, blocks, query_block, 0)
    for b in range(blocks):
        rows = slice(b * TILE, (b + 1) * TILE)
        pltpu.make_async_copy(ctx_ref.at[rows], ctx_out.at[rows], ctx_sems.at[b]).wait()


def attend_call(lo, hi, qa, ka, kv, q, tiles):
    slots, wide = kv.shape
    return pl.pallas_call(
        attend_kernel,
        in_specs=[SMEM_SPEC] * 2 + [VMEM_SPEC] * 2 + [ANY_SPEC] * 3,
        out_specs=[ANY_SPEC, VMEM_SPEC],
        out_shape=[
            jax.ShapeDtypeStruct((slots, wide), BF),
            jax.ShapeDtypeStruct((16, slots), F32),
        ],
        scratch_shapes=[
            pltpu.VMEM((slots, wide), BF),
            pltpu.VMEM((slots, wide), BF),
            pltpu.VMEM((slots, wide), BF),
            pltpu.VMEM((slots, wide), BF),
            pltpu.VMEM(tiles.shape, F32),
            pltpu.VMEM((TILE, TILE), F32),
            pltpu.VMEM((8, wide), F32),
            pltpu.SemaphoreType.DMA((3,)),
            pltpu.SemaphoreType.DMA((slots // TILE,)),
        ],
        compiler_params=pltpu.CompilerParams(vmem_limit_bytes=VMEM_LIMIT),
        cost_estimate=pl.CostEstimate(
            flops=25 * 10**9, bytes_accessed=10**7, transcendentals=10**7
        ),
        name="attend",
    )(lo, hi, qa, ka, kv, q, tiles)


def gelu_both(inner, upstream):
    square = inner * inner
    bent = jnp.tanh(inner * (GELU_C + (GELU_C * 0.044715) * square))
    half = 0.5 + 0.5 * bent
    activated = inner * half
    slope = half + activated * ((1.0 - half) * (2 * GELU_C + (6 * GELU_C * 0.044715) * square))
    return activated.astype(BF), (upstream * slope).astype(BF)


def feed_kernel(
    og_ref, qa_ref, gains_ref, x_hbm, ctx_hbm, w_hbm, trio_hbm, east_hbm, south_hbm, sib_hbm,
    last_hbm, lasted_hbm,
    out_hbm, gh_hbm,
    ff_v, ctx_ref, w_ref, x_ref, norm_ref, gb_ref, hid_ref, br_ref, dn_ref, out_ref, gh_ref,
    sems, fill, send, recv, out_sem,
):
    dp = lax.axis_index("dp")
    mp = lax.axis_index("mp")
    depth, wide = ff_v.shape[0], ff_v.shape[1]
    half = w_hbm.shape[3] // 2
    rows_half = ff_v.shape[3] // 2
    sib, east, south, corner = neighbours()
    flip = 1 - 2 * lax.rem(dp, 2)
    upper, lower = pl.ds(0, rows_half), pl.ds(rows_half, rows_half)
    inside = lax.rem(lax.div(mp + 1, 2), 2) == 1
    barrier = pltpu.get_barrier_semaphore()
    for peer in (sib, east, south):
        pl.semaphore_signal(barrier, inc=1, device_id={"dp": peer}, device_id_type=MESH)
    first = [
        pltpu.make_async_copy(ctx_hbm, ctx_ref, sems.at[0]),
        pltpu.make_async_copy(x_hbm, x_ref, sems.at[1]),
    ]
    for m in range(depth):
        first.append(
            pltpu.make_async_copy(
                w_hbm.at[m, :, :, half:],
                w_ref.at[:, :, m * half : (m + 1) * half],
                sems.at[2 + m],
            )
        )
    end = depth - 1
    for here, source in ((inside, last_hbm), (jnp.logical_not(inside), lasted_hbm)):
        pl.when(here)(pltpu.make_async_copy(source, ff_v.at[end, dp], fill.at[end, 0]).start)
    for copy in first:
        copy.start()
    pl.semaphore_wait(barrier, 3)

    def remote(src, dst, j, kind, peer):
        return pltpu.make_async_remote_copy(
            src_ref=src, dst_ref=dst, send_sem=send.at[j, kind], recv_sem=recv.at[j, kind],
            device_id={"dp": peer}, device_id_type=MESH,
        )

    sent = []

    def push(src, dst, j, kind, peer):
        copy = remote(src, dst, j, kind, peer)
        copy.start()
        sent.append(copy)

    def awaited(block, j, kind):
        remote(block, block, j, kind, sib).wait_recv()

    def relay(j, from_east, from_south):
        push(from_east.at[:, upper], ff_v.at[j, east, :, upper], j, 0, south)
        push(from_south.at[:, lower], ff_v.at[j, south, :, lower], j, 1, east)
        push(from_east, ff_v.at[j, east], j, 2, sib)
        push(from_south, ff_v.at[j, south], j, 3, sib)

    for j in range(end):
        relay(j, east_hbm.at[j], south_hbm.at[j])
        for kind, (src, place) in enumerate(
            ((trio_hbm, dp), (east_hbm, east), (south_hbm, south), (sib_hbm, sib))
        ):
            pltpu.make_async_copy(src.at[j], ff_v.at[j, place], fill.at[j, kind]).start()

    def spread(j):
        block = ff_v.at[j, dp]
        pltpu.make_async_copy(block, block, fill.at[j, 0]).wait()
        for kind, peer in ((5, east), (6, south), (7, sib)):
            push(block, block, j, kind, peer)

    spread(end)

    def pass_on(j):
        awaited(ff_v.at[j, east], j, 5)
        awaited(ff_v.at[j, south], j, 6)
        relay(j, ff_v.at[j, east], ff_v.at[j, south])

    def corners(j):
        block = ff_v.at[j, corner]
        awaited(ff_v.at[j, corner, :, upper], j, 0)
        awaited(ff_v.at[j, corner, :, lower], j, 1)
        push(block, block, j, 4, sib)

    def landed(j):
        for kind, place in ((2, east + flip), (3, south + flip), (4, corner + flip)):
            awaited(ff_v.at[j, place], j, kind)
        if j < end:
            for kind, place in enumerate((dp, east, south, sib)):
                block = ff_v.at[j, place]
                pltpu.make_async_copy(block, block, fill.at[j, kind]).wait()
        else:
            awaited(ff_v.at[j, sib], j, 7)

    slots = og_ref.shape[0]
    gain = gains_ref[9:10]
    blocks = [slice(f, f + BLK) for f in range(0, slots, BLK)]
    for rows in blocks:
        gb_ref[rows, :] = (
            og_ref[rows, :].astype(F32) * qa_ref[rows, ALIVE : ALIVE + 1].astype(F32)
        ).astype(BF)
    for copy in first:
        copy.wait()
    weight = w_ref[...].reshape(-1, depth * half)
    for i, rows in enumerate(blocks):
        hid_ref[rows, :] = x_ref[rows, :] + mm(ctx_ref[rows, :], weight, NT)
        if i == len(blocks) // 2 - 1:
            corners(0)
    corners(1)
    for rows in blocks:
        hidden = hid_ref[rows, :]
        norm_ref[rows, :] = (hidden * rms_factor(hidden) * gain).astype(BF)

    def unit_block(j, chosen):
        wi = ff_v[j, :, 0].reshape(-1, ff_v.shape[4])
        wo = ff_v[j, :, 1].reshape(-1, ff_v.shape[4])
        inner = [mm(norm_ref[rows, :], wi, NN) for rows in chosen]
        upstream = [mm(gb_ref[rows, :], wo, NN) for rows in chosen]
        pairs = [gelu_both(a, b) for a, b in zip(inner, upstream)]
        results = []
        for rows, (activated, grad_inner) in zip(chosen, pairs):
            branch, back = mm(activated, wo, NT), mm(grad_inner, wi, NT)
            if j:
                branch, back = br_ref[rows, :] + branch, dn_ref[rows, :] + back
            if j < end:
                br_ref[rows, :], dn_ref[rows, :] = branch, back
            results.append((branch, back))
        return results

    landed(0)
    unit_block(0, blocks)
    corners(2)
    pass_on(3)
    landed(1)
    unit_block(1, blocks)
    corners(3)
    landed(2)
    unit_block(2, blocks)
    landed(3)
    outs = []
    for i, (rows, (branch, back)) in enumerate(zip(blocks, unit_block(end, blocks))):
        hidden = hid_ref[rows, :]
        alive = qa_ref[rows, ALIVE : ALIVE + 1].astype(F32)
        out_ref[rows, :] = (alive * (hidden + branch)).astype(BF)
        factor = rms_factor(hidden)
        weighted = back * gain
        gh_ref[rows, :] = og_ref[rows, :].astype(F32) * alive + (
            factor * weighted
            - hidden
            * (factor * factor * factor)
            * jnp.mean(weighted * hidden, axis=-1, keepdims=True)
        )
        for at, (src, dst) in enumerate(((out_ref, out_hbm), (gh_ref, gh_hbm))):
            copy = pltpu.make_async_copy(src.at[rows], dst.at[rows], out_sem.at[2 * i + at])
            copy.start()
            outs.append(copy)
    for copy in outs:
        copy.wait()
    for copy in sent:
        copy.wait_send()


def feed_call(
    og, qa, gains, x, ctx, w, trio, from_east, from_south, from_sib, last, lasted
):
    slots, width = x.shape
    depth, wide, rows, units = w.shape
    dma = pltpu.SemaphoreType.DMA
    return pl.pallas_call(
        feed_kernel,
        in_specs=[VMEM_SPEC] * 3 + [ANY_SPEC] * 9,
        out_specs=[ANY_SPEC] * 2,
        out_shape=[
            jax.ShapeDtypeStruct((slots, width), BF),
            jax.ShapeDtypeStruct((slots, width), F32),
        ],
        scratch_shapes=[
            pltpu.VMEM((depth, wide) + trio.shape[1:], BF),
            pltpu.VMEM(ctx.shape, BF),
            pltpu.VMEM((wide, rows, depth * units // 2), BF),
            pltpu.VMEM((slots, width), F32),
            pltpu.VMEM((slots, width), BF),
            pltpu.VMEM((slots, width), BF),
            pltpu.VMEM((slots, width), F32),
            pltpu.VMEM((slots, width), F32),
            pltpu.VMEM((slots, width), F32),
            pltpu.VMEM((slots, width), BF),
            pltpu.VMEM((slots, width), F32),
            dma((2 + depth,)),
            dma((depth, 4)),
            dma((depth, 8)),
            dma((depth, 8)),
            dma((2 * (slots // BLK),)),
        ],
        compiler_params=pltpu.CompilerParams(
            collective_id=2, has_side_effects=True, vmem_limit_bytes=VMEM_LIMIT
        ),
        name="feed_forward",
    )(og, qa, gains, x, ctx, w, trio, from_east, from_south, from_sib, last, lasted)


def feed_local_kernel(
    x_ref, og_ref, qa_ref, gain_ref, ctx_hbm, w_hbm, wi_hbm, wo_hbm,
    out_ref, gh_ref,
    ctx_ref, w_ref, wi_ref, wo_ref, norm_ref, gb_ref, hid_ref, br_ref, dn_ref, sems,
):
    slots = x_ref.shape[0]
    groups = w_hbm.shape[0]
    half = w_hbm.shape[2] // 2
    first = [pltpu.make_async_copy(ctx_hbm, ctx_ref, sems.at[0])]
    for m in range(groups):
        first.append(
            pltpu.make_async_copy(w_hbm.at[m, :, half:], w_ref.at[m], sems.at[1 + m])
        )
    later = []
    for m in range(groups):
        later.append(
            (
                pltpu.make_async_copy(wi_hbm.at[m], wi_ref.at[m], sems.at[1 + groups + 2 * m]),
                pltpu.make_async_copy(wo_hbm.at[m], wo_ref.at[m], sems.at[2 + groups + 2 * m]),
            )
        )
    for copy in first:
        copy.start()
    for pair in later:
        pair[0].start()
        pair[1].start()
    for copy in first:
        copy.wait()
    gain = gain_ref[9:10]
    blocks = [slice(f, f + BLK) for f in range(0, slots, BLK)]
    for rows in blocks:
        hid_ref[rows, :] = x_ref[rows, :]
    for m in range(groups):
        cols = slice(m * half, (m + 1) * half)
        for rows in blocks:
            hid_ref[rows, :] += mm(ctx_ref[rows, cols], w_ref[m], NT)
    for rows in blocks:
        hidden = hid_ref[rows, :]
        norm_ref[rows, :] = (hidden * rms_factor(hidden) * gain).astype(BF)
        gb_ref[rows, :] = (
            og_ref[rows, :].astype(F32) * qa_ref[rows, ALIVE : ALIVE + 1].astype(F32)
        ).astype(BF)
    br_ref[...] = jnp.zeros_like(br_ref)
    dn_ref[...] = jnp.zeros_like(dn_ref)
    for m in range(groups):
        later[m][0].wait()
        later[m][1].wait()
    def unit_block(m, carry):
        inner = [mm(norm_ref[rows, :], wi_ref[m], NN) for rows in blocks]
        upstream = [mm(gb_ref[rows, :], wo_ref[m], NN) for rows in blocks]
        pairs = [gelu_both(a, b) for a, b in zip(inner, upstream)]
        for rows, (activated, grad_inner) in zip(blocks, pairs):
            br_ref[rows, :] += mm(activated, wo_ref[m], NT)
            dn_ref[rows, :] += mm(grad_inner, wi_ref[m], NT)
        return carry

    lax.fori_loop(0, groups, unit_block, 0)
    for rows in blocks:
        hidden = hid_ref[rows, :]
        alive = qa_ref[rows, ALIVE : ALIVE + 1].astype(F32)
        out_ref[rows, :] = (alive * (hidden + br_ref[rows, :])).astype(BF)
        factor = rms_factor(hidden)
        weighted = dn_ref[rows, :] * gain
        gh_ref[rows, :] = og_ref[rows, :].astype(F32) * alive + (
            factor * weighted
            - hidden
            * (factor * factor * factor)
            * jnp.mean(weighted * hidden, axis=-1, keepdims=True)
        )


def feed_local(x, og, qa, gain, ctx, w, wi, wo):
    slots, width = x.shape
    groups = w.shape[0]
    return pl.pallas_call(
        feed_local_kernel,
        in_specs=[VMEM_SPEC] * 4 + [ANY_SPEC] * 4,
        out_specs=[VMEM_SPEC] * 2,
        out_shape=[
            jax.ShapeDtypeStruct((slots, width), BF),
            jax.ShapeDtypeStruct((slots, width), F32),
        ],
        scratch_shapes=[
            pltpu.VMEM(ctx.shape, BF),
            pltpu.VMEM((groups, w.shape[1], w.shape[2] // 2), BF),
            pltpu.VMEM(wi.shape, BF),
            pltpu.VMEM(wo.shape, BF),
            pltpu.VMEM((slots, width), BF),
            pltpu.VMEM((slots, width), BF),
            pltpu.VMEM((slots, width), F32),
            pltpu.VMEM((slots, width), F32),
            pltpu.VMEM((slots, width), F32),
            pltpu.SemaphoreType.DMA((1 + 3 * groups,)),
        ],
        compiler_params=pltpu.CompilerParams(vmem_limit_bytes=VMEM_LIMIT),
        name="feed_forward_local",
    )(x, og, qa, gain, ctx, w, wi, wo)


def backward_kernel(
    lo_ref, hi_ref, gh_ref, lse_ref, qa_ref, ka_ref, marks_ref, gains_ref, kv_hbm, w_hbm, q_hbm,
    ctx_hbm, x_hbm, tiles_hbm, layer_hbm,
    ig_out, pg_ref, layer_out,
    kv_ref, w_ref, q_ref, ctx_ref, x_ref, tiles_ref, layer_ref, all_ref, kt_ref, dsum_ref,
    dqt_ref, ig_ref, sems, out_sem,
):
    slots = gh_ref.shape[0]
    count_blocks = slots // TILE
    groups = w_hbm.shape[0]
    half = w_hbm.shape[2] // 2
    wide = HEADS * TILE
    weights = [
        pltpu.make_async_copy(
            w_hbm.at[m, :, side * half : (side + 1) * half],
            w_ref.at[:, side * wide + m * half : side * wide + (m + 1) * half],
            sems.at[6 + side * groups + m],
        )
        for side in (1, 0)
        for m in range(groups)
    ]
    q_copy, ctx_copy, kv_copy, tiles_copy, x_copy, layer_copy = [
        pltpu.make_async_copy(src, dst, sems.at[i])
        for i, (src, dst) in enumerate(
            (
                (q_hbm, q_ref),
                (ctx_hbm, ctx_ref),
                (kv_hbm, kv_ref),
                (tiles_hbm, tiles_ref),
                (x_hbm, x_ref),
                (layer_hbm, layer_ref),
            )
        )
    ]
    for copy in [q_copy] + weights + [ctx_copy, kv_copy, tiles_copy, x_copy, layer_copy]:
        copy.start()
    dqt_ref[...] = jnp.zeros_like(dqt_ref)
    blocks = [slice(f, f + BLK) for f in range(0, slots, BLK)]
    q_copy.wait()
    grads_low = [gh_ref[rows, :].astype(BF) for rows in blocks]
    for copy in weights[:groups]:
        copy.wait()
    low_wide = low_lanes(wide)
    parts = [mm(grad, w_ref[:, wide:], NN) for grad in grads_low]
    for rows, part in zip(blocks, parts):
        q_ref[rows, :] = jnp.where(low_wide, q_ref[rows, :], part.astype(BF))
    ctx_copy.wait()
    pick = (
        lax.broadcasted_iota(jnp.int32, (wide, TILE), 0) // TILE
        == lax.broadcasted_iota(jnp.int32, (wide, TILE), 1)
    ).astype(F32).astype(BF)
    sums = []
    for rows in blocks:
        product = q_ref[rows, :].astype(F32) * ctx_ref[rows, :].astype(F32)
        upper = product.astype(BF)
        lower = (product - upper.astype(F32)).astype(BF)
        sums.append(mm(upper, pick, NN) + mm(lower, pick, NN))
    for rows, value in zip(blocks, sums):
        dsum_ref[:, rows] = value.T[0:16]
    kv_copy.wait()
    for h in range(HEADS):
        kt_ref[h] = kv_ref[:, h * TILE : (h + 1) * TILE].T[0:HEAD_DIM]
    tiles_copy.wait()
    low = low_lanes()

    def key_block(kb, carry):
        ks = span(kb, TILE)
        first, count = window_of(lo_ref, hi_ref, kb, count_blocks)

        def attend(pairs):
            size = 2 * pairs * TILE
            qs = pl.ds(pl.multiple_of(first * TILE, TILE), size)
            mask = mm(ka_ref[ks, :], qa_ref[qs, :], NT)

            def group_body(g, inner):
                heads = [g * GROUP + i for i in range(GROUP)]
                cols = [span(h, TILE) for h in heads]
                zero = jnp.zeros((TILE, TILE), BF)
                keys = [kv_ref[ks, c] for c in cols]
                raw = [
                    mm(
                        jnp.concatenate(
                            [jnp.where(low, key, zero), jnp.where(low, zero, key)], axis=0
                        ),
                        q_ref[qs, c],
                        NT,
                    )
                    for key, c in zip(keys, cols)
                ]
                probs = [
                    jnp.exp2(
                        both[:TILE]
                        + (bias_row(tiles_ref, h, first, kb, pairs) + mask)
                        - lse_ref[pl.ds(h, 1), qs]
                    )
                    for h, both in zip(heads, raw)
                ]
                outs = [
                    (p * (both[TILE:] - dsum_ref[pl.ds(h, 1), qs])).astype(BF)
                    for h, p, both in zip(heads, probs, raw)
                ]
                sides = [
                    jnp.concatenate([out, p.astype(BF)], axis=0) for out, p in zip(outs, probs)
                ]
                for h, c, out, side in zip(heads, cols, outs, sides):
                    both = mm(side, q_ref[qs, c], NN)
                    all_ref[ks, c] = jnp.where(
                        low, both[:TILE] * LN2, both[TILE:]
                    ).astype(BF)
                    dqt_ref[h, :, qs] += mm(kt_ref[h, :, ks], out, NN)
                return inner

            lax.fori_loop(0, HEADS // GROUP, group_body, 0)

        for pairs in range(1, count_blocks // 2 + 1):
            pl.when(count == pairs)(functools.partial(attend, pairs))

        @pl.when(count == 0)
        def _():
            all_ref[ks, :] = jnp.zeros((TILE, all_ref.shape[1]), BF)

        return carry

    lax.fori_loop(0, count_blocks, key_block, 0)
    rest = jnp.zeros((TILE - HEAD_DIM, slots), BF)
    for h in range(HEADS):
        place = wide + h * TILE
        all_ref[:, place : place + TILE] = jnp.concatenate(
            [dqt_ref[h].astype(BF), rest], axis=0
        ).T
    x_copy.wait()
    layer_copy.wait()
    layer_copy = pltpu.make_async_copy(layer_ref, layer_out, sems.at[5])
    layer_copy.start()
    gain = gains_ref[8:9]
    for copy in weights[groups:]:
        copy.wait()
    backs = [mm(all_ref[rows, :], w_ref[...], NT) for rows in blocks]
    outs = []
    total = None
    for i, (rows, back) in enumerate(zip(blocks, backs)):
        value = x_ref[rows, :]
        factor = rms_factor(value)
        weighted = back * gain
        grad = gh_ref[rows, :] + (
            factor * weighted
            - value
            * (factor * factor * factor)
            * jnp.mean(weighted * value, axis=-1, keepdims=True)
        )
        ig_ref[rows, :] = jnp.where(
            qa_ref[rows, IS_PROMPT : IS_PROMPT + 1].astype(F32) > 0, 0.0, grad
        )
        copy = pltpu.make_async_copy(ig_ref.at[rows], ig_out.at[rows], out_sem.at[i])
        copy.start()
        outs.append(copy)
        upper = grad.astype(BF)
        lower = (grad - upper.astype(F32)).astype(BF)
        hot = marks_ref[rows, :]
        part = mm(hot, upper, TN) + mm(hot, lower, TN)
        total = part if total is None else total + part
    pg_ref[...] = total
    layer_copy.wait()
    for copy in outs:
        copy.wait()


def backward_call(
    lo, hi, gh, lse, qa, ka, marks, gains, kv, w, q, ctx, x, tiles, layer_output
):
    slots, width = gh.shape
    groups = w.shape[0]
    return pl.pallas_call(
        backward_kernel,
        in_specs=[SMEM_SPEC] * 2 + [VMEM_SPEC] * 6 + [ANY_SPEC] * 7,
        out_specs=[ANY_SPEC, VMEM_SPEC, ANY_SPEC],
        out_shape=[
            jax.ShapeDtypeStruct((slots, width), F32),
            jax.ShapeDtypeStruct((TILE, width), F32),
            jax.ShapeDtypeStruct((slots, width), BF),
        ],
        scratch_shapes=[
            pltpu.VMEM(kv.shape, BF),
            pltpu.VMEM((w.shape[1], groups * w.shape[2]), BF),
            pltpu.VMEM(q.shape, BF),
            pltpu.VMEM(ctx.shape, BF),
            pltpu.VMEM(x.shape, F32),
            pltpu.VMEM(tiles.shape, F32),
            pltpu.VMEM(layer_output.shape, BF),
            pltpu.VMEM((slots, 2 * HEADS * TILE), BF),
            pltpu.VMEM((HEADS, HEAD_DIM, slots), BF),
            pltpu.VMEM((16, slots), F32),
            pltpu.VMEM((HEADS, HEAD_DIM, slots), F32),
            pltpu.VMEM((slots, width), F32),
            pltpu.SemaphoreType.DMA((2 * groups + 6,)),
            pltpu.SemaphoreType.DMA((slots // BLK,)),
        ],
        compiler_params=pltpu.CompilerParams(vmem_limit_bytes=VMEM_LIMIT),
        name="attend_back",
    )(lo, hi, gh, lse, qa, ka, marks, gains, kv, w, q, ctx, x, tiles, layer_output)


def slot_arrays(segments, live):
    slots = segments.shape[0]
    place = jnp.arange(slots, dtype=jnp.int32)
    first = jnp.sum((segments[None, :] < segments[:, None]).astype(jnp.int32), axis=1)
    position = place - first
    alive = live[:, None] == 1
    is_prompt = alive & (position < PROMPT)[:, None]
    lane = jnp.arange(TILE, dtype=jnp.int32)[None, :]
    marks = ((position[:, None] == lane) & is_prompt).astype(BF)
    same = segments[:, None] == lane
    query_side = jnp.where(lane == ALIVE, alive, same)
    query_side = jnp.where(lane == IS_PROMPT, is_prompt, query_side).astype(BF)
    key_side = jnp.where((lane < 16) & jnp.logical_not(same & alive), MASKED, 0.0).astype(BF)
    by_block = segments.reshape(-1, TILE)
    top = jnp.max(jnp.where(live.reshape(-1, TILE) == 1, by_block, -1), axis=1)
    hi = jnp.sum((segments[None, :] <= top[:, None]) & (live[None, :] == 1), axis=1)
    hi = (hi.astype(jnp.int32) + TILE - 1) // TILE
    lo = jnp.sum((segments[None, :] < by_block[:, :1]).astype(jnp.int32), axis=1) // TILE
    return marks, query_side, key_side, jnp.minimum(lo, hi)[None], hi[None]


def bias_tiles(table):
    place = jnp.arange(TILE, dtype=jnp.int32)
    kinds = jnp.arange(-2, 3, dtype=jnp.int32)[:, None, None] * TILE
    offset = jnp.clip(kinds + place[None, None, :] - place[None, :, None], -TILE, TILE)
    both = []
    for sign in (1, -1):
        both.append(
            table.astype(F32)[bucket_of(sign * offset, BUCKETS // 2)].transpose(3, 0, 1, 2) * LOG2E
        )
    return both


def tiles_of(first, second):
    rows = first.shape[0]
    shaped = [part.reshape(rows, -1, 1, HEAD_DIM) for part in (first, second)]
    return jnp.concatenate(shaped, axis=2).reshape(rows, -1)


def open_plain(
    tok, prompt, seg, live, w_query, w_key, w_value, w_output, w_inner, w_outer, gain_attn,
    gain_ffn, rel_table,
):
    slots, width = tok.shape
    packs = jnp.stack(
        [
            jnp.concatenate([tiles_of(w_key, w_value), tiles_of(w_query, w_output.T)], axis=1),
            w_inner,
            w_outer.T,
        ]
    )
    weights = lax.all_gather(lax.all_gather(packs, "dp", axis=1, tiled=True), "mp", axis=1)
    prompt_all = lax.all_gather(prompt.astype(BF), ("dp", "mp"), tiled=True)
    prompt_all = jnp.pad(prompt_all.reshape(PROMPT, width), ((0, TILE - PROMPT), (0, 0)))
    gains = lax.all_gather(jnp.stack([gain_attn, gain_ffn]), "dp", axis=1, tiled=True)
    gains = jnp.pad(gains.astype(F32), ((8, 6), (0, 0)))
    ahead, behind = bias_tiles(lax.all_gather(rel_table, "mp", axis=1, tiled=True))
    marks, query_side, key_side, lo, hi = slot_arrays(seg, live)
    placed = jnp.dot(marks, prompt_all, preferred_element_type=F32)
    x = jnp.where(query_side[:, IS_PROMPT:] > 0, placed, tok.astype(F32))
    normed = (x * rms_factor(x) * gains[8:9]).astype(BF)
    out = jnp.einsum("sd,mdc->smc", normed, weights[0], preferred_element_type=F32)
    half = out.shape[2] // 2
    kv = out[:, :, :half].astype(BF).reshape(slots, -1)
    q = jnp.where(low_lanes(half), out[:, :, half:] * LOG2E, 0.0).astype(BF).reshape(slots, -1)
    return weights, x, kv, q, ahead, behind, marks, query_side, key_side, gains, lo, hi


def adam_kernel(
    part_ref, state_ref, out_ref, land_one, land_two, mid_ref, send_one, recv_one, send_two,
    recv_two,
):
    dp = lax.axis_index("dp")
    mp = lax.axis_index("mp")
    wide = part_ref.shape[0]
    deep = mid_ref.shape[0]
    width = part_ref.shape[2]
    barrier = pltpu.get_barrier_semaphore()
    peers = [{"dp": lax.rem(dp + s, wide)} for s in range(1, wide)]
    peers += [{"mp": lax.rem(mp + s, deep)} for s in range(1, deep)]
    for peer in peers:
        pl.semaphore_signal(barrier, inc=1, device_id=peer, device_id_type=MESH)
    pl.semaphore_wait(barrier, len(peers))
    first = []
    for s in range(1, wide):
        to = lax.rem(dp + s, wide)
        copy = pltpu.make_async_remote_copy(
            src_ref=part_ref.at[to], dst_ref=land_one.at[s - 1],
            send_sem=send_one.at[s - 1], recv_sem=recv_one.at[s - 1],
            device_id={"dp": to}, device_id_type=MESH,
        )
        copy.start()
        first.append(copy)
    total = part_ref[dp]
    for s, copy in enumerate(first):
        copy.wait_recv()
        total = total + land_one[s]
    for m in range(deep):
        mid_ref[m, 0:4] = total[4 * m : 4 * m + 4]
        mid_ref[m, 4:8] = jnp.zeros((4, width), F32)
    second = []
    for s in range(1, deep):
        to = lax.rem(mp + s, deep)
        copy = pltpu.make_async_remote_copy(
            src_ref=mid_ref.at[to], dst_ref=land_two.at[s - 1],
            send_sem=send_two.at[s - 1], recv_sem=recv_two.at[s - 1],
            device_id={"mp": to}, device_id_type=MESH,
        )
        copy.start()
        second.append(copy)
    window = mid_ref[mp]
    for s, copy in enumerate(second):
        copy.wait_recv()
        window = window + land_two[s]
    begin = width // 8 * lax.rem(dp * deep + mp, 8)
    turned = pltpu.roll(window, lax.rem(width - begin, width), 1)
    lane = lax.broadcasted_iota(jnp.int32, (8, width), 1)
    grad = jnp.where(lane < width - begin, turned, pltpu.roll(turned, 7, 0))
    updated = adam_step(grad, state_ref[0], state_ref[1], state_ref[2])
    for i, value in enumerate(updated):
        out_ref[i] = value
    for copy in first + second:
        copy.wait_send()


def adam_step(grad, prompt, moment_one, moment_two):
    first_new = 0.9 * moment_one + 0.1 * grad
    second_new = 0.999 * moment_two + 0.001 * grad * grad
    correct_one = 1.0 - 0.9**ADAM_STEP
    correct_two = 1.0 - 0.999**ADAM_STEP
    prompt_new = prompt - 0.3 * (first_new / correct_one) / (
        jnp.sqrt(second_new / correct_two) + 1e-08
    )
    return prompt_new, first_new, second_new


def adam_call(part, state, deep):
    wide, rows, width = part.shape
    return pl.pallas_call(
        adam_kernel,
        in_specs=[VMEM_SPEC] * 2,
        out_specs=VMEM_SPEC,
        out_shape=jax.ShapeDtypeStruct(state.shape, F32),
        scratch_shapes=[
            pltpu.VMEM((wide - 1, rows, width), F32),
            pltpu.VMEM((deep - 1, 8, width), F32),
            pltpu.VMEM((deep, 8, width), F32),
            pltpu.SemaphoreType.DMA((wide - 1,)),
            pltpu.SemaphoreType.DMA((wide - 1,)),
            pltpu.SemaphoreType.DMA((deep - 1,)),
            pltpu.SemaphoreType.DMA((deep - 1,)),
        ],
        compiler_params=pltpu.CompilerParams(collective_id=1, has_side_effects=True),
        name="sum_and_step",
    )(part, state)


def body(
    dp, mp, tokens, prompt, moment_one, moment_two, segments, live, out_grad, w_query, w_key,
    w_value, w_output, w_inner, w_outer, gain_attn, gain_ffn, rel_table,
):
    _, slots, width = tokens.shape
    tuned = (dp, mp) == (8, 4)
    share = prompt.shape[0]
    if tuned:
        line = 8 * width
        state = functools.reduce(
            jnp.add,
            [
                jnp.pad(part, (i * line, (3 - i) * line - share))
                for i, part in enumerate((prompt, moment_one, moment_two))
            ],
        ).reshape(3, 8, width)
        (
            w, trio, last, x, kv, q, ahead, behind, marks, query_side, key_side, gains, lo, hi,
        ) = open_call(
            state, gain_attn[None], gain_ffn[None], rel_table.T, w_query, w_key, w_value,
            w_output, w_inner, w_outer.T, segments, live, tokens[0], dp, mp,
        )
        swap = lambda bit: lax.ppermute(trio, "dp", [(i, i ^ bit) for i in range(dp)])
        from_east, from_south, from_sib = swap(2), swap(4), swap(1)
        lasted = lax.ppermute(last, "mp", [(1, 0), (2, 3)])
    else:
        (
            weights, x, kv, q, ahead, behind, marks, query_side, key_side, gains, lo, hi,
        ) = open_plain(
            tokens[0], prompt, segments[0], live[0], w_query, w_key, w_value, w_output, w_inner,
            w_outer, gain_attn, gain_ffn, rel_table,
        )
    ctx, lse = attend_call(lo, hi, query_side, key_side, kv, q, ahead)
    if tuned:
        layer_output, grad_hidden = feed_call(
            out_grad[0], query_side, gains, x, ctx, w, trio, from_east, from_south, from_sib,
            last, lasted,
        )
        w = w.reshape(mp, width, -1)
    else:
        w = weights[0]
        layer_output, grad_hidden = feed_local(
            x, out_grad[0], query_side, gains, ctx, w, weights[1], weights[2]
        )
    input_grad, prompt_part, layer_output = backward_call(
        lo, hi, grad_hidden, lse, query_side, key_side, marks, gains, kv, w, q, ctx, x, behind,
        layer_output,
    )
    if tuned:
        stepped = adam_call(prompt_part.reshape(dp, -1, width), state, mp)
        stepped = stepped.reshape(3, -1)[:, :share]
        prompt_new, first_new, second_new = stepped[0], stepped[1], stepped[2]
    else:
        grad = lax.psum_scatter(
            prompt_part[:PROMPT].reshape(-1), ("dp", "mp"), scatter_dimension=0, tiled=True
        )
        prompt_new, first_new, second_new = adam_step(grad, prompt, moment_one, moment_two)
    return (layer_output[None], input_grad[None], prompt_new, first_new, second_new)


def solution(mesh):
    both = ("dp", "mp")
    return jax.shard_map(
        functools.partial(body, mesh.shape["dp"], mesh.shape["mp"]),
        mesh=mesh,
        in_specs=(
            P(both, None, None),
            P(both),
            P(both),
            P(both),
            P(both, None),
            P(both, None),
            P(both, None, None),
            P("dp", "mp"),
            P("dp", "mp"),
            P("dp", "mp"),
            P("mp", "dp"),
            P("dp", "mp"),
            P("mp", "dp"),
            P("dp"),
            P("dp"),
            P(None, "mp"),
        ),
        out_specs=(
            P(both, None, None),
            P(both, None, None),
            P(both),
            P(both),
            P(both),
        ),
        check_vma=False,
    )
```

```python
import functools

import jax
import jax.numpy as jnp
from jax import lax
from jax.experimental import pallas as pl
from jax.experimental.pallas import tpu as pltpu
from jax.sharding import PartitionSpec as P

HEADS = 12
HEAD_DIM = 64
BUCKETS = 32
PROMPT = 100
ADAM_STEP = 10
BOUNDS = (1, 2, 3, 4, 5, 6, 7, 8, 12, 16, 23, 32, 46, 64, 91)
EPSILON = 1e-06
MASKED = -1e30
LOG2E = 1.4426950408889634
LN2 = 0.6931471805599453
GELU_C = 0.7978845608028654

BLK = 256
TILE = 128
GROUP = 12
ALIVE = 126
IS_PROMPT = 127
BF = jnp.bfloat16
F32 = jnp.float32
NN = (((1,), (0,)), ((), ()))
NT = (((1,), (1,)), ((), ()))
TN = (((0,), (0,)), ((), ()))
MESH = pl.DeviceIdType.MESH
VMEM_LIMIT = 62 * 1024 * 1024
SMEM_SPEC = pl.BlockSpec(memory_space=pltpu.SMEM)
VMEM_SPEC = pl.BlockSpec(memory_space=pltpu.VMEM)
ANY_SPEC = pl.BlockSpec(memory_space=pl.ANY)


def mm(left, right, dims):
    return lax.dot_general(left, right, dims, preferred_element_type=F32)


def bucket_of(offset, half):
    distance = jnp.abs(offset)
    counted = sum(((distance >= limit).astype(jnp.int32) for limit in BOUNDS))
    return counted + jnp.where(offset > 0, half, 0).astype(jnp.int32)


def span(block, size=BLK):
    return pl.ds(pl.multiple_of(block * size, size), size)


def low_lanes(width=TILE):
    return lax.rem(lax.broadcasted_iota(jnp.int32, (1, width), 1), TILE) < HEAD_DIM


def fill_bias(line_ref, tiles_ref):
    def one(head, carry):
        row = line_ref[pl.ds(head, 1), :]
        wide = pltpu.roll(
            jnp.broadcast_to(row, (TILE, 4 * TILE)), 0, 1, stride=1, stride_axis=0
        )
        for near in range(1, 4):
            tiles_ref[head, near] = wide[:, near * TILE : (near + 1) * TILE]
        tiles_ref[head, 0] = jnp.broadcast_to(row[:, 0:1], (TILE, TILE))
        tiles_ref[head, 4] = jnp.broadcast_to(row[:, 4 * TILE - 1 :], (TILE, TILE))
        return carry

    lax.fori_loop(0, HEADS, one, 0)


def rms_factor(values):
    return lax.rsqrt(jnp.mean(values * values, axis=-1, keepdims=True) + EPSILON)


def neighbours():
    dp = lax.axis_index("dp")
    core = lax.rem(dp, 2)
    across = lax.rem(lax.div(dp, 2), 2)
    down = lax.div(dp, 4)
    return (
        dp + 1 - 2 * core,
        dp + 2 - 4 * across,
        dp + 4 - 8 * down,
        dp + 6 - 4 * across - 8 * down,
    )


def line_order(z, j):
    upper = lax.div(z, 2)
    return (z, z + 1 - 2 * lax.rem(z, 2), 2 - upper, 3 - 3 * upper)[j]


def flat_shift(rows, shift, width):
    lane = lax.broadcasted_iota(jnp.int32, (8, width), 1)
    turned = pltpu.roll(rows, shift, 1)
    return jnp.where(lane >= shift, turned, pltpu.roll(turned, 1, 0))


def interleave(first, second):
    parts = []
    for at in range(0, first.shape[1], HEAD_DIM):
        parts += [first[:, at : at + HEAD_DIM], second[:, at : at + HEAD_DIM]]
    return jnp.concatenate(parts, axis=1)


def open_kernel(
    state_ref, ga_ref, gf_ref, table_ref, wq_ref, wk_ref, wv_ref, wo_ref, wi_ref, wu_ref,
    seg_ref, live_ref, tok_ref,
    w_out, trio_out, last_out, x_out, kv_out, q_out, ahead_out, behind_out,
    marks_ref, qa_ref, ka_ref, gains_ref, lo_ref, hi_ref,
    small_src, small_v, pack_src, w_v, ff_src, x_v, norm_v, kv_v, q_v, lines_v, ahead_v,
    behind_v,
    own_sem, z_send, z_recv, send, recv, line_send, line_recv, out_sem,
):
    mp = lax.axis_index("mp")
    dp = lax.axis_index("dp")
    depth, wide = w_v.shape[0], w_v.shape[1]
    width = tok_ref.shape[1]
    sib, east, south, corner = neighbours()
    up, down = mp + 1 < depth, mp > 0
    barrier = pltpu.get_barrier_semaphore()

    def greet(peer):
        pl.semaphore_signal(barrier, inc=1, device_id=peer, device_id_type=MESH)

    for peer in (sib, east, south):
        greet({"dp": peer})
    pl.when(up)(lambda: greet({"mp": mp + 1}))
    pl.when(down)(lambda: greet({"mp": mp - 1}))

    share = lax.rem(dp * depth + mp, 8)
    part = ga_ref.shape[1]
    empty = jnp.zeros((1, width - part), F32)
    gain_rows = [
        pltpu.roll(jnp.concatenate([ref[...].astype(F32), empty], axis=1), part * dp, 1)
        for ref in (ga_ref, gf_ref)
    ]
    table_rows = jnp.concatenate(
        [table_ref[...].astype(F32), jnp.zeros((HEADS // depth, width - BUCKETS), F32)], axis=1
    )
    small_src[...] = jnp.concatenate(
        [flat_shift(state_ref[0], part * share, width)]
        + gain_rows
        + [table_rows, jnp.zeros((6 - HEADS // depth, width), F32)],
        axis=0,
    ).astype(BF)
    pack_src[...] = jnp.concatenate(
        [interleave(wk_ref[...], wv_ref[...]), interleave(wq_ref[...], wo_ref[...].T)], axis=1
    )
    ff_src[0] = wi_ref[...]
    ff_src[1] = wu_ref[...]
    pl.semaphore_wait(barrier, 3 + up.astype(jnp.int32) + down.astype(jnp.int32))

    def remote(src, dst, send_sem, recv_sem, peer):
        return pltpu.make_async_remote_copy(
            src_ref=src, dst_ref=dst, send_sem=send_sem, recv_sem=recv_sem,
            device_id=peer, device_id_type=MESH,
        )

    started = []
    local = []
    units = [(small_src, small_v), (pack_src, w_v)]

    def along(u, j, src):
        dst = units[u][1]
        z = line_order(mp, j)
        copies = []
        for at, (ahead, there, move) in enumerate(((up, z <= mp, 1), (down, z >= mp, -1))):
            copy = remote(
                src, dst.at[z, dp], z_send.at[u, j, at], z_recv.at[u, z], {"mp": mp + move}
            )
            copies.append((jnp.logical_and(ahead, there), copy))
        return copies

    lined = []

    def launch(copies):
        for condition, copy in copies:
            pl.when(condition)(copy.start)
        lined.extend(copies)

    def push(u, o, kind, src, dst, peer):
        copy = remote(src, dst, send.at[u, o, kind], recv.at[u, o, kind], peer)
        copy.start()
        started.append(copy)

    def landed(u, o, kind, dst):
        remote(dst, dst, send.at[u, o, kind], recv.at[u, o, kind], {"dp": sib}).wait_recv()

    def step(u, o):
        src, dst = units[u]
        z = line_order(mp, o)
        block = dst.at[z, dp]
        if o:
            remote(block, block, z_send.at[u, o, 0], z_recv.at[u, z], {"dp": sib}).wait_recv()
            src = block
        launch(along(u, o, src))
        push(u, o, 0, src, block, {"dp": east})
        push(u, o, 1, src, block, {"dp": south})
        push(u, o, 2, src, block, {"dp": sib})

    def forward(u, o):
        dst = units[u][1]
        z = line_order(mp, o)
        rows = dst.shape[2] // 2 if u else dst.shape[2]
        landed(u, o, 0, dst.at[z, east])
        push(u, o, 3, dst.at[z, east, 0:rows], dst.at[z, east, 0:rows], {"dp": south})
        push(u, o, 4, dst.at[z, east], dst.at[z, east], {"dp": sib})
        landed(u, o, 1, dst.at[z, south])
        if u:
            push(u, o, 5, dst.at[z, south, rows:], dst.at[z, south, rows:], {"dp": east})
        push(u, o, 6, dst.at[z, south], dst.at[z, south], {"dp": sib})

    def finish(u, o):
        dst = units[u][1]
        z = line_order(mp, o)
        rows = dst.shape[2] // 2 if u else dst.shape[2]
        landed(u, o, 3, dst.at[z, corner, 0:rows])
        if u:
            landed(u, o, 5, dst.at[z, corner, rows:])
        push(u, o, 7, dst.at[z, corner], dst.at[z, corner], {"dp": sib})

    flip = 1 - 2 * lax.rem(dp, 2)

    def complete(u, o):
        dst = units[u][1]
        z = line_order(mp, o)
        landed(u, o, 2, dst.at[z, sib])
        landed(u, o, 4, dst.at[z, east + flip])
        landed(u, o, 6, dst.at[z, south + flip])
        landed(u, o, 7, dst.at[z, corner + flip])

    for u in range(2):
        step(u, 0)
        src, dst = units[u]
        copy = pltpu.make_async_copy(src, dst.at[mp, dp], own_sem.at[u])
        copy.start()
        local.append(copy)
    own_copy = pltpu.make_async_copy(ff_src, trio_out.at[0], own_sem.at[2])
    own_copy.start()
    partner = line_order(mp, 1)
    across = depth - 1 - mp
    inside = lax.rem(lax.div(mp + 1, 2), 2) == 1
    at_end = jnp.logical_not(inside)

    def line_copy(src, dst, at, at_recv, to):
        return remote(src, dst, line_send.at[at], line_recv.at[at_recv], {"mp": to})

    pair_copy = line_copy(ff_src, trio_out.at[1], 0, 0, partner)
    over_copy = line_copy(ff_src, trio_out.at[2], 1, 1, across)
    far_copy = line_copy(trio_out.at[1], last_out, 2, 2, across)
    back_copy = line_copy(trio_out.at[2], trio_out.at[2], 3, 1, partner)

    slots = tok_ref.shape[0]
    segment_row = seg_ref[...].astype(F32)
    live_row = live_ref[...].astype(F32)
    lane = lax.broadcasted_iota(jnp.int32, (slots, TILE), 1)
    lane_f = lane.astype(F32)
    segment = jnp.broadcast_to(segment_row, (TILE, slots)).T
    alive = jnp.broadcast_to(live_row, (TILE, slots)).T
    same = segment == lane_f
    start = jnp.sum((segment < lane_f).astype(F32), axis=0, keepdims=True)
    first = jnp.sum(jnp.where(same, start, 0.0), axis=1, keepdims=True)
    position = lax.broadcasted_iota(jnp.int32, (slots, 1), 0).astype(F32) - first
    prompt_slot = (alive > 0) & (position < PROMPT)
    sides = jnp.where(lane == ALIVE, alive, same.astype(F32))
    qa_ref[...] = jnp.where(lane == IS_PROMPT, prompt_slot.astype(F32), sides).astype(BF)
    ka_ref[...] = jnp.where(
        (lane < 16) & jnp.logical_not(same & (alive > 0)), MASKED, 0.0
    ).astype(BF)
    step(0, 1)
    forward(0, 0)
    step(0, 2)
    step(1, 1)
    forward(1, 0)
    forward(0, 1)
    finish(0, 0)
    step(0, 3)
    forward(0, 2)
    finish(0, 1)

    def window_rows(device, inside):
        target = 25 * lax.div(device, 8) + 3 * lax.rem(device, 8) + inside
        return jnp.where(inside < 4, target, -1).astype(F32)

    at = lax.broadcasted_iota(jnp.int32, (1, TILE), 1)
    target = window_rows(lax.div(at, 4), lax.rem(at, 4))
    marks_ref[...] = jnp.where((position == target) & prompt_slot, 1.0, 0.0).astype(BF)
    forward(0, 3)
    finish(0, 2)
    step(1, 2)
    forward(1, 1)
    finish(0, 3)
    finish(1, 0)
    block_lane = lax.broadcasted_iota(jnp.int32, (8, TILE), 1)
    lows = jnp.zeros((8, TILE), F32)
    highs = jnp.zeros((8, TILE), F32)
    for block in range(slots // TILE):
        here = segment_row[:, block * TILE : (block + 1) * TILE]
        lives = live_row[:, block * TILE : (block + 1) * TILE] > 0
        top = jnp.max(jnp.where(lives, here, -1.0), axis=1, keepdims=True)
        bottom = jnp.min(here, axis=1, keepdims=True)
        before = jnp.sum((segment_row < bottom).astype(F32), axis=1, keepdims=True)
        through = (segment_row <= top) & (live_row > 0)
        through = jnp.sum(through.astype(F32), axis=1, keepdims=True)
        lows = jnp.where(block_lane == block, before, lows)
        highs = jnp.where(block_lane == block, through, highs)
    highs = lax.div(highs.astype(jnp.int32) + TILE - 1, TILE)
    hi_ref[...] = highs
    lo_ref[...] = jnp.minimum(lax.div(lows.astype(jnp.int32), TILE), highs)
    for o in range(depth):
        complete(0, o)
    local[0].wait()

    gains = functools.reduce(jnp.add, [small_v[0, d].astype(F32) for d in range(wide)])
    gains_ref[...] = gains
    rows_all = depth * wide * 16
    at = lax.broadcasted_iota(jnp.int32, (1, rows_all), 1)
    holder = lax.div(at, 16)
    target = window_rows(
        lax.rem(holder, wide) * depth + lax.div(holder, wide), lax.rem(at, 16)
    )
    windows = small_v[...].reshape(rows_all, width)
    gain = gains[8:9]

    def embed(f):
        rows = slice(f, f + BLK)
        hot = (position[rows] == target).astype(F32).astype(BF)
        placed = mm(hot, windows, NN)
        value = jnp.where(prompt_slot[rows, 0:1], placed, tok_ref[rows, :].astype(F32))
        x_v[rows, :] = value
        norm_v[rows, :] = (value * rms_factor(value) * gain).astype(BF)

    for f in range(0, slots, BLK):
        embed(f)
        if f == slots // 2 - BLK:
            step(1, 3)
            pair_copy.start()
            pl.when(inside)(over_copy.start)
            forward(1, 2)
            finish(1, 1)
    copy = pltpu.make_async_copy(x_v, x_out, out_sem.at[0])
    copy.start()
    local.append(copy)

    half = w_v.shape[3] // 2
    low = low_lanes(half)

    def project(o):
        complete(1, o)
        if o == 0:
            local[1].wait()
        z = line_order(mp, o)
        copy = pltpu.make_async_copy(w_v.at[z], w_out.at[z], out_sem.at[1 + o])
        copy.start()
        local.append(copy)
        weight = w_v[z].reshape(wide * w_v.shape[2], 2 * half)
        cols = span(z, half)
        parts = [mm(norm_v[f : f + BLK, :], weight, NN) for f in range(0, slots, BLK)]
        for i, piece in enumerate(parts):
            rows = slice(i * BLK, (i + 1) * BLK)
            kv_v[rows, cols] = piece[:, :half].astype(BF)
            q_v[rows, cols] = jnp.where(low, piece[:, half:] * LOG2E, 0.0).astype(BF)
        for at_sem, (src, dst) in enumerate(((kv_v, kv_out), (q_v, q_out))):
            copy = pltpu.make_async_copy(
                src.at[:, cols], dst.at[:, cols], out_sem.at[1 + depth + 2 * o + at_sem]
            )
            copy.start()
            local.append(copy)

    table = jnp.concatenate(
        [small_v[m, 0].astype(F32)[10 : 10 + HEADS // depth, 0:TILE] for m in range(depth)]
        + [jnp.zeros((16 - HEADS, TILE), F32)],
        axis=0,
    ).astype(BF)
    offset = lax.broadcasted_iota(jnp.int32, (1, 4 * TILE), 1) - 2 * TILE
    code = lax.broadcasted_iota(jnp.int32, (TILE, 4 * TILE), 0)
    def bias_out(at_sem, sign, tiles, out):
        hot = (code == bucket_of(sign * offset, BUCKETS // 2)).astype(F32).astype(BF)
        lines_v[...] = mm(table, hot, NN) * LOG2E
        fill_bias(lines_v, tiles)
        copy = pltpu.make_async_copy(tiles, out, out_sem.at[1 + 3 * depth + at_sem])
        copy.start()
        local.append(copy)

    bias_out(0, 1, ahead_v, ahead_out)
    forward(1, 3)
    finish(1, 2)
    @pl.when(inside)
    def _():
        pair_copy.wait_recv()
        far_copy.start()
        over_copy.wait_recv()
        back_copy.start()

    project(0)
    finish(1, 3)
    project(1)
    project(2)
    bias_out(1, -1, behind_v, behind_out)
    project(3)
    own_copy.wait()
    pair_copy.wait_send()

    @pl.when(at_end)
    def _():
        pair_copy.wait_recv()
        back_copy.wait_recv()

    @pl.when(inside)
    def _():
        over_copy.wait_send()
        far_copy.wait()
        back_copy.wait_send()

    for copy in local[2:]:
        copy.wait()
    for copy in started:
        copy.wait_send()
    for condition, copy in lined:
        pl.when(condition)(copy.wait_send)


def open_call(state, ga, gf, table, wq, wk, wv, wo, wi, wu, seg, live, tok, dp, mp):
    slots, width = tok.shape
    rows = wi.shape[0]
    wide = HEADS * TILE
    pack = (rows, width)
    shape = jax.ShapeDtypeStruct
    dma = pltpu.SemaphoreType.DMA
    tiles = (HEADS, 5, TILE, TILE)
    return pl.pallas_call(
        open_kernel,
        in_specs=[VMEM_SPEC] * 13,
        out_specs=[ANY_SPEC] * 8 + [VMEM_SPEC] * 6,
        out_shape=[
            shape((mp, dp) + pack, BF),
            shape((3, 2) + pack, BF),
            shape((2,) + pack, BF),
            shape((slots, width), F32),
            shape((slots, wide), BF),
            shape((slots, wide), BF),
            shape(tiles, F32),
            shape(tiles, F32),
            shape((slots, TILE), BF),
            shape((slots, TILE), BF),
            shape((slots, TILE), BF),
            shape((16, width), F32),
            shape((8, TILE), jnp.int32),
            shape((8, TILE), jnp.int32),
        ],
        scratch_shapes=[
            pltpu.VMEM((16, width), BF),
            pltpu.VMEM((mp, dp, 16, width), BF),
            pltpu.VMEM(pack, BF),
            pltpu.VMEM((mp, dp) + pack, BF),
            pltpu.VMEM((2,) + pack, BF),
            pltpu.VMEM((slots, width), F32),
            pltpu.VMEM((slots, width), BF),
            pltpu.VMEM((slots, wide), BF),
            pltpu.VMEM((slots, wide), BF),
            pltpu.VMEM((16, 4 * TILE), F32),
            pltpu.VMEM(tiles, F32),
            pltpu.VMEM(tiles, F32),
            dma((3,)),
            dma((2, mp, 2)),
            dma((2, mp)),
            dma((2, mp, 8)),
            dma((2, mp, 8)),
            dma((4,)),
            dma((3,)),
            dma((3 + 3 * mp,)),
        ],
        compiler_params=pltpu.CompilerParams(
            collective_id=0, has_side_effects=True, vmem_limit_bytes=VMEM_LIMIT
        ),
        cost_estimate=pl.CostEstimate(
            flops=16 * 10**9, bytes_accessed=40 * 10**6, transcendentals=0
        ),
        name="open_layer",
    )(state, ga, gf, table, wq, wk, wv, wo, wi, wu, seg, live, tok)


def window_of(lo_ref, hi_ref, block, blocks):
    lo = lo_ref[0, block]
    pairs = lax.div(hi_ref[0, block] - lo + 1, 2)
    return jnp.minimum(lo, blocks - 2 * pairs), pairs


def bias_row(tiles_ref, head, first, block, pairs):
    return jnp.concatenate(
        [
            tiles_ref[head, jnp.clip(first + j - block, -2, 2) + 2]
            for j in range(2 * pairs)
        ],
        axis=1,
    )


def attend_kernel(
    lo_ref, hi_ref, qa_ref, ka_ref, kv_hbm, q_hbm, tiles_hbm,
    ctx_out, lse_ref,
    kv_ref, val_ref, q_ref, ctx_ref, tiles_ref, lsem_ref, mean_ref, sems, ctx_sems,
):
    slots = qa_ref.shape[0]
    blocks = slots // TILE
    copies = [
        pltpu.make_async_copy(src, dst, sems.at[i])
        for i, (src, dst) in enumerate(
            ((kv_hbm, kv_ref), (q_hbm, q_ref), (tiles_hbm, tiles_ref))
        )
    ]
    for copy in copies:
        copy.start()
    copies[0].wait()
    mean_ref[...] = mm(jnp.full((8, slots), 1.0 / slots, BF), kv_ref[...], NN)
    high = jnp.logical_not(low_lanes())
    ones = jnp.ones((slots, TILE), BF)
    for h in range(HEADS):
        cols = slice(h * TILE, (h + 1) * TILE)
        val_ref[:, cols] = jnp.where(high, kv_ref[:, cols], ones)
    lane = lax.broadcasted_iota(jnp.int32, (1, TILE), 1)
    copies[1].wait()
    copies[2].wait()

    def query_block(qb, carry):
        qs = span(qb, TILE)
        first, count = window_of(lo_ref, hi_ref, qb, blocks)
        alive = qa_ref[qs, ALIVE : ALIVE + 1].astype(F32) > 0
        lsem_ref[...] = jnp.zeros_like(lsem_ref)

        def attend(pairs):
            size = 2 * pairs * TILE
            ks = pl.ds(pl.multiple_of(first * TILE, TILE), size)
            mask = mm(qa_ref[qs, :], ka_ref[ks, :], NT)

            def group_body(g, inner):
                heads = [g * GROUP + i for i in range(GROUP)]
                cols = [span(h, TILE) for h in heads]
                scores = [
                    mm(q_ref[qs, c], kv_ref[ks, c], NT)
                    + (bias_row(tiles_ref, h, first, qb, pairs) + mask)
                    for h, c in zip(heads, cols)
                ]
                tops = [jnp.max(row, axis=1, keepdims=True) for row in scores]
                weights = [jnp.exp2(row - top).astype(BF) for row, top in zip(scores, tops)]
                for h, c, top, weight in zip(heads, cols, tops, weights):
                    both = mm(weight, val_ref[ks, c], NN)
                    context = both / pltpu.roll(both, HEAD_DIM, 1)
                    context = jnp.where(alive, context, mean_ref[0:1, c])
                    ctx_ref[qs, c] = jnp.where(high, context, 0.0).astype(BF)
                    lsem_ref[...] = jnp.where(
                        (lane == h) & alive, top + jnp.log2(both), lsem_ref[...]
                    )
                return inner

            lax.fori_loop(0, HEADS // GROUP, group_body, 0)

        for pairs in range(1, blocks // 2 + 1):
            pl.when(count == pairs)(functools.partial(attend, pairs))

        @pl.when(count == 0)
        def _():
            every = jnp.logical_not(low_lanes(HEADS * TILE))
            ctx_ref[qs, :] = jnp.broadcast_to(
                jnp.where(every, mean_ref[0:1, :], 0.0), (TILE, HEADS * TILE)
            ).astype(BF)

        lse_ref[:, qs] = lsem_ref[...].T[0:16]
        pltpu.make_async_copy(ctx_ref.at[qs], ctx_out.at[qs], ctx_sems.at[qb]).start()
        return carry

    lax.fori_loop(0, blocks, query_block, 0)
    for b in range(blocks):
        rows = slice(b * TILE, (b + 1) * TILE)
        pltpu.make_async_copy(ctx_ref.at[rows], ctx_out.at[rows], ctx_sems.at[b]).wait()


def attend_call(lo, hi, qa, ka, kv, q, tiles):
    slots, wide = kv.shape
    return pl.pallas_call(
        attend_kernel,
        in_specs=[SMEM_SPEC] * 2 + [VMEM_SPEC] * 2 + [ANY_SPEC] * 3,
        out_specs=[ANY_SPEC, VMEM_SPEC],
        out_shape=[
            jax.ShapeDtypeStruct((slots, wide), BF),
            jax.ShapeDtypeStruct((16, slots), F32),
        ],
        scratch_shapes=[
            pltpu.VMEM((slots, wide), BF),
            pltpu.VMEM((slots, wide), BF),
            pltpu.VMEM((slots, wide), BF),
            pltpu.VMEM((slots, wide), BF),
            pltpu.VMEM(tiles.shape, F32),
            pltpu.VMEM((TILE, TILE), F32),
            pltpu.VMEM((8, wide), F32),
            pltpu.SemaphoreType.DMA((3,)),
            pltpu.SemaphoreType.DMA((slots // TILE,)),
        ],
        compiler_params=pltpu.CompilerParams(vmem_limit_bytes=VMEM_LIMIT),
        cost_estimate=pl.CostEstimate(
            flops=25 * 10**9, bytes_accessed=10**7, transcendentals=10**7
        ),
        name="attend",
    )(lo, hi, qa, ka, kv, q, tiles)


def gelu_both(inner, upstream):
    square = inner * inner
    bent = jnp.tanh(inner * (GELU_C + (GELU_C * 0.044715) * square))
    half = 0.5 + 0.5 * bent
    activated = inner * half
    slope = half + activated * ((1.0 - half) * (2 * GELU_C + (6 * GELU_C * 0.044715) * square))
    return activated.astype(BF), (upstream * slope).astype(BF)


def feed_kernel(
    og_ref, qa_ref, gains_ref, x_hbm, ctx_hbm, w_hbm, trio_hbm, east_hbm, south_hbm, last_hbm,
    lasted_hbm,
    out_hbm, gh_hbm,
    ff_v, ctx_ref, w_ref, x_ref, norm_ref, gb_ref, hid_ref, br_ref, dn_ref, out_ref, gh_ref,
    sems, fill, send, recv, out_sem,
):
    dp = lax.axis_index("dp")
    mp = lax.axis_index("mp")
    depth, wide = ff_v.shape[0], ff_v.shape[1]
    half = w_hbm.shape[3] // 2
    rows_half = ff_v.shape[3] // 2
    sib, east, south, corner = neighbours()
    flip = 1 - 2 * lax.rem(dp, 2)
    upper, lower = pl.ds(0, rows_half), pl.ds(rows_half, rows_half)
    inside = lax.rem(lax.div(mp + 1, 2), 2) == 1
    barrier = pltpu.get_barrier_semaphore()
    for peer in (sib, east, south):
        pl.semaphore_signal(barrier, inc=1, device_id={"dp": peer}, device_id_type=MESH)
    first = [
        pltpu.make_async_copy(ctx_hbm, ctx_ref, sems.at[0]),
        pltpu.make_async_copy(x_hbm, x_ref, sems.at[1]),
    ]
    for m in range(depth):
        first.append(
            pltpu.make_async_copy(
                w_hbm.at[m, :, :, half:],
                w_ref.at[:, :, m * half : (m + 1) * half],
                sems.at[2 + m],
            )
        )
    end = depth - 1
    for here, source in ((inside, last_hbm), (jnp.logical_not(inside), lasted_hbm)):
        pl.when(here)(pltpu.make_async_copy(source, ff_v.at[end, dp], fill.at[end, 0]).start)
    for copy in first:
        copy.start()
    pl.semaphore_wait(barrier, 3)

    def remote(src, dst, j, kind, peer):
        return pltpu.make_async_remote_copy(
            src_ref=src, dst_ref=dst, send_sem=send.at[j, kind], recv_sem=recv.at[j, kind],
            device_id={"dp": peer}, device_id_type=MESH,
        )

    sent = []

    def push(src, dst, j, kind, peer):
        copy = remote(src, dst, j, kind, peer)
        copy.start()
        sent.append(copy)

    def awaited(block, j, kind):
        remote(block, block, j, kind, sib).wait_recv()

    def relay(j, from_east, from_south):
        push(from_east.at[:, upper], ff_v.at[j, east, :, upper], j, 0, south)
        push(from_south.at[:, lower], ff_v.at[j, south, :, lower], j, 1, east)
        push(from_east, ff_v.at[j, east], j, 2, sib)
        push(from_south, ff_v.at[j, south], j, 3, sib)

    for j in range(end):
        relay(j, east_hbm.at[j], south_hbm.at[j])
        push(trio_hbm.at[j], ff_v.at[j, dp], j, 7, sib)
        for kind, (src, place) in enumerate(
            ((trio_hbm, dp), (east_hbm, east), (south_hbm, south))
        ):
            pltpu.make_async_copy(src.at[j], ff_v.at[j, place], fill.at[j, kind]).start()

    def spread(j):
        block = ff_v.at[j, dp]
        pltpu.make_async_copy(block, block, fill.at[j, 0]).wait()
        for kind, peer in ((5, east), (6, south), (7, sib)):
            push(block, block, j, kind, peer)

    spread(end)

    def pass_on(j):
        awaited(ff_v.at[j, east], j, 5)
        awaited(ff_v.at[j, south], j, 6)
        relay(j, ff_v.at[j, east], ff_v.at[j, south])

    def corners(j):
        block = ff_v.at[j, corner]
        awaited(ff_v.at[j, corner, :, upper], j, 0)
        awaited(ff_v.at[j, corner, :, lower], j, 1)
        push(block, block, j, 4, sib)

    def landed(j):
        for kind, place in ((2, east + flip), (3, south + flip), (4, corner + flip)):
            awaited(ff_v.at[j, place], j, kind)
        if j < end:
            for kind, place in enumerate((dp, east, south)):
                block = ff_v.at[j, place]
                pltpu.make_async_copy(block, block, fill.at[j, kind]).wait()
        awaited(ff_v.at[j, sib], j, 7)

    slots = og_ref.shape[0]
    gain = gains_ref[9:10]
    blocks = [slice(f, f + BLK) for f in range(0, slots, BLK)]
    for rows in blocks:
        gb_ref[rows, :] = (
            og_ref[rows, :].astype(F32) * qa_ref[rows, ALIVE : ALIVE + 1].astype(F32)
        ).astype(BF)
    for copy in first:
        copy.wait()
    weight = w_ref[...].reshape(-1, depth * half)
    for i, rows in enumerate(blocks):
        hid_ref[rows, :] = x_ref[rows, :] + mm(ctx_ref[rows, :], weight, NT)
        if i == len(blocks) // 2 - 1:
            corners(0)
    corners(1)
    for rows in blocks:
        hidden = hid_ref[rows, :]
        norm_ref[rows, :] = (hidden * rms_factor(hidden) * gain).astype(BF)

    def unit_block(j, chosen):
        wi = ff_v[j, :, 0].reshape(-1, ff_v.shape[4])
        wo = ff_v[j, :, 1].reshape(-1, ff_v.shape[4])
        inner = [mm(norm_ref[rows, :], wi, NN) for rows in chosen]
        upstream = [mm(gb_ref[rows, :], wo, NN) for rows in chosen]
        pairs = [gelu_both(a, b) for a, b in zip(inner, upstream)]
        results = []
        for rows, (activated, grad_inner) in zip(chosen, pairs):
            branch, back = mm(activated, wo, NT), mm(grad_inner, wi, NT)
            if j:
                branch, back = br_ref[rows, :] + branch, dn_ref[rows, :] + back
            if j < end:
                br_ref[rows, :], dn_ref[rows, :] = branch, back
            results.append((branch, back))
        return results

    landed(0)
    unit_block(0, blocks)
    corners(2)
    pass_on(3)
    landed(1)
    unit_block(1, blocks)
    corners(3)
    landed(2)
    unit_block(2, blocks)
    landed(3)
    outs = []
    for i, (rows, (branch, back)) in enumerate(zip(blocks, unit_block(end, blocks))):
        hidden = hid_ref[rows, :]
        alive = qa_ref[rows, ALIVE : ALIVE + 1].astype(F32)
        out_ref[rows, :] = (alive * (hidden + branch)).astype(BF)
        factor = rms_factor(hidden)
        weighted = back * gain
        gh_ref[rows, :] = og_ref[rows, :].astype(F32) * alive + (
            factor * weighted
            - hidden
            * (factor * factor * factor)
            * jnp.mean(weighted * hidden, axis=-1, keepdims=True)
        )
        for at, (src, dst) in enumerate(((out_ref, out_hbm), (gh_ref, gh_hbm))):
            copy = pltpu.make_async_copy(src.at[rows], dst.at[rows], out_sem.at[2 * i + at])
            copy.start()
            outs.append(copy)
    for copy in outs:
        copy.wait()
    for copy in sent:
        copy.wait_send()


def feed_call(
    og, qa, gains, x, ctx, w, trio, from_east, from_south, last, lasted
):
    slots, width = x.shape
    depth, wide, rows, units = w.shape
    dma = pltpu.SemaphoreType.DMA
    return pl.pallas_call(
        feed_kernel,
        in_specs=[VMEM_SPEC] * 3 + [ANY_SPEC] * 8,
        out_specs=[ANY_SPEC] * 2,
        out_shape=[
            jax.ShapeDtypeStruct((slots, width), BF),
            jax.ShapeDtypeStruct((slots, width), F32),
        ],
        scratch_shapes=[
            pltpu.VMEM((depth, wide) + trio.shape[1:], BF),
            pltpu.VMEM(ctx.shape, BF),
            pltpu.VMEM((wide, rows, depth * units // 2), BF),
            pltpu.VMEM((slots, width), F32),
            pltpu.VMEM((slots, width), BF),
            pltpu.VMEM((slots, width), BF),
            pltpu.VMEM((slots, width), F32),
            pltpu.VMEM((slots, width), F32),
            pltpu.VMEM((slots, width), F32),
            pltpu.VMEM((slots, width), BF),
            pltpu.VMEM((slots, width), F32),
            dma((2 + depth,)),
            dma((depth, 3)),
            dma((depth, 8)),
            dma((depth, 8)),
            dma((2 * (slots // BLK),)),
        ],
        compiler_params=pltpu.CompilerParams(
            collective_id=2, has_side_effects=True, vmem_limit_bytes=VMEM_LIMIT
        ),
        name="feed_forward",
    )(og, qa, gains, x, ctx, w, trio, from_east, from_south, last, lasted)


def feed_local_kernel(
    x_ref, og_ref, qa_ref, gain_ref, ctx_hbm, w_hbm, wi_hbm, wo_hbm,
    out_ref, gh_ref,
    ctx_ref, w_ref, wi_ref, wo_ref, norm_ref, gb_ref, hid_ref, br_ref, dn_ref, sems,
):
    slots = x_ref.shape[0]
    groups = w_hbm.shape[0]
    half = w_hbm.shape[2] // 2
    first = [pltpu.make_async_copy(ctx_hbm, ctx_ref, sems.at[0])]
    for m in range(groups):
        first.append(
            pltpu.make_async_copy(w_hbm.at[m, :, half:], w_ref.at[m], sems.at[1 + m])
        )
    later = []
    for m in range(groups):
        later.append(
            (
                pltpu.make_async_copy(wi_hbm.at[m], wi_ref.at[m], sems.at[1 + groups + 2 * m]),
                pltpu.make_async_copy(wo_hbm.at[m], wo_ref.at[m], sems.at[2 + groups + 2 * m]),
            )
        )
    for copy in first:
        copy.start()
    for pair in later:
        pair[0].start()
        pair[1].start()
    for copy in first:
        copy.wait()
    gain = gain_ref[9:10]
    blocks = [slice(f, f + BLK) for f in range(0, slots, BLK)]
    for rows in blocks:
        hid_ref[rows, :] = x_ref[rows, :]
    for m in range(groups):
        cols = slice(m * half, (m + 1) * half)
        for rows in blocks:
            hid_ref[rows, :] += mm(ctx_ref[rows, cols], w_ref[m], NT)
    for rows in blocks:
        hidden = hid_ref[rows, :]
        norm_ref[rows, :] = (hidden * rms_factor(hidden) * gain).astype(BF)
        gb_ref[rows, :] = (
            og_ref[rows, :].astype(F32) * qa_ref[rows, ALIVE : ALIVE + 1].astype(F32)
        ).astype(BF)
    br_ref[...] = jnp.zeros_like(br_ref)
    dn_ref[...] = jnp.zeros_like(dn_ref)
    for m in range(groups):
        later[m][0].wait()
        later[m][1].wait()
    def unit_block(m, carry):
        inner = [mm(norm_ref[rows, :], wi_ref[m], NN) for rows in blocks]
        upstream = [mm(gb_ref[rows, :], wo_ref[m], NN) for rows in blocks]
        pairs = [gelu_both(a, b) for a, b in zip(inner, upstream)]
        for rows, (activated, grad_inner) in zip(blocks, pairs):
            br_ref[rows, :] += mm(activated, wo_ref[m], NT)
            dn_ref[rows, :] += mm(grad_inner, wi_ref[m], NT)
        return carry

    lax.fori_loop(0, groups, unit_block, 0)
    for rows in blocks:
        hidden = hid_ref[rows, :]
        alive = qa_ref[rows, ALIVE : ALIVE + 1].astype(F32)
        out_ref[rows, :] = (alive * (hidden + br_ref[rows, :])).astype(BF)
        factor = rms_factor(hidden)
        weighted = dn_ref[rows, :] * gain
        gh_ref[rows, :] = og_ref[rows, :].astype(F32) * alive + (
            factor * weighted
            - hidden
            * (factor * factor * factor)
            * jnp.mean(weighted * hidden, axis=-1, keepdims=True)
        )


def feed_local(x, og, qa, gain, ctx, w, wi, wo):
    slots, width = x.shape
    groups = w.shape[0]
    return pl.pallas_call(
        feed_local_kernel,
        in_specs=[VMEM_SPEC] * 4 + [ANY_SPEC] * 4,
        out_specs=[VMEM_SPEC] * 2,
        out_shape=[
            jax.ShapeDtypeStruct((slots, width), BF),
            jax.ShapeDtypeStruct((slots, width), F32),
        ],
        scratch_shapes=[
            pltpu.VMEM(ctx.shape, BF),
            pltpu.VMEM((groups, w.shape[1], w.shape[2] // 2), BF),
            pltpu.VMEM(wi.shape, BF),
            pltpu.VMEM(wo.shape, BF),
            pltpu.VMEM((slots, width), BF),
            pltpu.VMEM((slots, width), BF),
            pltpu.VMEM((slots, width), F32),
            pltpu.VMEM((slots, width), F32),
            pltpu.VMEM((slots, width), F32),
            pltpu.SemaphoreType.DMA((1 + 3 * groups,)),
        ],
        compiler_params=pltpu.CompilerParams(vmem_limit_bytes=VMEM_LIMIT),
        name="feed_forward_local",
    )(x, og, qa, gain, ctx, w, wi, wo)


def backward_kernel(
    lo_ref, hi_ref, gh_ref, lse_ref, qa_ref, ka_ref, marks_ref, gains_ref, kv_hbm, w_hbm, q_hbm,
    ctx_hbm, x_hbm, tiles_hbm, layer_hbm,
    ig_out, pg_ref, layer_out,
    kv_ref, w_ref, q_ref, ctx_ref, x_ref, tiles_ref, layer_ref, all_ref, kt_ref, dsum_ref,
    dqt_ref, ig_ref, sems, out_sem,
):
    slots = gh_ref.shape[0]
    count_blocks = slots // TILE
    groups = w_hbm.shape[0]
    half = w_hbm.shape[2] // 2
    wide = HEADS * TILE
    weights = [
        pltpu.make_async_copy(
            w_hbm.at[m, :, side * half : (side + 1) * half],
            w_ref.at[:, side * wide + m * half : side * wide + (m + 1) * half],
            sems.at[6 + side * groups + m],
        )
        for side in (1, 0)
        for m in range(groups)
    ]
    q_copy, ctx_copy, kv_copy, tiles_copy, x_copy, layer_copy = [
        pltpu.make_async_copy(src, dst, sems.at[i])
        for i, (src, dst) in enumerate(
            (
                (q_hbm, q_ref),
                (ctx_hbm, ctx_ref),
                (kv_hbm, kv_ref),
                (tiles_hbm, tiles_ref),
                (x_hbm, x_ref),
                (layer_hbm, layer_ref),
            )
        )
    ]
    for copy in [q_copy] + weights + [ctx_copy, kv_copy, tiles_copy, x_copy, layer_copy]:
        copy.start()
    dqt_ref[...] = jnp.zeros_like(dqt_ref)
    blocks = [slice(f, f + BLK) for f in range(0, slots, BLK)]
    q_copy.wait()
    grads_low = [gh_ref[rows, :].astype(BF) for rows in blocks]
    for copy in weights[:groups]:
        copy.wait()
    low_wide = low_lanes(wide)
    parts = [mm(grad, w_ref[:, wide:], NN) for grad in grads_low]
    for rows, part in zip(blocks, parts):
        q_ref[rows, :] = jnp.where(low_wide, q_ref[rows, :], part.astype(BF))
    ctx_copy.wait()
    pick = (
        lax.broadcasted_iota(jnp.int32, (wide, TILE), 0) // TILE
        == lax.broadcasted_iota(jnp.int32, (wide, TILE), 1)
    ).astype(F32).astype(BF)
    sums = []
    for rows in blocks:
        product = q_ref[rows, :].astype(F32) * ctx_ref[rows, :].astype(F32)
        upper = product.astype(BF)
        lower = (product - upper.astype(F32)).astype(BF)
        sums.append(mm(upper, pick, NN) + mm(lower, pick, NN))
    for rows, value in zip(blocks, sums):
        dsum_ref[:, rows] = value.T[0:16]
    kv_copy.wait()
    for h in range(HEADS):
        kt_ref[h] = kv_ref[:, h * TILE : (h + 1) * TILE].T[0:HEAD_DIM]
    tiles_copy.wait()
    low = low_lanes()

    def key_block(kb, carry):
        ks = span(kb, TILE)
        first, count = window_of(lo_ref, hi_ref, kb, count_blocks)

        def attend(pairs):
            size = 2 * pairs * TILE
            qs = pl.ds(pl.multiple_of(first * TILE, TILE), size)
            mask = mm(ka_ref[ks, :], qa_ref[qs, :], NT)

            def group_body(g, inner):
                heads = [g * GROUP + i for i in range(GROUP)]
                cols = [span(h, TILE) for h in heads]
                zero = jnp.zeros((TILE, TILE), BF)
                keys = [kv_ref[ks, c] for c in cols]
                raw = [
                    mm(
                        jnp.concatenate(
                            [jnp.where(low, key, zero), jnp.where(low, zero, key)], axis=0
                        ),
                        q_ref[qs, c],
                        NT,
                    )
                    for key, c in zip(keys, cols)
                ]
                probs = [
                    jnp.exp2(
                        both[:TILE]
                        + (bias_row(tiles_ref, h, first, kb, pairs) + mask)
                        - lse_ref[pl.ds(h, 1), qs]
                    )
                    for h, both in zip(heads, raw)
                ]
                outs = [
                    (p * (both[TILE:] - dsum_ref[pl.ds(h, 1), qs])).astype(BF)
                    for h, p, both in zip(heads, probs, raw)
                ]
                sides = [
                    jnp.concatenate([out, p.astype(BF)], axis=0) for out, p in zip(outs, probs)
                ]
                for h, c, out, side in zip(heads, cols, outs, sides):
                    both = mm(side, q_ref[qs, c], NN)
                    all_ref[ks, c] = jnp.where(
                        low, both[:TILE] * LN2, both[TILE:]
                    ).astype(BF)
                    dqt_ref[h, :, qs] += mm(kt_ref[h, :, ks], out, NN)
                return inner

            lax.fori_loop(0, HEADS // GROUP, group_body, 0)

        for pairs in range(1, count_blocks // 2 + 1):
            pl.when(count == pairs)(functools.partial(attend, pairs))

        @pl.when(count == 0)
        def _():
            all_ref[ks, :] = jnp.zeros((TILE, all_ref.shape[1]), BF)

        return carry

    lax.fori_loop(0, count_blocks, key_block, 0)
    rest = jnp.zeros((TILE - HEAD_DIM, slots), BF)
    for h in range(HEADS):
        place = wide + h * TILE
        all_ref[:, place : place + TILE] = jnp.concatenate(
            [dqt_ref[h].astype(BF), rest], axis=0
        ).T
    x_copy.wait()
    layer_copy.wait()
    layer_copy = pltpu.make_async_copy(layer_ref, layer_out, sems.at[5])
    layer_copy.start()
    gain = gains_ref[8:9]
    for copy in weights[groups:]:
        copy.wait()
    backs = [mm(all_ref[rows, :], w_ref[...], NT) for rows in blocks]
    outs = []
    total = None
    for i, (rows, back) in enumerate(zip(blocks, backs)):
        value = x_ref[rows, :]
        factor = rms_factor(value)
        weighted = back * gain
        grad = gh_ref[rows, :] + (
            factor * weighted
            - value
            * (factor * factor * factor)
            * jnp.mean(weighted * value, axis=-1, keepdims=True)
        )
        ig_ref[rows, :] = jnp.where(
            qa_ref[rows, IS_PROMPT : IS_PROMPT + 1].astype(F32) > 0, 0.0, grad
        )
        copy = pltpu.make_async_copy(ig_ref.at[rows], ig_out.at[rows], out_sem.at[i])
        copy.start()
        outs.append(copy)
        upper = grad.astype(BF)
        lower = (grad - upper.astype(F32)).astype(BF)
        hot = marks_ref[rows, :]
        part = mm(hot, upper, TN) + mm(hot, lower, TN)
        total = part if total is None else total + part
    pg_ref[...] = total
    layer_copy.wait()
    for copy in outs:
        copy.wait()


def backward_call(
    lo, hi, gh, lse, qa, ka, marks, gains, kv, w, q, ctx, x, tiles, layer_output
):
    slots, width = gh.shape
    groups = w.shape[0]
    return pl.pallas_call(
        backward_kernel,
        in_specs=[SMEM_SPEC] * 2 + [VMEM_SPEC] * 6 + [ANY_SPEC] * 7,
        out_specs=[ANY_SPEC, VMEM_SPEC, ANY_SPEC],
        out_shape=[
            jax.ShapeDtypeStruct((slots, width), F32),
            jax.ShapeDtypeStruct((TILE, width), F32),
            jax.ShapeDtypeStruct((slots, width), BF),
        ],
        scratch_shapes=[
            pltpu.VMEM(kv.shape, BF),
            pltpu.VMEM((w.shape[1], groups * w.shape[2]), BF),
            pltpu.VMEM(q.shape, BF),
            pltpu.VMEM(ctx.shape, BF),
            pltpu.VMEM(x.shape, F32),
            pltpu.VMEM(tiles.shape, F32),
            pltpu.VMEM(layer_output.shape, BF),
            pltpu.VMEM((slots, 2 * HEADS * TILE), BF),
            pltpu.VMEM((HEADS, HEAD_DIM, slots), BF),
            pltpu.VMEM((16, slots), F32),
            pltpu.VMEM((HEADS, HEAD_DIM, slots), F32),
            pltpu.VMEM((slots, width), F32),
            pltpu.SemaphoreType.DMA((2 * groups + 6,)),
            pltpu.SemaphoreType.DMA((slots // BLK,)),
        ],
        compiler_params=pltpu.CompilerParams(vmem_limit_bytes=VMEM_LIMIT),
        name="attend_back",
    )(lo, hi, gh, lse, qa, ka, marks, gains, kv, w, q, ctx, x, tiles, layer_output)


def slot_arrays(segments, live):
    slots = segments.shape[0]
    place = jnp.arange(slots, dtype=jnp.int32)
    first = jnp.sum((segments[None, :] < segments[:, None]).astype(jnp.int32), axis=1)
    position = place - first
    alive = live[:, None] == 1
    is_prompt = alive & (position < PROMPT)[:, None]
    lane = jnp.arange(TILE, dtype=jnp.int32)[None, :]
    marks = ((position[:, None] == lane) & is_prompt).astype(BF)
    same = segments[:, None] == lane
    query_side = jnp.where(lane == ALIVE, alive, same)
    query_side = jnp.where(lane == IS_PROMPT, is_prompt, query_side).astype(BF)
    key_side = jnp.where((lane < 16) & jnp.logical_not(same & alive), MASKED, 0.0).astype(BF)
    by_block = segments.reshape(-1, TILE)
    top = jnp.max(jnp.where(live.reshape(-1, TILE) == 1, by_block, -1), axis=1)
    hi = jnp.sum((segments[None, :] <= top[:, None]) & (live[None, :] == 1), axis=1)
    hi = (hi.astype(jnp.int32) + TILE - 1) // TILE
    lo = jnp.sum((segments[None, :] < by_block[:, :1]).astype(jnp.int32), axis=1) // TILE
    return marks, query_side, key_side, jnp.minimum(lo, hi)[None], hi[None]


def bias_tiles(table):
    place = jnp.arange(TILE, dtype=jnp.int32)
    kinds = jnp.arange(-2, 3, dtype=jnp.int32)[:, None, None] * TILE
    offset = jnp.clip(kinds + place[None, None, :] - place[None, :, None], -TILE, TILE)
    both = []
    for sign in (1, -1):
        both.append(
            table.astype(F32)[bucket_of(sign * offset, BUCKETS // 2)].transpose(3, 0, 1, 2) * LOG2E
        )
    return both


def tiles_of(first, second):
    rows = first.shape[0]
    shaped = [part.reshape(rows, -1, 1, HEAD_DIM) for part in (first, second)]
    return jnp.concatenate(shaped, axis=2).reshape(rows, -1)


def open_plain(
    tok, prompt, seg, live, w_query, w_key, w_value, w_output, w_inner, w_outer, gain_attn,
    gain_ffn, rel_table,
):
    slots, width = tok.shape
    packs = jnp.stack(
        [
            jnp.concatenate([tiles_of(w_key, w_value), tiles_of(w_query, w_output.T)], axis=1),
            w_inner,
            w_outer.T,
        ]
    )
    weights = lax.all_gather(lax.all_gather(packs, "dp", axis=1, tiled=True), "mp", axis=1)
    prompt_all = lax.all_gather(prompt.astype(BF), ("dp", "mp"), tiled=True)
    prompt_all = jnp.pad(prompt_all.reshape(PROMPT, width), ((0, TILE - PROMPT), (0, 0)))
    gains = lax.all_gather(jnp.stack([gain_attn, gain_ffn]), "dp", axis=1, tiled=True)
    gains = jnp.pad(gains.astype(F32), ((8, 6), (0, 0)))
    ahead, behind = bias_tiles(lax.all_gather(rel_table, "mp", axis=1, tiled=True))
    marks, query_side, key_side, lo, hi = slot_arrays(seg, live)
    placed = jnp.dot(marks, prompt_all, preferred_element_type=F32)
    x = jnp.where(query_side[:, IS_PROMPT:] > 0, placed, tok.astype(F32))
    normed = (x * rms_factor(x) * gains[8:9]).astype(BF)
    out = jnp.einsum("sd,mdc->smc", normed, weights[0], preferred_element_type=F32)
    half = out.shape[2] // 2
    kv = out[:, :, :half].astype(BF).reshape(slots, -1)
    q = jnp.where(low_lanes(half), out[:, :, half:] * LOG2E, 0.0).astype(BF).reshape(slots, -1)
    return weights, x, kv, q, ahead, behind, marks, query_side, key_side, gains, lo, hi


def adam_kernel(
    part_ref, state_ref, out_ref, low_ref, land_one, land_two, mid_ref, send_one, recv_one,
    send_two, recv_two,
):
    dp = lax.axis_index("dp")
    mp = lax.axis_index("mp")
    wide = part_ref.shape[0]
    deep = mid_ref.shape[0]
    width = part_ref.shape[2]
    low_ref[...] = part_ref[...].astype(BF)
    barrier = pltpu.get_barrier_semaphore()
    peers = [{"dp": lax.rem(dp + s, wide)} for s in range(1, wide)]
    peers += [{"mp": lax.rem(mp + s, deep)} for s in range(1, deep)]
    for peer in peers:
        pl.semaphore_signal(barrier, inc=1, device_id=peer, device_id_type=MESH)
    pl.semaphore_wait(barrier, len(peers))
    first = []
    for s in range(1, wide):
        to = lax.rem(dp + s, wide)
        copy = pltpu.make_async_remote_copy(
            src_ref=low_ref.at[to], dst_ref=land_one.at[s - 1],
            send_sem=send_one.at[s - 1], recv_sem=recv_one.at[s - 1],
            device_id={"dp": to}, device_id_type=MESH,
        )
        copy.start()
        first.append(copy)
    total = part_ref[dp]
    for s, copy in enumerate(first):
        copy.wait_recv()
        total = total + land_one[s].astype(F32)
    for m in range(deep):
        mid_ref[m, 0:4] = total[4 * m : 4 * m + 4]
        mid_ref[m, 4:8] = jnp.zeros((4, width), F32)
    second = []
    for s in range(1, deep):
        to = lax.rem(mp + s, deep)
        copy = pltpu.make_async_remote_copy(
            src_ref=mid_ref.at[to], dst_ref=land_two.at[s - 1],
            send_sem=send_two.at[s - 1], recv_sem=recv_two.at[s - 1],
            device_id={"mp": to}, device_id_type=MESH,
        )
        copy.start()
        second.append(copy)
    window = mid_ref[mp]
    for s, copy in enumerate(second):
        copy.wait_recv()
        window = window + land_two[s]
    begin = width // 8 * lax.rem(dp * deep + mp, 8)
    turned = pltpu.roll(window, lax.rem(width - begin, width), 1)
    lane = lax.broadcasted_iota(jnp.int32, (8, width), 1)
    grad = jnp.where(lane < width - begin, turned, pltpu.roll(turned, 7, 0))
    updated = adam_step(grad, state_ref[0], state_ref[1], state_ref[2])
    for i, value in enumerate(updated):
        out_ref[i] = value
    for copy in first + second:
        copy.wait_send()


def adam_step(grad, prompt, moment_one, moment_two):
    first_new = 0.9 * moment_one + 0.1 * grad
    second_new = 0.999 * moment_two + 0.001 * grad * grad
    correct_one = 1.0 - 0.9**ADAM_STEP
    correct_two = 1.0 - 0.999**ADAM_STEP
    prompt_new = prompt - 0.3 * (first_new / correct_one) / (
        jnp.sqrt(second_new / correct_two) + 1e-08
    )
    return prompt_new, first_new, second_new


def adam_call(part, state, deep):
    wide, rows, width = part.shape
    return pl.pallas_call(
        adam_kernel,
        in_specs=[VMEM_SPEC] * 2,
        out_specs=VMEM_SPEC,
        out_shape=jax.ShapeDtypeStruct(state.shape, F32),
        scratch_shapes=[
            pltpu.VMEM(part.shape, BF),
            pltpu.VMEM((wide - 1, rows, width), BF),
            pltpu.VMEM((deep - 1, 8, width), F32),
            pltpu.VMEM((deep, 8, width), F32),
            pltpu.SemaphoreType.DMA((wide - 1,)),
            pltpu.SemaphoreType.DMA((wide - 1,)),
            pltpu.SemaphoreType.DMA((deep - 1,)),
            pltpu.SemaphoreType.DMA((deep - 1,)),
        ],
        compiler_params=pltpu.CompilerParams(collective_id=1, has_side_effects=True),
        name="sum_and_step",
    )(part, state)


def body(
    dp, mp, tokens, prompt, moment_one, moment_two, segments, live, out_grad, w_query, w_key,
    w_value, w_output, w_inner, w_outer, gain_attn, gain_ffn, rel_table,
):
    _, slots, width = tokens.shape
    tuned = (dp, mp) == (8, 4)
    share = prompt.shape[0]
    if tuned:
        line = 8 * width
        state = functools.reduce(
            jnp.add,
            [
                jnp.pad(part, (i * line, (3 - i) * line - share))
                for i, part in enumerate((prompt, moment_one, moment_two))
            ],
        ).reshape(3, 8, width)
        (
            w, trio, last, x, kv, q, ahead, behind, marks, query_side, key_side, gains, lo, hi,
        ) = open_call(
            state, gain_attn[None], gain_ffn[None], rel_table.T, w_query, w_key, w_value,
            w_output, w_inner, w_outer.T, segments, live, tokens[0], dp, mp,
        )
        swap = lambda bit: lax.ppermute(trio, "dp", [(i, i ^ bit) for i in range(dp)])
        from_east, from_south = swap(2), swap(4)
        lasted = lax.ppermute(last, "mp", [(1, 0), (2, 3)])
    else:
        (
            weights, x, kv, q, ahead, behind, marks, query_side, key_side, gains, lo, hi,
        ) = open_plain(
            tokens[0], prompt, segments[0], live[0], w_query, w_key, w_value, w_output, w_inner,
            w_outer, gain_attn, gain_ffn, rel_table,
        )
    ctx, lse = attend_call(lo, hi, query_side, key_side, kv, q, ahead)
    if tuned:
        layer_output, grad_hidden = feed_call(
            out_grad[0], query_side, gains, x, ctx, w, trio, from_east, from_south, last,
            lasted,
        )
        w = w.reshape(mp, width, -1)
    else:
        w = weights[0]
        layer_output, grad_hidden = feed_local(
            x, out_grad[0], query_side, gains, ctx, w, weights[1], weights[2]
        )
    input_grad, prompt_part, layer_output = backward_call(
        lo, hi, grad_hidden, lse, query_side, key_side, marks, gains, kv, w, q, ctx, x, behind,
        layer_output,
    )
    if tuned:
        stepped = adam_call(prompt_part.reshape(dp, -1, width), state, mp)
        stepped = stepped.reshape(3, -1)[:, :share]
        prompt_new, first_new, second_new = stepped[0], stepped[1], stepped[2]
    else:
        grad = lax.psum_scatter(
            prompt_part[:PROMPT].reshape(-1), ("dp", "mp"), scatter_dimension=0, tiled=True
        )
        prompt_new, first_new, second_new = adam_step(grad, prompt, moment_one, moment_two)
    return (layer_output[None], input_grad[None], prompt_new, first_new, second_new)


def solution(mesh):
    both = ("dp", "mp")
    return jax.shard_map(
        functools.partial(body, mesh.shape["dp"], mesh.shape["mp"]),
        mesh=mesh,
        in_specs=(
            P(both, None, None),
            P(both),
            P(both),
            P(both),
            P(both, None),
            P(both, None),
            P(both, None, None),
            P("dp", "mp"),
            P("dp", "mp"),
            P("dp", "mp"),
            P("mp", "dp"),
            P("dp", "mp"),
            P("mp", "dp"),
            P("dp"),
            P("dp"),
            P(None, "mp"),
        ),
        out_specs=(
            P(both, None, None),
            P(both, None, None),
            P(both),
            P(both),
            P(both),
        ),
        check_vma=False,
    )
```

```python
import functools

import jax
import jax.numpy as jnp
from jax import lax
from jax.experimental import pallas as pl
from jax.experimental.pallas import tpu as pltpu
from jax.sharding import PartitionSpec as P

HEADS = 12
HEAD_DIM = 64
BUCKETS = 32
PROMPT = 100
ADAM_STEP = 10
BOUNDS = (1, 2, 3, 4, 5, 6, 7, 8, 12, 16, 23, 32, 46, 64, 91)
EPSILON = 1e-06
MASKED = -1e30
LOG2E = 1.4426950408889634
LN2 = 0.6931471805599453
GELU_C = 0.7978845608028654

BLK = 256
TILE = 128
GROUP = 12
ALIVE = 126
IS_PROMPT = 127
BF = jnp.bfloat16
F32 = jnp.float32
NN = (((1,), (0,)), ((), ()))
NT = (((1,), (1,)), ((), ()))
TN = (((0,), (0,)), ((), ()))
MESH = pl.DeviceIdType.MESH
VMEM_LIMIT = 65024 * 1024
SMEM_SPEC = pl.BlockSpec(memory_space=pltpu.SMEM)
VMEM_SPEC = pl.BlockSpec(memory_space=pltpu.VMEM)
ANY_SPEC = pl.BlockSpec(memory_space=pl.ANY)


def mm(left, right, dims):
    return lax.dot_general(left, right, dims, preferred_element_type=F32)


def bucket_of(offset, half):
    distance = jnp.abs(offset)
    counted = sum(((distance >= limit).astype(jnp.int32) for limit in BOUNDS))
    return counted + jnp.where(offset > 0, half, 0).astype(jnp.int32)


def span(block, size=BLK):
    return pl.ds(pl.multiple_of(block * size, size), size)


def low_lanes(width=TILE):
    return lax.rem(lax.broadcasted_iota(jnp.int32, (1, width), 1), TILE) < HEAD_DIM


def fill_bias(line_ref, tiles_ref):
    def one(head, carry):
        row = line_ref[pl.ds(head, 1), :]
        wide = pltpu.roll(
            jnp.broadcast_to(row, (TILE, 4 * TILE)), 0, 1, stride=1, stride_axis=0
        )
        for near in range(1, 4):
            tiles_ref[head, near] = wide[:, near * TILE : (near + 1) * TILE]
        tiles_ref[head, 0] = jnp.broadcast_to(row[:, 0:1], (TILE, TILE))
        tiles_ref[head, 4] = jnp.broadcast_to(row[:, 4 * TILE - 1 :], (TILE, TILE))
        return carry

    lax.fori_loop(0, HEADS, one, 0)


def rms_factor(values):
    return lax.rsqrt(jnp.mean(values * values, axis=-1, keepdims=True) + EPSILON)


def neighbours():
    dp = lax.axis_index("dp")
    core = lax.rem(dp, 2)
    across = lax.rem(lax.div(dp, 2), 2)
    down = lax.div(dp, 4)
    return (
        dp + 1 - 2 * core,
        dp + 2 - 4 * across,
        dp + 4 - 8 * down,
        dp + 6 - 4 * across - 8 * down,
    )


def line_order(z, j):
    upper = lax.div(z, 2)
    return (z, z + 1 - 2 * lax.rem(z, 2), 2 - upper, 3 - 3 * upper)[j]


def flat_shift(rows, shift, width):
    lane = lax.broadcasted_iota(jnp.int32, (8, width), 1)
    turned = pltpu.roll(rows, shift, 1)
    return jnp.where(lane >= shift, turned, pltpu.roll(turned, 1, 0))


def interleave(first, second):
    parts = []
    for at in range(0, first.shape[1], HEAD_DIM):
        parts += [first[:, at : at + HEAD_DIM], second[:, at : at + HEAD_DIM]]
    return jnp.concatenate(parts, axis=1)


def open_kernel(
    state_ref, ga_ref, gf_ref, table_ref, wq_ref, wk_ref, wv_ref, wo_ref, wi_ref, wu_ref,
    seg_ref, live_ref, tok_ref,
    w_out, trio_out, last_out, x_out, kv_out, q_out, ahead_out, behind_out,
    marks_ref, qa_ref, ka_ref, gains_ref, lo_ref, hi_ref,
    small_src, small_v, pack_src, w_v, ff_src, x_v, norm_v, kv_v, q_v, lines_v, ahead_v,
    behind_v,
    own_sem, z_send, z_recv, send, recv, line_send, line_recv, out_sem,
):
    mp = lax.axis_index("mp")
    dp = lax.axis_index("dp")
    depth, wide = w_v.shape[0], w_v.shape[1]
    width = tok_ref.shape[1]
    sib, east, south, corner = neighbours()
    up, down = mp + 1 < depth, mp > 0
    barrier = pltpu.get_barrier_semaphore()

    def greet(peer):
        pl.semaphore_signal(barrier, inc=1, device_id=peer, device_id_type=MESH)

    for peer in (sib, east, south):
        greet({"dp": peer})
    pl.when(up)(lambda: greet({"mp": mp + 1}))
    pl.when(down)(lambda: greet({"mp": mp - 1}))

    share = lax.rem(dp * depth + mp, 8)
    part = ga_ref.shape[1]
    empty = jnp.zeros((1, width - part), F32)
    gain_rows = [
        pltpu.roll(jnp.concatenate([ref[...].astype(F32), empty], axis=1), part * dp, 1)
        for ref in (ga_ref, gf_ref)
    ]
    table_rows = jnp.concatenate(
        [table_ref[...].astype(F32), jnp.zeros((HEADS // depth, width // 2 - BUCKETS), F32)],
        axis=1,
    )
    window = flat_shift(state_ref[0], part * share, width)
    mid = width // 2
    small_src[...] = jnp.concatenate(
        [window[0:4, :mid], window[0:4, mid:]]
        + [row[:, :mid] for row in gain_rows]
        + [row[:, mid:] for row in gain_rows]
        + [table_rows, jnp.zeros((4 - HEADS // depth, mid), F32)],
        axis=0,
    ).astype(BF)
    pack_src[...] = jnp.concatenate(
        [interleave(wk_ref[...], wv_ref[...]), interleave(wq_ref[...], wo_ref[...].T)], axis=1
    )
    ff_src[0] = wi_ref[...]
    ff_src[1] = wu_ref[...]
    pl.semaphore_wait(barrier, 3 + up.astype(jnp.int32) + down.astype(jnp.int32))

    def remote(src, dst, send_sem, recv_sem, peer):
        return pltpu.make_async_remote_copy(
            src_ref=src, dst_ref=dst, send_sem=send_sem, recv_sem=recv_sem,
            device_id=peer, device_id_type=MESH,
        )

    started = []
    local = []
    units = [(small_src, small_v), (pack_src, w_v)]

    def along(u, j, src):
        dst = units[u][1]
        z = line_order(mp, j)
        copies = []
        for at, (ahead, there, move) in enumerate(((up, z <= mp, 1), (down, z >= mp, -1))):
            copy = remote(
                src, dst.at[z, dp], z_send.at[u, j, at], z_recv.at[u, z], {"mp": mp + move}
            )
            copies.append((jnp.logical_and(ahead, there), copy))
        return copies

    lined = []

    def launch(copies):
        for condition, copy in copies:
            pl.when(condition)(copy.start)
        lined.extend(copies)

    def push(u, o, kind, src, dst, peer):
        copy = remote(src, dst, send.at[u, o, kind], recv.at[u, o, kind], peer)
        copy.start()
        started.append(copy)

    def landed(u, o, kind, dst):
        remote(dst, dst, send.at[u, o, kind], recv.at[u, o, kind], {"dp": sib}).wait_recv()

    def step(u, o):
        src, dst = units[u]
        z = line_order(mp, o)
        block = dst.at[z, dp]
        if o:
            remote(block, block, z_send.at[u, o, 0], z_recv.at[u, z], {"dp": sib}).wait_recv()
            src = block
        launch(along(u, o, src))
        push(u, o, 0, src, block, {"dp": east})
        push(u, o, 1, src, block, {"dp": south})
        push(u, o, 2, src, block, {"dp": sib})

    def forward(u, o):
        dst = units[u][1]
        z = line_order(mp, o)
        rows = dst.shape[2] // 2 if u else dst.shape[2]
        landed(u, o, 0, dst.at[z, east])
        push(u, o, 3, dst.at[z, east, 0:rows], dst.at[z, east, 0:rows], {"dp": south})
        push(u, o, 4, dst.at[z, east], dst.at[z, east], {"dp": sib})
        landed(u, o, 1, dst.at[z, south])
        if u:
            push(u, o, 5, dst.at[z, south, rows:], dst.at[z, south, rows:], {"dp": east})
        push(u, o, 6, dst.at[z, south], dst.at[z, south], {"dp": sib})

    def finish(u, o):
        dst = units[u][1]
        z = line_order(mp, o)
        rows = dst.shape[2] // 2 if u else dst.shape[2]
        landed(u, o, 3, dst.at[z, corner, 0:rows])
        if u:
            landed(u, o, 5, dst.at[z, corner, rows:])
        push(u, o, 7, dst.at[z, corner], dst.at[z, corner], {"dp": sib})

    flip = 1 - 2 * lax.rem(dp, 2)

    def complete(u, o):
        dst = units[u][1]
        z = line_order(mp, o)
        landed(u, o, 2, dst.at[z, sib])
        landed(u, o, 4, dst.at[z, east + flip])
        landed(u, o, 6, dst.at[z, south + flip])
        landed(u, o, 7, dst.at[z, corner + flip])

    for u in range(2):
        step(u, 0)
        src, dst = units[u]
        copy = pltpu.make_async_copy(src, dst.at[mp, dp], own_sem.at[u])
        copy.start()
        local.append(copy)
    own_copy = pltpu.make_async_copy(ff_src, trio_out.at[0], own_sem.at[2])
    own_copy.start()
    partner = line_order(mp, 1)
    across = depth - 1 - mp
    inside = lax.rem(lax.div(mp + 1, 2), 2) == 1
    at_end = jnp.logical_not(inside)

    def line_copy(src, dst, at, at_recv, to):
        return remote(src, dst, line_send.at[at], line_recv.at[at_recv], {"mp": to})

    pair_copy = line_copy(ff_src, trio_out.at[1], 0, 0, partner)
    over_copy = line_copy(ff_src, trio_out.at[2], 1, 1, across)
    far_copy = line_copy(trio_out.at[1], last_out, 2, 2, across)
    back_copy = line_copy(trio_out.at[2], trio_out.at[2], 3, 1, partner)

    slots = tok_ref.shape[0]
    segment_row = seg_ref[...].astype(F32)
    live_row = live_ref[...].astype(F32)
    lane = lax.broadcasted_iota(jnp.int32, (slots, TILE), 1)
    lane_f = lane.astype(F32)
    segment = jnp.broadcast_to(segment_row, (TILE, slots)).T
    alive = jnp.broadcast_to(live_row, (TILE, slots)).T
    same = segment == lane_f
    start = jnp.sum((segment < lane_f).astype(F32), axis=0, keepdims=True)
    first = jnp.sum(jnp.where(same, start, 0.0), axis=1, keepdims=True)
    position = lax.broadcasted_iota(jnp.int32, (slots, 1), 0).astype(F32) - first
    prompt_slot = (alive > 0) & (position < PROMPT)
    sides = jnp.where(lane == ALIVE, alive, same.astype(F32))
    qa_ref[...] = jnp.where(lane == IS_PROMPT, prompt_slot.astype(F32), sides).astype(BF)
    ka_ref[...] = jnp.where(
        (lane < 16) & jnp.logical_not(same & (alive > 0)), MASKED, 0.0
    ).astype(BF)
    step(0, 1)
    forward(0, 0)
    step(0, 2)
    step(1, 1)
    forward(1, 0)
    forward(0, 1)
    finish(0, 0)
    step(0, 3)
    forward(0, 2)
    finish(0, 1)

    def window_rows(device, inside):
        target = 25 * lax.div(device, 8) + 3 * lax.rem(device, 8) + inside
        return jnp.where(inside < 4, target, -1).astype(F32)

    at = lax.broadcasted_iota(jnp.int32, (1, TILE), 1)
    target = window_rows(lax.div(at, 4), lax.rem(at, 4))
    marks_ref[...] = jnp.where((position == target) & prompt_slot, 1.0, 0.0).astype(BF)
    forward(0, 3)
    finish(0, 2)
    step(1, 2)
    forward(1, 1)
    finish(0, 3)
    finish(1, 0)
    block_lane = lax.broadcasted_iota(jnp.int32, (8, TILE), 1)
    lows = jnp.zeros((8, TILE), F32)
    highs = jnp.zeros((8, TILE), F32)
    for block in range(slots // TILE):
        here = segment_row[:, block * TILE : (block + 1) * TILE]
        lives = live_row[:, block * TILE : (block + 1) * TILE] > 0
        top = jnp.max(jnp.where(lives, here, -1.0), axis=1, keepdims=True)
        bottom = jnp.min(here, axis=1, keepdims=True)
        before = jnp.sum((segment_row < bottom).astype(F32), axis=1, keepdims=True)
        through = (segment_row <= top) & (live_row > 0)
        through = jnp.sum(through.astype(F32), axis=1, keepdims=True)
        lows = jnp.where(block_lane == block, before, lows)
        highs = jnp.where(block_lane == block, through, highs)
    highs = lax.div(highs.astype(jnp.int32) + TILE - 1, TILE)
    hi_ref[...] = highs
    lo_ref[...] = jnp.minimum(lax.div(lows.astype(jnp.int32), TILE), highs)
    for o in range(depth):
        complete(0, o)
    local[0].wait()

    gains = functools.reduce(jnp.add, [small_v[0, d].astype(F32) for d in range(wide)])
    attn_gain = jnp.concatenate([gains[8:9], gains[10:11]], axis=1)
    ffn_gain = jnp.concatenate([gains[9:10], gains[11:12]], axis=1)
    gains_ref[...] = jnp.concatenate(
        [jnp.zeros((8, width), F32), attn_gain, ffn_gain, jnp.zeros((6, width), F32)], axis=0
    )
    rows_all = depth * wide * 16
    at = lax.broadcasted_iota(jnp.int32, (1, rows_all), 1)
    holder = lax.div(at, 16)
    holder = lax.rem(holder, wide) * depth + lax.div(holder, wide)
    left = window_rows(holder, lax.rem(at, 16))
    right = window_rows(holder, lax.rem(at + 12, 16))
    windows = small_v[...].reshape(rows_all, mid)
    gain = attn_gain

    def embed(f):
        rows = slice(f, f + BLK)
        hots = [(position[rows] == target).astype(F32).astype(BF) for target in (left, right)]
        placed = jnp.concatenate([mm(hot, windows, NN) for hot in hots], axis=1)
        value = jnp.where(prompt_slot[rows, 0:1], placed, tok_ref[rows, :].astype(F32))
        x_v[rows, :] = value
        norm_v[rows, :] = (value * rms_factor(value) * gain).astype(BF)

    for f in range(0, slots, BLK):
        embed(f)
        if f == slots // 2 - BLK:
            step(1, 3)
            pair_copy.start()
            pl.when(inside)(over_copy.start)
            forward(1, 2)
            finish(1, 1)
    copy = pltpu.make_async_copy(x_v, x_out, out_sem.at[0])
    copy.start()
    local.append(copy)

    half = w_v.shape[3] // 2
    low = low_lanes(half)

    def project(o):
        complete(1, o)
        if o == 0:
            local[1].wait()
        z = line_order(mp, o)
        copy = pltpu.make_async_copy(w_v.at[z], w_out.at[z], out_sem.at[1 + o])
        copy.start()
        local.append(copy)
        weight = w_v[z].reshape(wide * w_v.shape[2], 2 * half)
        cols = span(z, half)
        parts = [mm(norm_v[f : f + BLK, :], weight, NN) for f in range(0, slots, BLK)]
        for i, piece in enumerate(parts):
            rows = slice(i * BLK, (i + 1) * BLK)
            kv_v[rows, cols] = piece[:, :half].astype(BF)
            q_v[rows, cols] = jnp.where(low, piece[:, half:] * LOG2E, 0.0).astype(BF)
        for at_sem, (src, dst) in enumerate(((kv_v, kv_out), (q_v, q_out))):
            copy = pltpu.make_async_copy(
                src.at[:, cols], dst.at[:, cols], out_sem.at[1 + depth + 2 * o + at_sem]
            )
            copy.start()
            local.append(copy)

    table = jnp.concatenate(
        [small_v[m, 0].astype(F32)[12 : 12 + HEADS // depth, 0:TILE] for m in range(depth)]
        + [jnp.zeros((16 - HEADS, TILE), F32)],
        axis=0,
    ).astype(BF)
    offset = lax.broadcasted_iota(jnp.int32, (1, 4 * TILE), 1) - 2 * TILE
    code = lax.broadcasted_iota(jnp.int32, (TILE, 4 * TILE), 0)
    def bias_out(at_sem, sign, tiles, out):
        hot = (code == bucket_of(sign * offset, BUCKETS // 2)).astype(F32).astype(BF)
        lines_v[...] = mm(table, hot, NN) * LOG2E
        fill_bias(lines_v, tiles)
        copy = pltpu.make_async_copy(tiles, out, out_sem.at[1 + 3 * depth + at_sem])
        copy.start()
        local.append(copy)

    bias_out(0, 1, ahead_v, ahead_out)
    forward(1, 3)
    finish(1, 2)
    @pl.when(inside)
    def _():
        pair_copy.wait_recv()
        far_copy.start()
        over_copy.wait_recv()
        back_copy.start()

    project(0)
    finish(1, 3)
    project(1)
    project(2)
    bias_out(1, -1, behind_v, behind_out)
    project(3)
    own_copy.wait()
    pair_copy.wait_send()

    @pl.when(at_end)
    def _():
        pair_copy.wait_recv()
        back_copy.wait_recv()

    @pl.when(inside)
    def _():
        over_copy.wait_send()
        far_copy.wait()
        back_copy.wait_send()

    for copy in local[2:]:
        copy.wait()
    for copy in started:
        copy.wait_send()
    for condition, copy in lined:
        pl.when(condition)(copy.wait_send)


def open_call(state, ga, gf, table, wq, wk, wv, wo, wi, wu, seg, live, tok, dp, mp):
    slots, width = tok.shape
    rows = wi.shape[0]
    wide = HEADS * TILE
    pack = (rows, width)
    shape = jax.ShapeDtypeStruct
    dma = pltpu.SemaphoreType.DMA
    tiles = (HEADS, 5, TILE, TILE)
    return pl.pallas_call(
        open_kernel,
        in_specs=[VMEM_SPEC] * 13,
        out_specs=[ANY_SPEC] * 8 + [VMEM_SPEC] * 6,
        out_shape=[
            shape((mp, dp) + pack, BF),
            shape((3, 2) + pack, BF),
            shape((2,) + pack, BF),
            shape((slots, width), F32),
            shape((slots, wide), BF),
            shape((slots, wide), BF),
            shape(tiles, F32),
            shape(tiles, F32),
            shape((slots, TILE), BF),
            shape((slots, TILE), BF),
            shape((slots, TILE), BF),
            shape((16, width), F32),
            shape((8, TILE), jnp.int32),
            shape((8, TILE), jnp.int32),
        ],
        scratch_shapes=[
            pltpu.VMEM((16, width // 2), BF),
            pltpu.VMEM((mp, dp, 16, width // 2), BF),
            pltpu.VMEM(pack, BF),
            pltpu.VMEM((mp, dp) + pack, BF),
            pltpu.VMEM((2,) + pack, BF),
            pltpu.VMEM((slots, width), F32),
            pltpu.VMEM((slots, width), BF),
            pltpu.VMEM((slots, wide), BF),
            pltpu.VMEM((slots, wide), BF),
            pltpu.VMEM((16, 4 * TILE), F32),
            pltpu.VMEM(tiles, F32),
            pltpu.VMEM(tiles, F32),
            dma((3,)),
            dma((2, mp, 2)),
            dma((2, mp)),
            dma((2, mp, 8)),
            dma((2, mp, 8)),
            dma((4,)),
            dma((3,)),
            dma((3 + 3 * mp,)),
        ],
        compiler_params=pltpu.CompilerParams(
            collective_id=0, has_side_effects=True, vmem_limit_bytes=VMEM_LIMIT
        ),
        cost_estimate=pl.CostEstimate(
            flops=16 * 10**9, bytes_accessed=40 * 10**6, transcendentals=0
        ),
        name="open_layer",
    )(state, ga, gf, table, wq, wk, wv, wo, wi, wu, seg, live, tok)


def window_of(lo_ref, hi_ref, block, blocks):
    lo = lo_ref[0, block]
    pairs = lax.div(hi_ref[0, block] - lo + 1, 2)
    return jnp.minimum(lo, blocks - 2 * pairs), pairs


def bias_row(tiles_ref, head, first, block, pairs):
    return jnp.concatenate(
        [
            tiles_ref[head, jnp.clip(first + j - block, -2, 2) + 2]
            for j in range(2 * pairs)
        ],
        axis=1,
    )


def attend_kernel(
    lo_ref, hi_ref, qa_ref, ka_ref, kv_hbm, q_hbm, tiles_hbm,
    ctx_out, lse_ref,
    kv_ref, val_ref, q_ref, ctx_ref, tiles_ref, lsem_ref, mean_ref, sems, ctx_sems,
):
    slots = qa_ref.shape[0]
    blocks = slots // TILE
    copies = [
        pltpu.make_async_copy(src, dst, sems.at[i])
        for i, (src, dst) in enumerate(
            ((kv_hbm, kv_ref), (q_hbm, q_ref), (tiles_hbm, tiles_ref))
        )
    ]
    for copy in copies:
        copy.start()
    copies[0].wait()
    mean_ref[...] = mm(jnp.full((8, slots), 1.0 / slots, BF), kv_ref[...], NN)
    high = jnp.logical_not(low_lanes())
    ones = jnp.ones((slots, TILE), BF)
    for h in range(HEADS):
        cols = slice(h * TILE, (h + 1) * TILE)
        val_ref[:, cols] = jnp.where(high, kv_ref[:, cols], ones)
    lane = lax.broadcasted_iota(jnp.int32, (1, TILE), 1)
    copies[1].wait()
    copies[2].wait()

    def query_block(qb, carry):
        qs = span(qb, TILE)
        first, count = window_of(lo_ref, hi_ref, qb, blocks)
        alive = qa_ref[qs, ALIVE : ALIVE + 1].astype(F32) > 0
        lsem_ref[...] = jnp.zeros_like(lsem_ref)

        def attend(pairs):
            size = 2 * pairs * TILE
            ks = pl.ds(pl.multiple_of(first * TILE, TILE), size)
            mask = mm(qa_ref[qs, :], ka_ref[ks, :], NT)

            def group_body(g, inner):
                heads = [g * GROUP + i for i in range(GROUP)]
                cols = [span(h, TILE) for h in heads]
                scores = [
                    mm(q_ref[qs, c], kv_ref[ks, c], NT)
                    + (bias_row(tiles_ref, h, first, qb, pairs) + mask)
                    for h, c in zip(heads, cols)
                ]
                tops = [jnp.max(row, axis=1, keepdims=True) for row in scores]
                weights = [jnp.exp2(row - top).astype(BF) for row, top in zip(scores, tops)]
                for h, c, top, weight in zip(heads, cols, tops, weights):
                    both = mm(weight, val_ref[ks, c], NN)
                    context = both / pltpu.roll(both, HEAD_DIM, 1)
                    context = jnp.where(alive, context, mean_ref[0:1, c])
                    ctx_ref[qs, c] = jnp.where(high, context, 0.0).astype(BF)
                    lsem_ref[...] = jnp.where(
                        (lane == h) & alive, top + jnp.log2(both), lsem_ref[...]
                    )
                return inner

            lax.fori_loop(0, HEADS // GROUP, group_body, 0)

        for pairs in range(1, blocks // 2 + 1):
            pl.when(count == pairs)(functools.partial(attend, pairs))

        @pl.when(count == 0)
        def _():
            every = jnp.logical_not(low_lanes(HEADS * TILE))
            ctx_ref[qs, :] = jnp.broadcast_to(
                jnp.where(every, mean_ref[0:1, :], 0.0), (TILE, HEADS * TILE)
            ).astype(BF)

        lse_ref[:, qs] = lsem_ref[...].T[0:16]
        pltpu.make_async_copy(ctx_ref.at[qs], ctx_out.at[qs], ctx_sems.at[qb]).start()
        return carry

    lax.fori_loop(0, blocks, query_block, 0)
    for b in range(blocks):
        rows = slice(b * TILE, (b + 1) * TILE)
        pltpu.make_async_copy(ctx_ref.at[rows], ctx_out.at[rows], ctx_sems.at[b]).wait()


def attend_call(lo, hi, qa, ka, kv, q, tiles):
    slots, wide = kv.shape
    return pl.pallas_call(
        attend_kernel,
        in_specs=[SMEM_SPEC] * 2 + [VMEM_SPEC] * 2 + [ANY_SPEC] * 3,
        out_specs=[ANY_SPEC, VMEM_SPEC],
        out_shape=[
            jax.ShapeDtypeStruct((slots, wide), BF),
            jax.ShapeDtypeStruct((16, slots), F32),
        ],
        scratch_shapes=[
            pltpu.VMEM((slots, wide), BF),
            pltpu.VMEM((slots, wide), BF),
            pltpu.VMEM((slots, wide), BF),
            pltpu.VMEM((slots, wide), BF),
            pltpu.VMEM(tiles.shape, F32),
            pltpu.VMEM((TILE, TILE), F32),
            pltpu.VMEM((8, wide), F32),
            pltpu.SemaphoreType.DMA((3,)),
            pltpu.SemaphoreType.DMA((slots // TILE,)),
        ],
        compiler_params=pltpu.CompilerParams(vmem_limit_bytes=VMEM_LIMIT),
        cost_estimate=pl.CostEstimate(
            flops=25 * 10**9, bytes_accessed=10**7, transcendentals=10**7
        ),
        name="attend",
    )(lo, hi, qa, ka, kv, q, tiles)


def gelu_both(inner, upstream):
    square = inner * inner
    bent = jnp.tanh(inner * (GELU_C + (GELU_C * 0.044715) * square))
    half = 0.5 + 0.5 * bent
    activated = inner * half
    slope = half + activated * ((1.0 - half) * (2 * GELU_C + (6 * GELU_C * 0.044715) * square))
    return activated.astype(BF), (upstream * slope).astype(BF)


def feed_kernel(
    og_ref, qa_ref, gains_ref, x_hbm, ctx_hbm, w_hbm, trio_hbm, east_hbm, south_hbm, last_hbm,
    lasted_hbm,
    out_hbm, gh_hbm,
    ff_v, ctx_ref, w_ref, x_ref, norm_ref, gb_ref, hid_ref, br_ref, dn_ref, out_ref, gh_ref,
    sems, fill, send, recv, out_sem,
):
    dp = lax.axis_index("dp")
    mp = lax.axis_index("mp")
    depth, wide = ff_v.shape[0], ff_v.shape[1]
    half = w_hbm.shape[3] // 2
    rows_half = ff_v.shape[3] // 2
    sib, east, south, corner = neighbours()
    flip = 1 - 2 * lax.rem(dp, 2)
    upper, lower = pl.ds(0, rows_half), pl.ds(rows_half, rows_half)
    inside = lax.rem(lax.div(mp + 1, 2), 2) == 1
    barrier = pltpu.get_barrier_semaphore()
    for peer in (sib, east, south):
        pl.semaphore_signal(barrier, inc=1, device_id={"dp": peer}, device_id_type=MESH)
    first = [
        pltpu.make_async_copy(ctx_hbm, ctx_ref, sems.at[0]),
        pltpu.make_async_copy(x_hbm, x_ref, sems.at[1]),
    ]
    for m in range(depth):
        first.append(
            pltpu.make_async_copy(
                w_hbm.at[m, :, :, half:],
                w_ref.at[:, :, m * half : (m + 1) * half],
                sems.at[2 + m],
            )
        )
    end = depth - 1
    for here, source in ((inside, last_hbm), (jnp.logical_not(inside), lasted_hbm)):
        pl.when(here)(pltpu.make_async_copy(source, ff_v.at[end, dp], fill.at[end, 0]).start)
    for copy in first:
        copy.start()
    pl.semaphore_wait(barrier, 3)

    def remote(src, dst, j, kind, peer):
        return pltpu.make_async_remote_copy(
            src_ref=src, dst_ref=dst, send_sem=send.at[j, kind], recv_sem=recv.at[j, kind],
            device_id={"dp": peer}, device_id_type=MESH,
        )

    sent = []

    def push(src, dst, j, kind, peer):
        copy = remote(src, dst, j, kind, peer)
        copy.start()
        sent.append(copy)

    def awaited(block, j, kind):
        remote(block, block, j, kind, sib).wait_recv()

    def relay(j, from_east, from_south):
        push(from_east.at[:, upper], ff_v.at[j, east, :, upper], j, 0, south)
        push(from_south.at[:, lower], ff_v.at[j, south, :, lower], j, 1, east)
        push(from_east, ff_v.at[j, east], j, 2, sib)
        push(from_south, ff_v.at[j, south], j, 3, sib)

    for j in range(end):
        relay(j, east_hbm.at[j], south_hbm.at[j])
        push(trio_hbm.at[j], ff_v.at[j, dp], j, 7, sib)
        for kind, (src, place) in enumerate(
            ((trio_hbm, dp), (east_hbm, east), (south_hbm, south))
        ):
            pltpu.make_async_copy(src.at[j], ff_v.at[j, place], fill.at[j, kind]).start()

    def spread(j):
        block = ff_v.at[j, dp]
        pltpu.make_async_copy(block, block, fill.at[j, 0]).wait()
        for kind, peer in ((5, east), (6, south), (7, sib)):
            push(block, block, j, kind, peer)

    spread(end)

    def pass_on(j):
        awaited(ff_v.at[j, east], j, 5)
        awaited(ff_v.at[j, south], j, 6)
        relay(j, ff_v.at[j, east], ff_v.at[j, south])

    def corners(j):
        block = ff_v.at[j, corner]
        awaited(ff_v.at[j, corner, :, upper], j, 0)
        awaited(ff_v.at[j, corner, :, lower], j, 1)
        push(block, block, j, 4, sib)

    def landed(j):
        for kind, place in ((2, east + flip), (3, south + flip), (4, corner + flip)):
            awaited(ff_v.at[j, place], j, kind)
        if j < end:
            for kind, place in enumerate((dp, east, south)):
                block = ff_v.at[j, place]
                pltpu.make_async_copy(block, block, fill.at[j, kind]).wait()
        awaited(ff_v.at[j, sib], j, 7)

    slots = og_ref.shape[0]
    gain = gains_ref[9:10]
    blocks = [slice(f, f + BLK) for f in range(0, slots, BLK)]
    for rows in blocks:
        gb_ref[rows, :] = (
            og_ref[rows, :].astype(F32) * qa_ref[rows, ALIVE : ALIVE + 1].astype(F32)
        ).astype(BF)
    for copy in first:
        copy.wait()
    weight = w_ref[...].reshape(-1, depth * half)
    for i, rows in enumerate(blocks):
        hid_ref[rows, :] = x_ref[rows, :] + mm(ctx_ref[rows, :], weight, NT)
        if i == len(blocks) // 2 - 1:
            corners(0)
    corners(1)
    for rows in blocks:
        hidden = hid_ref[rows, :]
        norm_ref[rows, :] = (hidden * rms_factor(hidden) * gain).astype(BF)

    def unit_block(j, chosen):
        wi = ff_v[j, :, 0].reshape(-1, ff_v.shape[4])
        wo = ff_v[j, :, 1].reshape(-1, ff_v.shape[4])
        inner = [mm(norm_ref[rows, :], wi, NN) for rows in chosen]
        upstream = [mm(gb_ref[rows, :], wo, NN) for rows in chosen]
        pairs = [gelu_both(a, b) for a, b in zip(inner, upstream)]
        results = []
        for rows, (activated, grad_inner) in zip(chosen, pairs):
            branch, back = mm(activated, wo, NT), mm(grad_inner, wi, NT)
            if j:
                branch, back = br_ref[rows, :] + branch, dn_ref[rows, :] + back
            if j < end:
                br_ref[rows, :], dn_ref[rows, :] = branch, back
            results.append((branch, back))
        return results

    landed(0)
    unit_block(0, blocks)
    corners(2)
    pass_on(3)
    landed(1)
    unit_block(1, blocks)
    corners(3)
    landed(2)
    unit_block(2, blocks)
    landed(3)
    outs = []
    for i, (rows, (branch, back)) in enumerate(zip(blocks, unit_block(end, blocks))):
        hidden = hid_ref[rows, :]
        alive = qa_ref[rows, ALIVE : ALIVE + 1].astype(F32)
        out_ref[rows, :] = (alive * (hidden + branch)).astype(BF)
        factor = rms_factor(hidden)
        weighted = back * gain
        gh_ref[rows, :] = og_ref[rows, :].astype(F32) * alive + (
            factor * weighted
            - hidden
            * (factor * factor * factor)
            * jnp.mean(weighted * hidden, axis=-1, keepdims=True)
        )
        for at, (src, dst) in enumerate(((out_ref, out_hbm), (gh_ref, gh_hbm))):
            copy = pltpu.make_async_copy(src.at[rows], dst.at[rows], out_sem.at[2 * i + at])
            copy.start()
            outs.append(copy)
    for copy in outs:
        copy.wait()
    for copy in sent:
        copy.wait_send()


def feed_call(
    og, qa, gains, x, ctx, w, trio, from_east, from_south, last, lasted
):
    slots, width = x.shape
    depth, wide, rows, units = w.shape
    dma = pltpu.SemaphoreType.DMA
    return pl.pallas_call(
        feed_kernel,
        in_specs=[VMEM_SPEC] * 3 + [ANY_SPEC] * 8,
        out_specs=[ANY_SPEC] * 2,
        out_shape=[
            jax.ShapeDtypeStruct((slots, width), BF),
            jax.ShapeDtypeStruct((slots, width), F32),
        ],
        scratch_shapes=[
            pltpu.VMEM((depth, wide) + trio.shape[1:], BF),
            pltpu.VMEM(ctx.shape, BF),
            pltpu.VMEM((wide, rows, depth * units // 2), BF),
            pltpu.VMEM((slots, width), F32),
            pltpu.VMEM((slots, width), BF),
            pltpu.VMEM((slots, width), BF),
            pltpu.VMEM((slots, width), F32),
            pltpu.VMEM((slots, width), F32),
            pltpu.VMEM((slots, width), F32),
            pltpu.VMEM((slots, width), BF),
            pltpu.VMEM((slots, width), F32),
            dma((2 + depth,)),
            dma((depth, 3)),
            dma((depth, 8)),
            dma((depth, 8)),
            dma((2 * (slots // BLK),)),
        ],
        compiler_params=pltpu.CompilerParams(
            collective_id=2, has_side_effects=True, vmem_limit_bytes=VMEM_LIMIT
        ),
        name="feed_forward",
    )(og, qa, gains, x, ctx, w, trio, from_east, from_south, last, lasted)


def feed_local_kernel(
    x_ref, og_ref, qa_ref, gain_ref, ctx_hbm, w_hbm, wi_hbm, wo_hbm,
    out_ref, gh_ref,
    ctx_ref, w_ref, wi_ref, wo_ref, norm_ref, gb_ref, hid_ref, br_ref, dn_ref, sems,
):
    slots = x_ref.shape[0]
    groups = w_hbm.shape[0]
    half = w_hbm.shape[2] // 2
    first = [pltpu.make_async_copy(ctx_hbm, ctx_ref, sems.at[0])]
    for m in range(groups):
        first.append(
            pltpu.make_async_copy(w_hbm.at[m, :, half:], w_ref.at[m], sems.at[1 + m])
        )
    later = []
    for m in range(groups):
        later.append(
            (
                pltpu.make_async_copy(wi_hbm.at[m], wi_ref.at[m], sems.at[1 + groups + 2 * m]),
                pltpu.make_async_copy(wo_hbm.at[m], wo_ref.at[m], sems.at[2 + groups + 2 * m]),
            )
        )
    for copy in first:
        copy.start()
    for pair in later:
        pair[0].start()
        pair[1].start()
    for copy in first:
        copy.wait()
    gain = gain_ref[9:10]
    blocks = [slice(f, f + BLK) for f in range(0, slots, BLK)]
    for rows in blocks:
        hid_ref[rows, :] = x_ref[rows, :]
    for m in range(groups):
        cols = slice(m * half, (m + 1) * half)
        for rows in blocks:
            hid_ref[rows, :] += mm(ctx_ref[rows, cols], w_ref[m], NT)
    for rows in blocks:
        hidden = hid_ref[rows, :]
        norm_ref[rows, :] = (hidden * rms_factor(hidden) * gain).astype(BF)
        gb_ref[rows, :] = (
            og_ref[rows, :].astype(F32) * qa_ref[rows, ALIVE : ALIVE + 1].astype(F32)
        ).astype(BF)
    br_ref[...] = jnp.zeros_like(br_ref)
    dn_ref[...] = jnp.zeros_like(dn_ref)
    for m in range(groups):
        later[m][0].wait()
        later[m][1].wait()
    def unit_block(m, carry):
        inner = [mm(norm_ref[rows, :], wi_ref[m], NN) for rows in blocks]
        upstream = [mm(gb_ref[rows, :], wo_ref[m], NN) for rows in blocks]
        pairs = [gelu_both(a, b) for a, b in zip(inner, upstream)]
        for rows, (activated, grad_inner) in zip(blocks, pairs):
            br_ref[rows, :] += mm(activated, wo_ref[m], NT)
            dn_ref[rows, :] += mm(grad_inner, wi_ref[m], NT)
        return carry

    lax.fori_loop(0, groups, unit_block, 0)
    for rows in blocks:
        hidden = hid_ref[rows, :]
        alive = qa_ref[rows, ALIVE : ALIVE + 1].astype(F32)
        out_ref[rows, :] = (alive * (hidden + br_ref[rows, :])).astype(BF)
        factor = rms_factor(hidden)
        weighted = dn_ref[rows, :] * gain
        gh_ref[rows, :] = og_ref[rows, :].astype(F32) * alive + (
            factor * weighted
            - hidden
            * (factor * factor * factor)
            * jnp.mean(weighted * hidden, axis=-1, keepdims=True)
        )


def feed_local(x, og, qa, gain, ctx, w, wi, wo):
    slots, width = x.shape
    groups = w.shape[0]
    return pl.pallas_call(
        feed_local_kernel,
        in_specs=[VMEM_SPEC] * 4 + [ANY_SPEC] * 4,
        out_specs=[VMEM_SPEC] * 2,
        out_shape=[
            jax.ShapeDtypeStruct((slots, width), BF),
            jax.ShapeDtypeStruct((slots, width), F32),
        ],
        scratch_shapes=[
            pltpu.VMEM(ctx.shape, BF),
            pltpu.VMEM((groups, w.shape[1], w.shape[2] // 2), BF),
            pltpu.VMEM(wi.shape, BF),
            pltpu.VMEM(wo.shape, BF),
            pltpu.VMEM((slots, width), BF),
            pltpu.VMEM((slots, width), BF),
            pltpu.VMEM((slots, width), F32),
            pltpu.VMEM((slots, width), F32),
            pltpu.VMEM((slots, width), F32),
            pltpu.SemaphoreType.DMA((1 + 3 * groups,)),
        ],
        compiler_params=pltpu.CompilerParams(vmem_limit_bytes=VMEM_LIMIT),
        name="feed_forward_local",
    )(x, og, qa, gain, ctx, w, wi, wo)


def backward_kernel(
    lo_ref, hi_ref, gh_ref, lse_ref, qa_ref, ka_ref, marks_ref, gains_ref, kv_hbm, w_hbm, q_hbm,
    ctx_hbm, x_hbm, tiles_hbm, layer_hbm,
    ig_out, pg_ref, layer_out,
    kv_ref, w_ref, q_ref, ctx_ref, x_ref, tiles_ref, layer_ref, all_ref, kt_ref, dsum_ref,
    dqt_ref, ig_ref, sems, out_sem,
):
    slots = gh_ref.shape[0]
    count_blocks = slots // TILE
    groups = w_hbm.shape[0]
    half = w_hbm.shape[2] // 2
    wide = HEADS * TILE
    weights = [
        pltpu.make_async_copy(
            w_hbm.at[m, :, side * half : (side + 1) * half],
            w_ref.at[:, side * wide + m * half : side * wide + (m + 1) * half],
            sems.at[6 + side * groups + m],
        )
        for side in (1, 0)
        for m in range(groups)
    ]
    q_copy, ctx_copy, kv_copy, tiles_copy, x_copy, layer_copy = [
        pltpu.make_async_copy(src, dst, sems.at[i])
        for i, (src, dst) in enumerate(
            (
                (q_hbm, q_ref),
                (ctx_hbm, ctx_ref),
                (kv_hbm, kv_ref),
                (tiles_hbm, tiles_ref),
                (x_hbm, x_ref),
                (layer_hbm, layer_ref),
            )
        )
    ]
    for copy in [q_copy] + weights + [ctx_copy, kv_copy, tiles_copy, x_copy, layer_copy]:
        copy.start()
    dqt_ref[...] = jnp.zeros_like(dqt_ref)
    blocks = [slice(f, f + BLK) for f in range(0, slots, BLK)]
    q_copy.wait()
    grads_low = [gh_ref[rows, :].astype(BF) for rows in blocks]
    for copy in weights[:groups]:
        copy.wait()
    low_wide = low_lanes(wide)
    parts = [mm(grad, w_ref[:, wide:], NN) for grad in grads_low]
    for rows, part in zip(blocks, parts):
        q_ref[rows, :] = jnp.where(low_wide, q_ref[rows, :], part.astype(BF))
    ctx_copy.wait()
    pick = (
        lax.broadcasted_iota(jnp.int32, (wide, TILE), 0) // TILE
        == lax.broadcasted_iota(jnp.int32, (wide, TILE), 1)
    ).astype(F32).astype(BF)
    sums = []
    for rows in blocks:
        product = q_ref[rows, :].astype(F32) * ctx_ref[rows, :].astype(F32)
        upper = product.astype(BF)
        lower = (product - upper.astype(F32)).astype(BF)
        sums.append(mm(upper, pick, NN) + mm(lower, pick, NN))
    for rows, value in zip(blocks, sums):
        dsum_ref[:, rows] = value.T[0:16]
    kv_copy.wait()
    for h in range(HEADS):
        kt_ref[h] = kv_ref[:, h * TILE : (h + 1) * TILE].T[0:HEAD_DIM]
    tiles_copy.wait()
    low = low_lanes()

    def key_block(kb, carry):
        ks = span(kb, TILE)
        first, count = window_of(lo_ref, hi_ref, kb, count_blocks)

        def attend(pairs):
            size = 2 * pairs * TILE
            qs = pl.ds(pl.multiple_of(first * TILE, TILE), size)
            mask = mm(ka_ref[ks, :], qa_ref[qs, :], NT)

            def group_body(g, inner):
                heads = [g * GROUP + i for i in range(GROUP)]
                cols = [span(h, TILE) for h in heads]
                zero = jnp.zeros((TILE, TILE), BF)
                keys = [kv_ref[ks, c] for c in cols]
                raw = [
                    mm(
                        jnp.concatenate(
                            [jnp.where(low, key, zero), jnp.where(low, zero, key)], axis=0
                        ),
                        q_ref[qs, c],
                        NT,
                    )
                    for key, c in zip(keys, cols)
                ]
                probs = [
                    jnp.exp2(
                        both[:TILE]
                        + (bias_row(tiles_ref, h, first, kb, pairs) + mask)
                        - lse_ref[pl.ds(h, 1), qs]
                    )
                    for h, both in zip(heads, raw)
                ]
                outs = [
                    (p * (both[TILE:] - dsum_ref[pl.ds(h, 1), qs])).astype(BF)
                    for h, p, both in zip(heads, probs, raw)
                ]
                sides = [
                    jnp.concatenate([out, p.astype(BF)], axis=0) for out, p in zip(outs, probs)
                ]
                for h, c, out, side in zip(heads, cols, outs, sides):
                    both = mm(side, q_ref[qs, c], NN)
                    all_ref[ks, c] = jnp.where(
                        low, both[:TILE] * LN2, both[TILE:]
                    ).astype(BF)
                    dqt_ref[h, :, qs] += mm(kt_ref[h, :, ks], out, NN)
                return inner

            lax.fori_loop(0, HEADS // GROUP, group_body, 0)

        for pairs in range(1, count_blocks // 2 + 1):
            pl.when(count == pairs)(functools.partial(attend, pairs))

        @pl.when(count == 0)
        def _():
            all_ref[ks, :] = jnp.zeros((TILE, all_ref.shape[1]), BF)

        return carry

    lax.fori_loop(0, count_blocks, key_block, 0)
    rest = jnp.zeros((TILE - HEAD_DIM, slots), BF)
    for h in range(HEADS):
        place = wide + h * TILE
        all_ref[:, place : place + TILE] = jnp.concatenate(
            [dqt_ref[h].astype(BF), rest], axis=0
        ).T
    x_copy.wait()
    layer_copy.wait()
    layer_copy = pltpu.make_async_copy(layer_ref, layer_out, sems.at[5])
    layer_copy.start()
    gain = gains_ref[8:9]
    for copy in weights[groups:]:
        copy.wait()
    backs = [mm(all_ref[rows, :], w_ref[...], NT) for rows in blocks]
    outs = []
    total = None
    for i, (rows, back) in enumerate(zip(blocks, backs)):
        value = x_ref[rows, :]
        factor = rms_factor(value)
        weighted = back * gain
        grad = gh_ref[rows, :] + (
            factor * weighted
            - value
            * (factor * factor * factor)
            * jnp.mean(weighted * value, axis=-1, keepdims=True)
        )
        ig_ref[rows, :] = jnp.where(
            qa_ref[rows, IS_PROMPT : IS_PROMPT + 1].astype(F32) > 0, 0.0, grad
        )
        copy = pltpu.make_async_copy(ig_ref.at[rows], ig_out.at[rows], out_sem.at[i])
        copy.start()
        outs.append(copy)
        upper = grad.astype(BF)
        lower = (grad - upper.astype(F32)).astype(BF)
        hot = marks_ref[rows, :]
        part = mm(hot, upper, TN) + mm(hot, lower, TN)
        total = part if total is None else total + part
    pg_ref[...] = total
    layer_copy.wait()
    for copy in outs:
        copy.wait()


def backward_call(
    lo, hi, gh, lse, qa, ka, marks, gains, kv, w, q, ctx, x, tiles, layer_output
):
    slots, width = gh.shape
    groups = w.shape[0]
    return pl.pallas_call(
        backward_kernel,
        in_specs=[SMEM_SPEC] * 2 + [VMEM_SPEC] * 6 + [ANY_SPEC] * 7,
        out_specs=[ANY_SPEC, VMEM_SPEC, ANY_SPEC],
        out_shape=[
            jax.ShapeDtypeStruct((slots, width), F32),
            jax.ShapeDtypeStruct((TILE, width), F32),
            jax.ShapeDtypeStruct((slots, width), BF),
        ],
        scratch_shapes=[
            pltpu.VMEM(kv.shape, BF),
            pltpu.VMEM((w.shape[1], groups * w.shape[2]), BF),
            pltpu.VMEM(q.shape, BF),
            pltpu.VMEM(ctx.shape, BF),
            pltpu.VMEM(x.shape, F32),
            pltpu.VMEM(tiles.shape, F32),
            pltpu.VMEM(layer_output.shape, BF),
            pltpu.VMEM((slots, 2 * HEADS * TILE), BF),
            pltpu.VMEM((HEADS, HEAD_DIM, slots), BF),
            pltpu.VMEM((16, slots), F32),
            pltpu.VMEM((HEADS, HEAD_DIM, slots), F32),
            pltpu.VMEM((slots, width), F32),
            pltpu.SemaphoreType.DMA((2 * groups + 6,)),
            pltpu.SemaphoreType.DMA((slots // BLK,)),
        ],
        compiler_params=pltpu.CompilerParams(vmem_limit_bytes=VMEM_LIMIT),
        name="attend_back",
    )(lo, hi, gh, lse, qa, ka, marks, gains, kv, w, q, ctx, x, tiles, layer_output)


def slot_arrays(segments, live):
    slots = segments.shape[0]
    place = jnp.arange(slots, dtype=jnp.int32)
    first = jnp.sum((segments[None, :] < segments[:, None]).astype(jnp.int32), axis=1)
    position = place - first
    alive = live[:, None] == 1
    is_prompt = alive & (position < PROMPT)[:, None]
    lane = jnp.arange(TILE, dtype=jnp.int32)[None, :]
    marks = ((position[:, None] == lane) & is_prompt).astype(BF)
    same = segments[:, None] == lane
    query_side = jnp.where(lane == ALIVE, alive, same)
    query_side = jnp.where(lane == IS_PROMPT, is_prompt, query_side).astype(BF)
    key_side = jnp.where((lane < 16) & jnp.logical_not(same & alive), MASKED, 0.0).astype(BF)
    by_block = segments.reshape(-1, TILE)
    top = jnp.max(jnp.where(live.reshape(-1, TILE) == 1, by_block, -1), axis=1)
    hi = jnp.sum((segments[None, :] <= top[:, None]) & (live[None, :] == 1), axis=1)
    hi = (hi.astype(jnp.int32) + TILE - 1) // TILE
    lo = jnp.sum((segments[None, :] < by_block[:, :1]).astype(jnp.int32), axis=1) // TILE
    return marks, query_side, key_side, jnp.minimum(lo, hi)[None], hi[None]


def bias_tiles(table):
    place = jnp.arange(TILE, dtype=jnp.int32)
    kinds = jnp.arange(-2, 3, dtype=jnp.int32)[:, None, None] * TILE
    offset = jnp.clip(kinds + place[None, None, :] - place[None, :, None], -TILE, TILE)
    both = []
    for sign in (1, -1):
        both.append(
            table.astype(F32)[bucket_of(sign * offset, BUCKETS // 2)].transpose(3, 0, 1, 2) * LOG2E
        )
    return both


def tiles_of(first, second):
    rows = first.shape[0]
    shaped = [part.reshape(rows, -1, 1, HEAD_DIM) for part in (first, second)]
    return jnp.concatenate(shaped, axis=2).reshape(rows, -1)


def open_plain(
    tok, prompt, seg, live, w_query, w_key, w_value, w_output, w_inner, w_outer, gain_attn,
    gain_ffn, rel_table,
):
    slots, width = tok.shape
    packs = jnp.stack(
        [
            jnp.concatenate([tiles_of(w_key, w_value), tiles_of(w_query, w_output.T)], axis=1),
            w_inner,
            w_outer.T,
        ]
    )
    weights = lax.all_gather(lax.all_gather(packs, "dp", axis=1, tiled=True), "mp", axis=1)
    prompt_all = lax.all_gather(prompt.astype(BF), ("dp", "mp"), tiled=True)
    prompt_all = jnp.pad(prompt_all.reshape(PROMPT, width), ((0, TILE - PROMPT), (0, 0)))
    gains = lax.all_gather(jnp.stack([gain_attn, gain_ffn]), "dp", axis=1, tiled=True)
    gains = jnp.pad(gains.astype(F32), ((8, 6), (0, 0)))
    ahead, behind = bias_tiles(lax.all_gather(rel_table, "mp", axis=1, tiled=True))
    marks, query_side, key_side, lo, hi = slot_arrays(seg, live)
    placed = jnp.dot(marks, prompt_all, preferred_element_type=F32)
    x = jnp.where(query_side[:, IS_PROMPT:] > 0, placed, tok.astype(F32))
    normed = (x * rms_factor(x) * gains[8:9]).astype(BF)
    out = jnp.einsum("sd,mdc->smc", normed, weights[0], preferred_element_type=F32)
    half = out.shape[2] // 2
    kv = out[:, :, :half].astype(BF).reshape(slots, -1)
    q = jnp.where(low_lanes(half), out[:, :, half:] * LOG2E, 0.0).astype(BF).reshape(slots, -1)
    return weights, x, kv, q, ahead, behind, marks, query_side, key_side, gains, lo, hi


def adam_kernel(
    part_ref, state_ref, out_ref, low_ref, land_one, land_two, mid_ref, send_one, recv_one,
    send_two, recv_two,
):
    dp = lax.axis_index("dp")
    mp = lax.axis_index("mp")
    wide = part_ref.shape[0]
    deep = mid_ref.shape[0]
    width = part_ref.shape[2]
    low_ref[...] = part_ref[...].astype(BF)
    barrier = pltpu.get_barrier_semaphore()
    peers = [{"dp": lax.rem(dp + s, wide)} for s in range(1, wide)]
    peers += [{"mp": lax.rem(mp + s, deep)} for s in range(1, deep)]
    for peer in peers:
        pl.semaphore_signal(barrier, inc=1, device_id=peer, device_id_type=MESH)
    pl.semaphore_wait(barrier, len(peers))
    first = []
    for s in range(1, wide):
        to = lax.rem(dp + s, wide)
        copy = pltpu.make_async_remote_copy(
            src_ref=low_ref.at[to], dst_ref=land_one.at[s - 1],
            send_sem=send_one.at[s - 1], recv_sem=recv_one.at[s - 1],
            device_id={"dp": to}, device_id_type=MESH,
        )
        copy.start()
        first.append(copy)
    total = part_ref[dp]
    for s, copy in enumerate(first):
        copy.wait_recv()
        total = total + land_one[s].astype(F32)
    for m in range(deep):
        mid_ref[m, 0:4] = total[4 * m : 4 * m + 4]
        mid_ref[m, 4:8] = jnp.zeros((4, width), F32)
    second = []
    for s in range(1, deep):
        to = lax.rem(mp + s, deep)
        copy = pltpu.make_async_remote_copy(
            src_ref=mid_ref.at[to], dst_ref=land_two.at[s - 1],
            send_sem=send_two.at[s - 1], recv_sem=recv_two.at[s - 1],
            device_id={"mp": to}, device_id_type=MESH,
        )
        copy.start()
        second.append(copy)
    window = mid_ref[mp]
    for s, copy in enumerate(second):
        copy.wait_recv()
        window = window + land_two[s]
    begin = width // 8 * lax.rem(dp * deep + mp, 8)
    turned = pltpu.roll(window, lax.rem(width - begin, width), 1)
    lane = lax.broadcasted_iota(jnp.int32, (8, width), 1)
    grad = jnp.where(lane < width - begin, turned, pltpu.roll(turned, 7, 0))
    updated = adam_step(grad, state_ref[0], state_ref[1], state_ref[2])
    for i, value in enumerate(updated):
        out_ref[i] = value
    for copy in first + second:
        copy.wait_send()


def adam_step(grad, prompt, moment_one, moment_two):
    first_new = 0.9 * moment_one + 0.1 * grad
    second_new = 0.999 * moment_two + 0.001 * grad * grad
    correct_one = 1.0 - 0.9**ADAM_STEP
    correct_two = 1.0 - 0.999**ADAM_STEP
    prompt_new = prompt - 0.3 * (first_new / correct_one) / (
        jnp.sqrt(second_new / correct_two) + 1e-08
    )
    return prompt_new, first_new, second_new


def adam_call(part, state, deep):
    wide, rows, width = part.shape
    return pl.pallas_call(
        adam_kernel,
        in_specs=[VMEM_SPEC] * 2,
        out_specs=VMEM_SPEC,
        out_shape=jax.ShapeDtypeStruct(state.shape, F32),
        scratch_shapes=[
            pltpu.VMEM(part.shape, BF),
            pltpu.VMEM((wide - 1, rows, width), BF),
            pltpu.VMEM((deep - 1, 8, width), F32),
            pltpu.VMEM((deep, 8, width), F32),
            pltpu.SemaphoreType.DMA((wide - 1,)),
            pltpu.SemaphoreType.DMA((wide - 1,)),
            pltpu.SemaphoreType.DMA((deep - 1,)),
            pltpu.SemaphoreType.DMA((deep - 1,)),
        ],
        compiler_params=pltpu.CompilerParams(collective_id=1, has_side_effects=True),
        name="sum_and_step",
    )(part, state)


def body(
    dp, mp, tokens, prompt, moment_one, moment_two, segments, live, out_grad, w_query, w_key,
    w_value, w_output, w_inner, w_outer, gain_attn, gain_ffn, rel_table,
):
    _, slots, width = tokens.shape
    tuned = (dp, mp) == (8, 4)
    share = prompt.shape[0]
    if tuned:
        line = 8 * width
        state = functools.reduce(
            jnp.add,
            [
                jnp.pad(part, (i * line, (3 - i) * line - share))
                for i, part in enumerate((prompt, moment_one, moment_two))
            ],
        ).reshape(3, 8, width)
        (
            w, trio, last, x, kv, q, ahead, behind, marks, query_side, key_side, gains, lo, hi,
        ) = open_call(
            state, gain_attn[None], gain_ffn[None], rel_table.T, w_query, w_key, w_value,
            w_output, w_inner, w_outer.T, segments, live, tokens[0], dp, mp,
        )
        swap = lambda bit: lax.ppermute(trio, "dp", [(i, i ^ bit) for i in range(dp)])
        from_east, from_south = swap(2), swap(4)
        lasted = lax.ppermute(last, "mp", [(1, 0), (2, 3)])
    else:
        (
            weights, x, kv, q, ahead, behind, marks, query_side, key_side, gains, lo, hi,
        ) = open_plain(
            tokens[0], prompt, segments[0], live[0], w_query, w_key, w_value, w_output, w_inner,
            w_outer, gain_attn, gain_ffn, rel_table,
        )
    ctx, lse = attend_call(lo, hi, query_side, key_side, kv, q, ahead)
    if tuned:
        layer_output, grad_hidden = feed_call(
            out_grad[0], query_side, gains, x, ctx, w, trio, from_east, from_south, last,
            lasted,
        )
        w = w.reshape(mp, width, -1)
    else:
        w = weights[0]
        layer_output, grad_hidden = feed_local(
            x, out_grad[0], query_side, gains, ctx, w, weights[1], weights[2]
        )
    input_grad, prompt_part, layer_output = backward_call(
        lo, hi, grad_hidden, lse, query_side, key_side, marks, gains, kv, w, q, ctx, x, behind,
        layer_output,
    )
    if tuned:
        stepped = adam_call(prompt_part.reshape(dp, -1, width), state, mp)
        stepped = stepped.reshape(3, -1)[:, :share]
        prompt_new, first_new, second_new = stepped[0], stepped[1], stepped[2]
    else:
        grad = lax.psum_scatter(
            prompt_part[:PROMPT].reshape(-1), ("dp", "mp"), scatter_dimension=0, tiled=True
        )
        prompt_new, first_new, second_new = adam_step(grad, prompt, moment_one, moment_two)
    return (layer_output[None], input_grad[None], prompt_new, first_new, second_new)


def solution(mesh):
    both = ("dp", "mp")
    return jax.shard_map(
        functools.partial(body, mesh.shape["dp"], mesh.shape["mp"]),
        mesh=mesh,
        in_specs=(
            P(both, None, None),
            P(both),
            P(both),
            P(both),
            P(both, None),
            P(both, None),
            P(both, None, None),
            P("dp", "mp"),
            P("dp", "mp"),
            P("dp", "mp"),
            P("mp", "dp"),
            P("dp", "mp"),
            P("mp", "dp"),
            P("dp"),
            P("dp"),
            P(None, "mp"),
        ),
        out_specs=(
            P(both, None, None),
            P(both, None, None),
            P(both),
            P(both),
            P(both),
        ),
        check_vma=False,
    )
```
